32 devices in a mesh: section: 2 (over core), row: 4 (over z), col: 4 (over y, x).
Axes of the slice: x: 2, y: 2, z: 4, core: 2. Of those that a mesh axis runs over, the one named last changes fastest.
Arguments:
- tokens_in: bfloat16 [2, 1024, 2048], P(None, 'row', 'col'), may hold values from -6 to 6
- out_grad: bfloat16 [2, 1024, 2048], P(None, 'row', 'col'), may hold values from -6 to 6
- segments: int32 [2, 1024], P(None, 'row'), may hold values from 0 to 3, as said below
- positions: int32 [2, 1024], P(None, 'row'), may hold values from 0 to 511, as said below
- w_qkv: bfloat16 [2, 2048, 3, 2048], P('section', 'row', None, 'col'), may hold values from -0.125 to 0.125
- b_qkv: bfloat16 [2, 3, 2048], P('section', None, 'col'), may hold values from -4 to 4
- w_out: bfloat16 [2, 2048, 2048], P('section', 'row', 'col'), may hold values from -0.75 to 0.75
- w_gate_up: bfloat16 [2, 2048, 2, 5632], P('section', 'row', None, 'col'), may hold values from -0.125 to 0.125
- w_down: bfloat16 [2, 5632, 2048], P('section', 'row', 'col'), may hold values from -0.109375 to 0.109375
- norm_gains: bfloat16 [2, 2, 2048], P('section', None, 'col'), may hold values from 0.5 to 1.5
- norm_biases: bfloat16 [2, 2, 2048], P('section', None, 'col'), may hold values from -4 to 4
Outputs:
- layer_outputs: float32 [2, 2, 1024, 2048], P('section', None, 'row', 'col')
- input_grads: float32 [2, 2, 1024, 2048], P('section', None, 'row', 'col')
- grad_qkv: float32 [2, 2048, 3, 2048], P('section', 'row', None, 'col')
- grad_qkv_bias: float32 [2, 3, 2048], P('section', None, 'col')
- grad_out: float32 [2, 2048, 2048], P('section', 'row', 'col')
- grad_gate_up: float32 [2, 2048, 2, 5632], P('section', 'row', None, 'col')
- grad_down: float32 [2, 5632, 2048], P('section', 'row', 'col')
- grad_norm_gains: float32 [2, 2, 2048], P('section', None, 'col')
- grad_norm_biases: float32 [2, 2, 2048], P('section', None, 'col')
The draws below stay inside these ranges and needn't reach their ends.
Inputs may be any that keep to these rules, and one draw needn't show every extreme that they name: `segments`: in each sequence (each aligned block of 256 tokens of a micro-batch) segment numbers start at 0, never fall and take every value up to 3. Within a document positions rise by one from token to token; the first document of each sequence starts at position 0, documents between the first and the last at a position below 256, and the last document of each sequence ends at position 511.
All inputs are finite; a program needn't handle non-finite values.
Results may differ from the reference program's by a relative error of at most 0.018.
Values may be sent and summed in bfloat16 or wider, within the bound.
No kernel may reach another device: no remote copies, remote signals or barrier semaphores. Data moves between devices by JAX's collectives and lax.ppermute only.
A program may use at most 256 MiB of HBM per device.

```python
import jax
import jax.numpy as jnp
from jax import lax

D = 2048
HEADS = 32
FF = 5632
HEAD_DIM = 64
ROT = 16
TOK_DEV = 256
MICRO = 2
DOCS = 4
TOKENS = 1024
LAYERS = 2


def doc_layout(key):
    sequences = MICRO * TOKENS // TOK_DEV
    row_keys = jax.random.split(key, sequences)
    places = jnp.arange(TOK_DEV, dtype=jnp.int32)

    def one_sequence(row_key):
        cuts = jax.random.permutation(row_key, TOK_DEV - 1)[:DOCS - 1].astype(jnp.int32) + 1
        after_cut = places[:, None] >= cuts[None, :]
        segment = jnp.sum(after_cut.astype(jnp.int32), axis=1)
        begins = jnp.max(jnp.where(after_cut, cuts[None, :], 0), axis=1)
        return (segment, places - begins)
    segment, within = jax.vmap(one_sequence)(row_keys)
    return (segment.reshape(MICRO, TOKENS), within.reshape(MICRO, TOKENS))


def draw_segments(key, part):
    segment, within = doc_layout(key)
    return segment


def draw_positions(key, part):
    segment, within = doc_layout(key)
    key = jax.random.fold_in(key, 7)
    seq_count = TOKENS // TOK_DEV
    starts = jax.random.randint(key, (MICRO, seq_count, DOCS), 0, TOK_DEV).astype(jnp.int32)
    starts = starts.at[:, :, 0].set(0)
    within_rows = within.reshape(MICRO, seq_count, TOK_DEV)
    last_start = (2 * TOK_DEV - 1 - within_rows[:, :, TOK_DEV - 1]).astype(jnp.int32)
    starts = starts.at[:, :, DOCS - 1].set(last_start)
    starts_tokens = jnp.repeat(starts, TOK_DEV, axis=1)
    chosen = jnp.sum(jnp.where(segment[..., None] == jnp.arange(DOCS, dtype=jnp.int32), starts_tokens, 0), axis=-1)
    return (within + chosen).astype(jnp.int32)


def steps_of(key, extent, shards, smallest, largest):
    def one(dim, shards_of):
        draws = jax.random.uniform(jax.random.fold_in(jax.random.fold_in(key, 6), dim), (shards_of,), jnp.float32, smallest / len(shards), largest / len(shards))
        return jnp.repeat(jnp.exp(draws), extent[dim] // shards_of).reshape((-1,) + (1,) * (len(extent) - dim - 1))

    level = one(*shards[0])
    for cut in shards[1:]:
        level = level * one(*cut)
    return level


def bell_draw(rng, dims, scale, limit, shards=(), kind=jnp.bfloat16):
    loudness = steps_of(rng, dims, shards, -0.22, 0.18) if shards else 1.0
    array = jax.random.normal(rng, dims, jnp.float32) * scale * loudness
    return jnp.minimum(jnp.maximum(array, -limit), limit).astype(kind)


def setup_inputs(seed: int = 0) -> dict:
    streams_of = jax.random.split(jax.random.key(seed), 12)
    return {
        "tokens_in": bell_draw(streams_of[0], (MICRO, TOKENS, D), 1.0, 6.0, ((1, 4), (2, 4))),
        "out_grad": bell_draw(streams_of[1], (MICRO, TOKENS, D), 1.0, 6.0, ((1, 4), (2, 4))),
        "segments": draw_segments(jax.random.fold_in(streams_of[11], 71), 0),
        "positions": draw_positions(jax.random.fold_in(streams_of[11], 71), 0),
        "w_qkv": bell_draw(streams_of[4], (LAYERS, D, 3, D), D ** -0.5, 0.125, ((0, 2), (1, 4), (3, 4))),
        "b_qkv": bell_draw(streams_of[5], (LAYERS, 3, D), 0.3, 4.0, ((0, 2), (2, 4))),
        "w_out": bell_draw(streams_of[6], (LAYERS, D, D), (D // 32) ** -0.5, 0.75, ((0, 2), (1, 4), (2, 4))),
        "w_gate_up": bell_draw(streams_of[7], (LAYERS, D, 2, FF), D ** -0.5, 0.125, ((0, 2), (1, 4), (3, 4))),
        "w_down": bell_draw(streams_of[8], (LAYERS, FF, D), (FF // 2) ** -0.5, 0.109375, ((0, 2), (1, 4), (2, 4))),
        "norm_gains": jnp.clip(1.0 + 0.1 * jax.random.normal(streams_of[9], (LAYERS, 2, D), jnp.float32), 0.5, 1.5).astype(jnp.bfloat16),
        "norm_biases": bell_draw(streams_of[10], (LAYERS, 2, D), 0.3, 4.0, ((0, 2), (2, 4))),
    }


NORM_EPSILON = 1e-05
ROPE_BASE = 10000.0
SCORE_SCALE = 0.125
MASKED_SCORE = -1e+30
HIGHEST = lax.Precision.HIGHEST

@jax.custom_vjp
def low(v):
    return lax.optimization_barrier(v.astype(jnp.bfloat16)).astype(jnp.float32)

@jax.custom_vjp
def low_back(v):
    return v

def low_keep(v):
    return (low(v), None)

def low_pass(kept, grad):
    return (grad,)

def back_keep(v):
    return (v, None)

def back_low(kept, grad):
    return (low(grad),)
low.defvjp(low_keep, low_pass)
low_back.defvjp(back_keep, back_low)

def norm_apply(values, gain, shift):
    mean_value = lax.optimization_barrier(jnp.mean(values, axis=-1, keepdims=True))
    centred = values - mean_value
    spread = lax.optimization_barrier(jnp.mean(centred * centred, axis=-1, keepdims=True))
    return centred * lax.rsqrt(spread + NORM_EPSILON) * gain + shift

def rope_tables(places):
    freq_index = jnp.arange(ROT // 2, dtype=jnp.float32)
    inv_freq = jnp.power(ROPE_BASE, -2.0 * freq_index / ROT)
    angles = places.astype(jnp.float32)[:, None] * inv_freq[None, :]
    return (jnp.cos(angles), jnp.sin(angles))

def rotate_pairs(values, cosines, sines):
    half_rot = ROT // 2
    first_half = values[..., :half_rot]
    second_half = values[..., half_rot:ROT]
    remainder = values[..., ROT:]
    cos_rows = cosines[:, None, :]
    sin_rows = sines[:, None, :]
    return jnp.concatenate([first_half * cos_rows - second_half * sin_rows, second_half * cos_rows + first_half * sin_rows, remainder], axis=-1)

def attend_one(sequence_parts):
    queries, key_rows, value_rows, segment = sequence_parts
    scores = low_back(jnp.einsum('thd,shd->hts', queries, key_rows, precision=HIGHEST) * SCORE_SCALE)
    places = jnp.arange(segment.shape[0])
    allowed = (segment[:, None] == segment[None, :]) & (places[None, :] <= places[:, None])
    scores = jnp.where(allowed[None], scores, MASKED_SCORE)
    probabilities = low(jax.nn.softmax(scores, axis=-1))
    return jnp.einsum('hts,shd->thd', probabilities, value_rows, precision=HIGHEST)

def layer_apply(inputs, w_qkv, b_qkv, w_out, w_gate_up, w_down, gains, shifts, segment_ids, cosines, sines):
    row_count = inputs.shape[0]
    normed = low(norm_apply(inputs, gains[0], shifts[0]))
    projected = low_back(jnp.einsum('td,dkc->tkc', normed, w_qkv, precision=HIGHEST) + b_qkv)
    projected = projected.reshape(row_count, 3, HEADS, HEAD_DIM)
    queries = low(rotate_pairs(projected[:, 0], cosines, sines))
    key_rows = low(rotate_pairs(projected[:, 1], cosines, sines))
    value_rows = low(projected[:, 2])
    sequences = row_count // TOK_DEV
    split_shape = (sequences, TOK_DEV, HEADS, HEAD_DIM)
    attended = lax.map(jax.checkpoint(attend_one), (queries.reshape(split_shape), key_rows.reshape(split_shape), value_rows.reshape(split_shape), segment_ids.reshape(sequences, TOK_DEV)))
    attended = low_back(low(attended.reshape(row_count, D)))
    hidden_state = inputs + low_back(jnp.dot(attended, w_out, precision=HIGHEST))
    normed_mid = low(norm_apply(low(hidden_state), gains[1], shifts[1]))
    gate_up = low_back(jnp.einsum('td,dkf->tkf', normed_mid, w_gate_up, precision=HIGHEST))
    activated = low(jax.nn.silu(gate_up[:, 0]) * gate_up[:, 1])
    return hidden_state + low_back(jnp.dot(activated, w_down, precision=HIGHEST))

def reference(tokens_in, out_grad, segments, positions, w_qkv, b_qkv, w_out, w_gate_up, w_down, norm_gains, norm_biases):
    row_count = MICRO * TOKENS
    first_input = tokens_in.astype(jnp.float32).reshape(row_count, D)
    cotangent = out_grad.astype(jnp.float32).reshape(row_count, D)
    segment_ids = segments.reshape(row_count)
    cosines, sines = rope_tables(positions.reshape(row_count))
    weights = tuple((array_in.astype(jnp.float32) for array_in in (w_qkv, b_qkv, w_out, w_gate_up, w_down, norm_gains, norm_biases)))

    def forward(layer_input, probe_add, qkv_all, bias_all, out_all, gate_all, down_all, gain_all, shift_all):

        def run_layer(inputs, layer_index):
            return layer_apply(inputs, qkv_all[layer_index], bias_all[layer_index], out_all[layer_index], gate_all[layer_index], down_all[layer_index], gain_all[layer_index], shift_all[layer_index], segment_ids, cosines, sines)
        first_out = run_layer(layer_input, 0)
        second_out = run_layer(low_back(low(first_out)) + probe_add, 1)
        return (first_out, second_out)
    probe_add = jnp.zeros((row_count, D), jnp.float32)
    results, pullback = jax.vjp(forward, first_input, probe_add, *weights)
    gradients = pullback((jnp.zeros_like(results[0]), cotangent))
    layer_outputs = jnp.stack([results[0], results[1]]).reshape(LAYERS, MICRO, TOKENS, D)
    input_grads = jnp.stack([gradients[0], gradients[1]]).reshape(LAYERS, MICRO, TOKENS, D)
    return (layer_outputs, input_grads, gradients[2], gradients[3], gradients[4], gradients[5], gradients[6], gradients[7], gradients[8])
```

```python
import jax
import jax.numpy as jnp
from jax import lax
from jax.sharding import PartitionSpec as P

HEAD_DIM = 64
ROT = 16
NORM_EPSILON = 1e-05
ROPE_BASE = 10000.0
SCORE_SCALE = 0.125
MASKED_SCORE = -1e30
BF = jnp.bfloat16
F32 = jnp.float32


def swap(value):
    return lax.ppermute(value, "section", [(0, 1), (1, 0)])


def hop(value, axis, step):
    return lax.ppermute(value, axis, [(i, i ^ step) for i in range(lax.axis_size(axis))])


def spread(value, axis):
    return [value] + [hop(value, axis, k) for k in range(1, lax.axis_size(axis))]


def trade(pieces, axis):
    return [pieces[0]] + [hop(pieces[k], axis, k) for k in range(1, len(pieces))]


def total(pieces, axis):
    parts = trade(pieces, axis)
    out = parts[0].astype(F32)
    for part in parts[1:]:
        out = out + part.astype(F32)
    return out


def by_place(pieces, me):
    bit = 1
    while bit < len(pieces):
        flip = (me & bit) != 0
        pieces = [jnp.where(flip, pieces[i ^ bit], pieces[i]) for i in range(len(pieces))]
        bit *= 2
    return pieces


def pick(stack, index):
    return lax.dynamic_index_in_dim(stack, index, 0, keepdims=False)


def dot(a, b):
    return lax.dot_general(a, b, (((1,), (0,)), ((), ())), preferred_element_type=F32)


def dot_nt(a, b):
    return lax.dot_general(a, b, (((1,), (1,)), ((), ())), preferred_element_type=F32)


def dot_tn(a, b):
    return lax.dot_general(a, b, (((0,), (0,)), ((), ())), preferred_element_type=F32)


def norm(values, gain, shift):
    mean_value = jnp.mean(values, axis=-1, keepdims=True)
    centred = values - mean_value
    spread_ = jnp.mean(centred * centred, axis=-1, keepdims=True)
    inv = lax.rsqrt(spread_ + NORM_EPSILON)
    scaled = centred * inv
    return (scaled * gain + shift).astype(BF), scaled, inv


def norm_back(grad, scaled, inv, gain):
    e = grad * gain
    mean_e = jnp.mean(e, axis=-1, keepdims=True)
    mean_p = jnp.mean(e * scaled, axis=-1, keepdims=True)
    return inv * (e - mean_e - scaled * mean_p), jnp.sum(grad * scaled, axis=0), jnp.sum(grad, axis=0)


def rotate_pairs(values, cosines, sines):
    half = ROT // 2
    u, w, rest = values[..., :half], values[..., half:ROT], values[..., ROT:]
    c, s = cosines[:, None, :], sines[:, None, :]
    return jnp.concatenate([u * c - w * s, w * c + u * s, rest], axis=-1)


def attend(projected, allowed, cosines, sines):
    n = projected.shape[0]
    heads = projected.reshape(n, 3, -1, HEAD_DIM)
    q = rotate_pairs(heads[:, 0], cosines, sines).astype(BF)
    k = rotate_pairs(heads[:, 1], cosines, sines).astype(BF)
    v = heads[:, 2].astype(BF)
    scores = jnp.einsum("thd,shd->hts", q, k, preferred_element_type=F32) * SCORE_SCALE
    scores = jnp.where(allowed[None], scores, MASKED_SCORE)
    shifted = jnp.exp(scores - jnp.max(scores, axis=-1, keepdims=True))
    probs = shifted / jnp.sum(shifted, axis=-1, keepdims=True)
    out = jnp.einsum("hts,shd->thd", probs.astype(BF), v, preferred_element_type=F32)
    return out.reshape(n, -1).astype(BF), (q, k, v, probs)


def attend_back(kept, grad_out, cosines, sines):
    q, k, v, probs = kept
    n = grad_out.shape[0]
    g = grad_out.reshape(n, -1, HEAD_DIM)
    dprobs = jnp.einsum("thd,shd->hts", g, v, preferred_element_type=F32)
    row = jnp.sum(dprobs * probs, axis=-1, keepdims=True)
    ds = (probs * (dprobs - row)).astype(BF)
    dq = jnp.einsum("hts,shd->thd", ds, k, preferred_element_type=F32) * SCORE_SCALE
    dk = jnp.einsum("hts,thd->shd", ds, q, preferred_element_type=F32) * SCORE_SCALE
    dv = jnp.einsum("hts,thd->shd", probs.astype(BF), g, preferred_element_type=F32)
    out = jnp.stack([rotate_pairs(dq, cosines, -sines), rotate_pairs(dk, cosines, -sines), dv], axis=1)
    return out.reshape(n, -1).astype(BF)


def shards(
    tokens_in, out_grad, segments, positions, w_qkv, b_qkv, w_out, w_gate_up, w_down, norm_gains, norm_biases
):
    rows, cols = lax.axis_size("row"), lax.axis_size("col")
    me_s, me_r, me_c = lax.axis_index("section"), lax.axis_index("row"), lax.axis_index("col")
    first = me_s == 0
    seq, dc = tokens_in.shape[1:]
    width = dc * cols
    tq = seq // cols
    dr = width // rows
    fc, fr = w_gate_up.shape[3], w_down.shape[1]
    w2, v2 = dc // 2, dr // 2
    sub = rows // cols
    band = dr // cols

    def own_first(a, b):
        return jnp.where(first, a, b), jnp.where(first, b, a)

    def share(halves):
        mine, theirs = own_first(halves[0], halves[1])
        got = swap(theirs)
        return own_first(mine, got)

    def unshare(l0, l1):
        mine, theirs = own_first(l0, l1)
        return own_first(mine, swap(theirs))

    def halves_of(x, blocks):
        x = x.reshape(x.shape[0], blocks, 2, -1)
        a, b = own_first(x[:, :, 0], x[:, :, 1])
        return a.reshape(a.shape[0], -1), b.reshape(b.shape[0], -1)

    def join_halves(own, other, blocks):
        a, b = own_first(own, other)
        n = own.shape[0]
        return jnp.stack([a.reshape(n, blocks, -1), b.reshape(n, blocks, -1)], axis=2).reshape(n, -1)

    def perm_cols(x):
        n = x.shape[0]
        parts = x.reshape(n, cols, -1)
        return jnp.concatenate(by_place([parts[:, i] for i in range(cols)], me_c), axis=1)

    small = jnp.concatenate([norm_gains[0], norm_biases[0], b_qkv[0]], axis=0)
    mate = swap(small)
    params = []
    for own_small in own_first(small, mate):
        wide = jnp.stack(by_place(spread(own_small[:4], "col"), me_c), axis=1).reshape(4, width).astype(F32)
        params.append((wide, own_small[4:].astype(F32).reshape(1, 3 * dc)))

    q_half = share(w_qkv[0].reshape(2, v2, 3 * dc))
    o_half = share([w_out[0, :, :w2], w_out[0, :, w2:]])
    g_half = share([w_gate_up[0, :, 0], w_gate_up[0, :, 1]])
    d_half = share([w_down[0, :, :w2], w_down[0, :, w2:]])

    def gather_qkv(half):
        own = lax.all_gather(half, "row", axis=0, tiled=True)
        return own, swap(own)

    def gather_out(half):
        whole = lax.all_gather(half, "row", axis=0, tiled=True).reshape(cols, dc, w2)
        parts = trade([pick(whole, me_c ^ k) for k in range(cols)], "col")
        own = jnp.concatenate(by_place(parts, me_c), axis=1)
        return own, swap(own)

    def gather_gate(half):
        bands = half.reshape(cols, band, fc)
        parts = trade([pick(bands, me_c ^ k) for k in range(cols)], "col")
        blocks = jnp.stack(parts).reshape(cols, band, sub, fr).transpose(0, 2, 1, 3).reshape(rows, band, fr)
        sends = []
        for j in range(rows):
            to = me_r ^ j
            sends.append(pick(blocks, (me_c ^ (to // sub)) * sub + to % sub))
        piece = jnp.concatenate(by_place(trade(sends, "row"), me_r), axis=0)
        own = jnp.concatenate(spread(piece, "col"), axis=0)
        return own, swap(own)

    def gather_down(half):
        own = jnp.concatenate(spread(half, "col"), axis=1)
        return own, swap(own)

    def to_gate(x):
        x = x.reshape(x.shape[0], rows, cols, band).transpose(0, 2, 1, 3).reshape(x.shape[0], width)
        return perm_cols(x)

    def from_gate(x):
        x = perm_cols(x).reshape(x.shape[0], cols, rows, band).transpose(0, 2, 1, 3)
        return x.reshape(x.shape[0], width)

    def to_tokens(x):
        parts = trade([pick(x.reshape(cols, tq, dc), me_c ^ k) for k in range(cols)], "col")
        return jnp.concatenate(by_place(parts, me_c), axis=1)

    own_tokens = pick(tokens_in, me_s)
    own_grad = pick(out_grad, me_s)
    places = jnp.arange(seq, dtype=jnp.int32).reshape(cols, tq)
    place = jnp.concatenate([pick(places, me_c ^ k) for k in range(cols)])
    segment = pick(segments, me_s).reshape(cols, tq)
    segment = jnp.concatenate([pick(segment, me_c ^ k) for k in range(cols)])
    position = pick(positions, me_s).reshape(cols, tq)
    position = jnp.concatenate([pick(position, me_c ^ k) for k in range(cols)])
    allowed = (segment[:, None] == segment[None, :]) & (place[None, :] <= place[:, None])
    freq = jnp.power(ROPE_BASE, -2.0 * jnp.arange(ROT // 2, dtype=F32) / ROT)
    angles = position.astype(F32)[:, None] * freq[None, :]
    cosines, sines = jnp.cos(angles), jnp.sin(angles)

    def gather_tokens(parts, axis):
        sizes = [p.shape[1] for p in parts]
        got = jnp.concatenate(spread(jnp.concatenate(parts, axis=1), axis), axis=0)
        out, at = [], 0
        for size in sizes:
            out.append(got[:, at : at + size])
            at += size
        return out

    def sum_tokens(parts, axis):
        whole = jnp.concatenate([p.astype(BF) for p in parts], axis=1)
        n = whole.shape[0] // tq
        return total([whole[k * tq : (k + 1) * tq] for k in range(n)], axis)

    x = to_tokens(own_tokens).astype(F32)
    grad = to_tokens(own_grad).astype(F32)
    weights, kept, outputs = [], [], []
    for layer in range(2):
        (g1, g2, c1, c2), bias = params[layer][0], params[layer][1]
        wq = gather_qkv(q_half[layer])
        wg = gather_gate(g_half[layer])
        wo = gather_out(o_half[layer])
        wd = gather_down(d_half[layer])
        weights.append((wq, wo, wg, wd))
        a, scaled1, inv1 = norm(x, g1, c1)
        a_own, a_oth = gather_tokens(halves_of(a, rows), "col")
        projected = dot(a_own, wq[0]) + dot(a_oth, wq[1]) + bias
        o, att = attend(projected, allowed, cosines, sines)
        got = sum_tokens([dot(o, wo[0]), dot(o, wo[1])], "col")
        h = x + join_halves(got[:, : width // 2], got[:, width // 2 :], cols)
        b, scaled2, inv2 = norm(h.astype(BF).astype(F32), g2, c2)
        (b_all,) = gather_tokens([to_gate(b)], "row")
        gate, up = own_first(dot(b_all, wg[0]), dot(b_all, wg[1]))
        m = (gate * jax.nn.sigmoid(gate) * up).astype(BF)
        got = sum_tokens([dot(m, wd[0]), dot(m, wd[1])], "row")
        y = h + join_halves(perm_cols(got[:, : width // 2]), perm_cols(got[:, width // 2 :]), cols)
        outputs.append(y)
        kept.append((a_own, a_oth, scaled1, inv1, att, o, scaled2, inv2, b_all, gate, up, m))
        x = y.astype(BF).astype(F32)

    input_grads, q_grads, o_grads, g_grads, d_grads, smalls = [None] * 2, [None] * 2, [None] * 2, [None] * 2, [None] * 2, [None] * 2
    for layer in (1, 0):
        (g1, g2, c1, c2) = params[layer][0]
        wq, wo, wg, wd = weights[layer]
        a_own, a_oth, scaled1, inv1, att, o, scaled2, inv2, b_all, gate, up, m = kept[layer]
        dyb = grad.astype(BF)
        h_own, h_oth = halves_of(dyb, cols)
        y_own, y_oth = gather_tokens([perm_cols(h_own), perm_cols(h_oth)], "row")
        dm = dot_nt(y_own, wd[0]) + dot_nt(y_oth, wd[1])
        sig = jax.nn.sigmoid(gate)
        d_gate = (dm * up * sig * (1.0 + gate * (1.0 - sig))).astype(BF)
        d_up = (dm * gate * sig).astype(BF)
        e_own, e_oth = own_first(d_gate, d_up)
        got = sum_tokens([dot_nt(e_own, wg[0]) + dot_nt(e_oth, wg[1])], "row")
        back, gain2, shift2 = norm_back(from_gate(got), scaled2, inv2, g2)
        dh = grad + back
        wide = dot_tn(jnp.concatenate([m, swap(m)]), jnp.concatenate([y_own, swap(y_oth)])).astype(BF)
        d_grads[layer] = total([wide[:, k * w2 : (k + 1) * w2] for k in range(cols)], "col")
        wide = dot_tn(jnp.concatenate([b_all, swap(b_all)]), jnp.concatenate([e_own, swap(e_oth)])).astype(BF)
        tall = rows * band
        piece = total([wide[k * tall : (k + 1) * tall] for k in range(cols)], "col").astype(BF).reshape(rows, band, fr)
        parts = trade([pick(piece, me_r ^ j) for j in range(rows)], "row")
        blocks = jnp.stack(by_place(parts, me_r)).reshape(cols, sub, band, fr).transpose(0, 2, 1, 3).reshape(cols, band, fc)
        parts = trade([pick(blocks, me_c ^ k) for k in range(cols)], "col")
        g_grads[layer] = jnp.concatenate(by_place(parts, me_c), axis=0).astype(F32)
        dhb = dh.astype(BF)
        h_own, h_oth = gather_tokens(halves_of(dhb, cols), "col")
        d_o = (dot_nt(h_own, wo[0]) + dot_nt(h_oth, wo[1])).astype(BF)
        dp = attend_back(att, d_o, cosines, sines)
        got = sum_tokens([dot_nt(dp, wq[0]), dot_nt(dp, wq[1])], "col")
        back, gain1, shift1 = norm_back(
            join_halves(got[:, : width // 2], got[:, width // 2 :], rows), scaled1, inv1, g1
        )
        dx = dh + back
        wide = dot_tn(jnp.concatenate([o, swap(o)]), jnp.concatenate([h_own, swap(h_oth)])).astype(BF)
        wide = wide.reshape(dc, cols, w2).transpose(1, 0, 2)
        parts = trade([pick(wide, me_c ^ k) for k in range(cols)], "col")
        tall = jnp.concatenate(by_place(parts, me_c), axis=0)
        o_grads[layer] = lax.psum_scatter(tall, "row", scatter_dimension=0, tiled=True).astype(F32)
        wide = dot_tn(jnp.concatenate([a_own, swap(a_oth)]), jnp.concatenate([dp, swap(dp)])).astype(BF)
        q_grads[layer] = lax.psum_scatter(wide, "row", scatter_dimension=0, tiled=True).astype(F32)
        input_grads[layer] = dx
        bias_sum = jnp.sum(dp.astype(F32), axis=0)
        smalls[layer] = (jnp.stack([gain1, gain2, shift1, shift2]), bias_sum)
        grad = dx.astype(BF).astype(F32)

    def to_output(l0, l1):
        mine, theirs = own_first(l0, l1)
        both = jnp.stack(own_first(mine, swap(theirs)))
        blocks = both.reshape(2, tq, cols, dc).transpose(2, 0, 1, 3)
        parts = trade([pick(blocks, me_c ^ k) for k in range(cols)], "col")
        return jnp.concatenate(by_place(parts, me_c), axis=1)[None]

    norm_sums = jnp.stack([smalls[0][0], smalls[1][0]]).reshape(2, 4, cols, dc).transpose(2, 0, 1, 3)
    norm_sums = total([pick(norm_sums, me_c ^ k) for k in range(cols)], "col")
    bias_sums = jnp.stack([smalls[0][1], smalls[1][1]]).reshape(2, 3, dc)
    sums = jnp.concatenate([norm_sums, bias_sums], axis=1)
    sums = total([sums] * rows, "row")
    mine, theirs = own_first(sums[0], sums[1])
    sums = mine + swap(theirs)
    grad_qkv = jnp.concatenate(unshare(*q_grads), axis=0).reshape(1, dr, 3, dc)
    grad_out = jnp.concatenate(unshare(*o_grads), axis=1)[None]
    grad_gate_up = jnp.stack(unshare(*g_grads), axis=1)[None]
    grad_down = jnp.concatenate(unshare(*d_grads), axis=1)[None]
    return (
        to_output(*outputs),
        to_output(*input_grads),
        grad_qkv,
        sums[None, 4:],
        grad_out,
        grad_gate_up,
        grad_down,
        sums[None, 0:2],
        sums[None, 2:4],
    )


def solution(mesh):
    return jax.shard_map(
        shards,
        mesh=mesh,
        in_specs=(
            P(None, "row", "col"),
            P(None, "row", "col"),
            P(None, "row"),
            P(None, "row"),
            P("section", "row", None, "col"),
            P("section", None, "col"),
            P("section", "row", "col"),
            P("section", "row", None, "col"),
            P("section", "row", "col"),
            P("section", None, "col"),
            P("section", None, "col"),
        ),
        out_specs=(
            P("section", None, "row", "col"),
            P("section", None, "row", "col"),
            P("section", "row", None, "col"),
            P("section", None, "col"),
            P("section", "row", "col"),
            P("section", "row", None, "col"),
            P("section", "row", "col"),
            P("section", None, "col"),
            P("section", None, "col"),
        ),
        check_vma=False,
    )
```

```python
import jax
import jax.numpy as jnp
from jax import lax
from jax.experimental import pallas as pl
from jax.experimental.pallas import tpu as pltpu
from jax.sharding import PartitionSpec as P

HEAD_DIM = 64
ROT = 16
NORM_EPSILON = 1e-05
ROPE_BASE = 10000.0
SCORE_SCALE = 0.125
MASKED_SCORE = -1e30
BF = jnp.bfloat16
F32 = jnp.float32


def trade(stack, axis):
    return lax.all_to_all(stack, axis, split_axis=0, concat_axis=0)


def gather(value, axis):
    return trade(jnp.broadcast_to(value, (lax.axis_size(axis), *value.shape)), axis)


def total(stack, axis):
    return jnp.sum(trade(stack, axis).astype(F32), axis=0)


def tie(point, *values):
    return lax.optimization_barrier((point, *values))


def dot(a, b):
    return lax.dot_general(a, b, (((1,), (0,)), ((), ())), preferred_element_type=F32)


def dot_nt(a, b):
    return lax.dot_general(a, b, (((1,), (1,)), ((), ())), preferred_element_type=F32)


def dot_tn(a, b):
    return lax.dot_general(a, b, (((0,), (0,)), ((), ())), preferred_element_type=F32)


def norm(values, gain, shift):
    mean_value = jnp.mean(values, axis=-1, keepdims=True)
    centred = values - mean_value
    variance = jnp.mean(centred * centred, axis=-1, keepdims=True)
    inv = lax.rsqrt(variance + NORM_EPSILON)
    scaled = centred * inv
    return (scaled * gain + shift).astype(BF), scaled, inv


def norm_back(grad, scaled, inv, gain):
    e = grad * gain
    mean_e = jnp.mean(e, axis=-1, keepdims=True)
    mean_p = jnp.mean(e * scaled, axis=-1, keepdims=True)
    return inv * (e - mean_e - scaled * mean_p), jnp.sum(grad * scaled, axis=0), jnp.sum(grad, axis=0)


def call(body, grid, in_specs, out_specs, out_shape, scratch, flops, moved, *args):
    return pl.pallas_call(
        body,
        grid=(grid,),
        in_specs=in_specs,
        out_specs=out_specs,
        out_shape=out_shape,
        scratch_shapes=scratch,
        compiler_params=pltpu.CompilerParams(vmem_limit_bytes=48 * 2**20),
        cost_estimate=pl.CostEstimate(flops=int(flops), bytes_accessed=int(moved), transcendentals=0),
    )(*args)


def turn(x, cosines, sines, sign):
    ahead = pltpu.roll(x, 128 - ROT // 2, 1)
    behind = pltpu.roll(x, ROT // 2, 1)
    return x * cosines + sign * (ahead * sines[0] + behind * sines[1])


def head_lanes(n):
    lanes = lax.broadcasted_iota(jnp.int32, (n, 128), 1)
    return lanes < HEAD_DIM


def softmax_of(q, k, allowed):
    scores = jnp.where(allowed, dot_nt(q, k) * SCORE_SCALE, MASKED_SCORE)
    shifted = jnp.exp(scores - jnp.max(scores, axis=1, keepdims=True))
    return shifted / jnp.sum(shifted, axis=1, keepdims=True)


def attention(a, w, bias, tables, mask):
    n, width = a.shape
    m = w.shape[1] // 4
    steps = 4
    depth = width // steps

    def body(a_ref, w_ref, bias_ref, tab_ref, mask_ref, qkv_ref, o_ref, acc):
        step = pl.program_id(0)

        @pl.when(step == 0)
        def _():
            acc[...] = jnp.broadcast_to(bias_ref[...], acc.shape)

        acc[...] += dot(a_ref[...], w_ref[...])

        @pl.when(step == steps - 1)
        def _():
            low = head_lanes(n)
            zero = jnp.zeros((n, 128), BF)
            allowed = mask_ref[...] > 0
            cosines, sines = tab_ref[0], (tab_ref[1], tab_ref[2])
            for pair in range(m // 128):
                at = pair * 128
                q = turn(acc[:, at : at + 128], cosines, sines, 1.0).astype(BF)
                k = turn(acc[:, m + at : m + at + 128], cosines, sines, 1.0).astype(BF)
                v = acc[:, 2 * m + at : 2 * m + at + 128].astype(BF)
                qkv_ref[:, at : at + 128] = q
                qkv_ref[:, m + at : m + at + 128] = k
                qkv_ref[:, 2 * m + at : 2 * m + at + 128] = v
                p0 = softmax_of(jnp.where(low, q, zero), k, allowed).astype(BF)
                p1 = softmax_of(jnp.where(low, zero, q), k, allowed).astype(BF)
                o_ref[:, at : at + 128] = jnp.where(low, dot(p0, v), dot(p1, v)).astype(BF)

    return call(
        body,
        steps,
        [
            pl.BlockSpec((n, depth), lambda i: (0, i)),
            pl.BlockSpec((depth, 3 * m), lambda i: (i, 0)),
            pl.BlockSpec((1, 3 * m), lambda i: (0, 0)),
            pl.BlockSpec((3, n, 128), lambda i: (0, 0, 0)),
            pl.BlockSpec((n, n), lambda i: (0, 0)),
        ],
        [pl.BlockSpec((n, 3 * m), lambda i: (0, 0)), pl.BlockSpec((n, m), lambda i: (0, 0))],
        [jax.ShapeDtypeStruct((n, 3 * m), BF), jax.ShapeDtypeStruct((n, m), BF)],
        [pltpu.VMEM((n, 3 * m), F32)],
        2 * n * width * 3 * m,
        2 * width * 3 * m,
        a,
        w,
        bias,
        tables,
        mask,
    )


def attention_back(d_o, qkv, w, tables, mask):
    n, m = d_o.shape
    width = w.shape[0]
    steps = 4
    depth = width // steps

    def body(d_ref, qkv_ref, w_ref, tab_ref, mask_ref, dp_ref, sum_ref, da_ref):
        step = pl.program_id(0)

        @pl.when(step == 0)
        def _():
            low = head_lanes(n)
            zero = jnp.zeros((n, 128), BF)
            allowed = mask_ref[...] > 0
            cosines, sines = tab_ref[0], (tab_ref[1], tab_ref[2])
            for pair in range(m // 128):
                at = pair * 128
                q = qkv_ref[:, at : at + 128]
                k = qkv_ref[:, m + at : m + at + 128]
                v = qkv_ref[:, 2 * m + at : 2 * m + at + 128]
                g = d_ref[:, at : at + 128]
                out = []
                for mine in (True, False):
                    pick_q = jnp.where(low, q, zero) if mine else jnp.where(low, zero, q)
                    pick_g = jnp.where(low, g, zero) if mine else jnp.where(low, zero, g)
                    probs = softmax_of(pick_q, k, allowed)
                    d_probs = dot_nt(pick_g, v)
                    row = jnp.sum(d_probs * probs, axis=1, keepdims=True)
                    ds = (probs * (d_probs - row)).astype(BF)
                    out.append((dot(ds, k), dot_tn(ds, q), dot_tn(probs.astype(BF), g)))
                dq, dk, dv = (jnp.where(low, x, y) for x, y in zip(*out))
                dq = turn(dq * SCORE_SCALE, cosines, sines, -1.0)
                dk = turn(dk * SCORE_SCALE, cosines, sines, -1.0)
                for place, part in enumerate((dq, dk, dv)):
                    part = part.astype(BF)
                    dp_ref[:, place * m + at : place * m + at + 128] = part
                    sum_ref[:, place * m + at : place * m + at + 128] = jnp.sum(part.astype(F32), axis=0, keepdims=True)

        da_ref[...] = dot_nt(dp_ref[...], w_ref[...]).astype(BF)

    return call(
        body,
        steps,
        [
            pl.BlockSpec((n, m), lambda i: (0, 0)),
            pl.BlockSpec((n, 3 * m), lambda i: (0, 0)),
            pl.BlockSpec((depth, 3 * m), lambda i: (i, 0)),
            pl.BlockSpec((3, n, 128), lambda i: (0, 0, 0)),
            pl.BlockSpec((n, n), lambda i: (0, 0)),
        ],
        [
            pl.BlockSpec((n, 3 * m), lambda i: (0, 0)),
            pl.BlockSpec((1, 3 * m), lambda i: (0, 0)),
            pl.BlockSpec((n, depth), lambda i: (0, i)),
        ],
        [
            jax.ShapeDtypeStruct((n, 3 * m), BF),
            jax.ShapeDtypeStruct((1, 3 * m), F32),
            jax.ShapeDtypeStruct((n, width), BF),
        ],
        [],
        2 * n * width * 3 * m,
        2 * width * 3 * m,
        d_o,
        qkv,
        w,
        tables,
        mask,
    )


def heads_out(o, w):
    c, n, m = o.shape

    def body(o_ref, w_ref, out_ref, acc):
        part = dot(o_ref[0], w_ref[...])

        @pl.when(pl.program_id(0) == 0)
        def _():
            acc[...] = part

        @pl.when(pl.program_id(0) > 0)
        def _():
            acc[...] += part

        @pl.when(pl.program_id(0) == c - 1)
        def _():
            out_ref[...] = acc[...].astype(BF)

    return call(
        body,
        c,
        [pl.BlockSpec((1, n, m), lambda i: (i, 0, 0)), pl.BlockSpec((m, m), lambda i: (i, 3))],
        pl.BlockSpec((n, m), lambda i: (0, 0)),
        jax.ShapeDtypeStruct((n, m), BF),
        [pltpu.VMEM((n, m), F32)],
        2 * c * n * m * m,
        2 * c * m * m,
        o,
        w,
    )


def heads_back(d_h, w):
    n, m = d_h.shape
    c = w.shape[0] // m

    def body(d_ref, w_ref, out_ref):
        out_ref[0] = dot_nt(d_ref[...], w_ref[...]).astype(BF)

    return call(
        body,
        c,
        [pl.BlockSpec((n, m), lambda i: (0, 0)), pl.BlockSpec((m, m), lambda i: (i, 3))],
        pl.BlockSpec((1, n, m), lambda i: (i, 0, 0)),
        jax.ShapeDtypeStruct((c, n, m), BF),
        [],
        2 * c * n * m * m,
        2 * c * m * m,
        d_h,
        w,
    )


def attention_grads(a, o, dp, d_h):
    n, width = a.shape
    m = d_h.shape[1]
    steps = 8
    depth = width // steps
    per = m // depth

    def body(a_ref, o_ref, dp_ref, dh_ref, out_ref):
        out_ref[:, : 3 * m] = dot_tn(a_ref[...], dp_ref[...]).astype(BF)
        out_ref[:, 3 * m :] = dot_tn(o_ref[0], dh_ref[...]).astype(BF)

    return call(
        body,
        steps,
        [
            pl.BlockSpec((n, depth), lambda i: (0, i)),
            pl.BlockSpec((1, n, depth), lambda i: (i // per, 0, i % per)),
            pl.BlockSpec((n, 3 * m), lambda i: (0, 0)),
            pl.BlockSpec((n, m), lambda i: (0, 0)),
        ],
        pl.BlockSpec((depth, 4 * m), lambda i: (i, 0)),
        jax.ShapeDtypeStruct((width, 4 * m), BF),
        [],
        2 * n * width * 4 * m,
        2 * width * 4 * m,
        a,
        o,
        dp,
        d_h,
    )


def mlp(b, w):
    n, width = b.shape
    blocks, _, w2, f = w.shape
    c = blocks // 2
    depth = width // c

    def body(b_ref, wg_ref, wd_ref, gate_ref, up_ref, m_ref, y_ref):
        step = pl.program_id(0)

        @pl.when(step < blocks)
        def _():
            weight = wg_ref[0].reshape(depth, f)
            part = dot(b_ref[...], weight)
            for kind, ref in ((0, gate_ref), (1, up_ref)):

                @pl.when(step == kind * c)
                def _():
                    ref[...] = part

                @pl.when((step > kind * c) & (step < (kind + 1) * c))
                def _():
                    ref[...] += part

        @pl.when(step == blocks - 1)
        def _():
            gate = gate_ref[...]
            m_ref[...] = (gate * jax.nn.sigmoid(gate) * up_ref[...]).astype(BF)

        @pl.when(step >= blocks)
        def _():
            y_ref[...] = dot_nt(m_ref[...], wd_ref[0, 0]).astype(BF)

    def down(i):
        return jnp.maximum(i - blocks, 0)

    return call(
        body,
        2 * blocks,
        [
            pl.BlockSpec((n, depth), lambda i: (0, jnp.minimum(i, blocks - 1) % c)),
            pl.BlockSpec((1, 2, w2, f), lambda i: (jnp.minimum(i, blocks - 1), 0, 0, 0)),
            pl.BlockSpec((1, 1, w2, f), lambda i: (down(i), 2, 0, 0)),
        ],
        [pl.BlockSpec((n, f), lambda i: (0, 0))] * 3
        + [pl.BlockSpec((n, w2), lambda i: (0, down(i) % c * 2 + down(i) // c))],
        [jax.ShapeDtypeStruct((n, f), F32)] * 2 + [jax.ShapeDtypeStruct((n, f), BF), jax.ShapeDtypeStruct((n, width), BF)],
        [],
        2 * n * width * 3 * f,
        2 * width * 3 * f,
        b,
        w,
        w,
    )


def mlp_back(dy, gate, up, w):
    n, width = dy.shape
    blocks, _, w2, f = w.shape
    c = blocks // 2
    depth = width // c

    def body(dy_ref, gate_ref, up_ref, wd_ref, wg_ref, wu_ref, d_ref, db_ref, acc):
        step = pl.program_id(0)

        @pl.when(step == 0)
        def _():
            acc[...] = jnp.zeros_like(acc)

        @pl.when(step < blocks)
        def _():
            acc[...] += dot(dy_ref[...], wd_ref[0, 0])

        @pl.when(step == blocks - 1)
        def _():
            gate, dm = gate_ref[...], acc[...]
            sig = jax.nn.sigmoid(gate)
            d_ref[0] = (dm * up_ref[...] * sig * (1.0 + gate * (1.0 - sig))).astype(BF)
            d_ref[1] = (dm * gate * sig).astype(BF)

        @pl.when(step >= blocks)
        def _():
            part = dot_nt(d_ref[0], wg_ref[0].reshape(depth, f))
            db_ref[...] = (part + dot_nt(d_ref[1], wu_ref[0].reshape(depth, f))).astype(BF)

    def early(i):
        return jnp.minimum(i, blocks - 1)

    def late(i):
        return jnp.maximum(i - blocks, 0)

    return call(
        body,
        blocks + c,
        [
            pl.BlockSpec((n, w2), lambda i: (0, early(i) % c * 2 + early(i) // c)),
            pl.BlockSpec((n, f), lambda i: (0, 0)),
            pl.BlockSpec((n, f), lambda i: (0, 0)),
            pl.BlockSpec((1, 1, w2, f), lambda i: (early(i), 2, 0, 0)),
            pl.BlockSpec((1, 2, w2, f), lambda i: (late(i), 0, 0, 0)),
            pl.BlockSpec((1, 2, w2, f), lambda i: (c + late(i), 0, 0, 0)),
        ],
        [pl.BlockSpec((2, n, f), lambda i: (0, 0, 0)), pl.BlockSpec((n, depth), lambda i: (0, late(i)))],
        [jax.ShapeDtypeStruct((2, n, f), BF), jax.ShapeDtypeStruct((n, width), BF)],
        [pltpu.VMEM((n, f), F32)],
        2 * n * width * 3 * f,
        2 * width * 3 * f,
        dy,
        gate,
        up,
        w,
        w,
        w,
    )


def mlp_grads(b, d, dy, m):
    n, width = b.shape
    f = m.shape[1]
    c = lax.axis_size("col")
    depth, w2 = width // c, width // c // 2

    def body(b_ref, d_ref, dy_ref, m_ref, out_ref):
        out_ref[0, :depth] = dot_tn(b_ref[...], d_ref[0]).astype(BF)
        out_ref[0, depth:] = dot_tn(dy_ref[...], m_ref[...]).astype(BF)

    return call(
        body,
        2 * c,
        [
            pl.BlockSpec((n, depth), lambda i: (0, i % c)),
            pl.BlockSpec((1, n, f), lambda i: (i // c, 0, 0)),
            pl.BlockSpec((n, w2), lambda i: (0, i % c * 2 + i // c)),
            pl.BlockSpec((n, f), lambda i: (0, 0)),
        ],
        pl.BlockSpec((1, depth + w2, f), lambda i: (i, 0, 0)),
        jax.ShapeDtypeStruct((2 * c, depth + w2, f), BF),
        [],
        2 * n * width * 3 * f,
        2 * width * 3 * f,
        b,
        d,
        dy,
        m,
    )


def swap(value):
    return lax.ppermute(value, "section", [(0, 1), (1, 0)])


def hop(value, axis, step):
    return lax.ppermute(value, axis, [(i, i ^ step) for i in range(lax.axis_size(axis))])


def pick(stack, index):
    return lax.dynamic_index_in_dim(stack, index, 0, keepdims=False)


def place_all(pieces, me):
    out = jnp.zeros((len(pieces), *pieces[0].shape), pieces[0].dtype)
    for k, piece in enumerate(pieces):
        out = lax.dynamic_update_index_in_dim(out, piece, me ^ k, 0)
    return out


def send_all(value, axis):
    return [value] + [hop(value, axis, k) for k in range(1, lax.axis_size(axis))]


def send_parts(stack, axis):
    me = lax.axis_index(axis)
    return [pick(stack, me)] + [hop(pick(stack, me ^ k), axis, k) for k in range(1, stack.shape[0])]


def add_all(parts):
    out = parts[0].astype(F32)
    for part in parts[1:]:
        out = out + part.astype(F32)
    return out


def shards(
    tokens_in, out_grad, segments, positions, w_qkv, b_qkv, w_out, w_gate_up, w_down, norm_gains, norm_biases
):
    rows, cols = lax.axis_size("row"), lax.axis_size("col")
    me_s = lax.axis_index("section")
    first = me_s == 0
    seq, dc = tokens_in.shape[1:]
    width = dc * cols
    tq = seq // cols
    dr = width // rows
    fc, fr = w_gate_up.shape[3], w_down.shape[1]
    w2, v2 = dc // 2, dr // 2
    sub = rows // cols
    band = dr // cols

    def own_first(a, b):
        return jnp.where(first, a, b), jnp.where(first, b, a)

    def to_gate(x):
        return x.reshape(-1, rows, cols, band).transpose(0, 2, 1, 3).reshape(-1, width)

    def from_gate(x):
        return x.reshape(-1, cols, rows, band).transpose(0, 2, 1, 3).reshape(-1, width)

    def to_features(stack):
        return stack.transpose(1, 0, 2).reshape(stack.shape[1], width)

    def by_feature(x):
        return x.reshape(x.shape[0], cols, dc).transpose(1, 0, 2)

    me_r, me_c = lax.axis_index("row"), lax.axis_index("col")
    qo = jnp.concatenate([w_qkv[0], w_out[0][:, None]], axis=1).reshape(2, v2, 4 * dc)
    qo_half = trade(qo, "section")
    qo_half, w_gate_up = tie(qo_half, w_gate_up)

    def gather_qo(layer):
        return lax.all_gather(qo_half[layer], ("row", "section"), axis=0, tiled=True)

    wqo0 = gather_qo(0)
    g_half = trade(w_gate_up[0].transpose(1, 0, 2), "section")

    def to_blocks(bands):
        return bands.reshape(cols, band, sub, fr).transpose(0, 2, 1, 3).reshape(rows, band, fr)

    def from_blocks(blocks):
        return blocks.reshape(cols, sub, band, fr).transpose(0, 2, 1, 3).reshape(cols, band, fc)

    def gather_mlp(piece, down):
        both = jnp.concatenate([piece.reshape(dc, fr), down])
        return lax.all_gather(both, ("section", "col"), axis=0, tiled=True).reshape(2 * cols, 3, w2, fr)

    own_tokens = pick(tokens_in, me_s)
    own_grad = pick(out_grad, me_s)
    both = jnp.stack([own_tokens, own_grad]).reshape(2, cols, tq, dc).transpose(1, 0, 2, 3)
    small = jnp.concatenate([norm_gains[0], norm_biases[0], b_qkv[0]], axis=0)
    g_half, both, small, w_down = tie(g_half, both, small, w_down)
    g_parts = send_parts(g_half[0].reshape(cols, band, fc), "col")
    both = trade(both, "col").transpose(1, 2, 0, 3).reshape(2, tq, width)
    x = both[0].astype(F32)
    small = gather(small, "section")
    wide = gather(small[:, :4], "col").transpose(1, 2, 0, 3).reshape(2, 4, width).astype(F32)
    bias = small[:, 4:].astype(F32).reshape(2, 1, 3 * dc)

    segment = pick(segments, me_s)
    position = pick(positions, me_s)
    place = jnp.arange(seq, dtype=jnp.int32)
    allowed = (segment[:, None] == segment[None, :]) & (place[None, :] <= place[:, None])
    mask = allowed.astype(F32)
    freq = jnp.power(ROPE_BASE, -2.0 * jnp.arange(ROT // 2, dtype=F32) / ROT)
    angles = position.astype(F32)[:, None] * freq[None, :]
    cosines, sines = jnp.cos(angles), jnp.sin(angles)
    rest = jnp.zeros((seq, HEAD_DIM - ROT), F32)
    none = jnp.zeros_like(sines)
    tables = jnp.stack(
        [
            jnp.concatenate([cosines, cosines, rest + 1.0] * 2, axis=1),
            jnp.concatenate([-sines, none, rest] * 2, axis=1),
            jnp.concatenate([none, sines, rest] * 2, axis=1),
        ]
    )

    weights, kept, outputs = [], [], []
    for layer in range(2):
        g1, g2, c1, c2 = wide[layer]
        a, scaled1, inv1 = norm(x, g1, c1)
        if layer == 0:
            scaled1, *g_parts = tie(scaled1, *g_parts)
            g_parts = send_parts(to_blocks(place_all(g_parts, me_c)), "row")
            d_half = trade(w_down[0].T.reshape(2, w2, fr), "section")
        a_all = gather(a, "col").reshape(seq, width)
        a_kept = a_all
        if layer == 0:
            wqo0, *g_parts = tie(wqo0, *g_parts)
            wgd0 = gather_mlp(place_all(g_parts, me_r), d_half[0])
            wqo = wqo0
        else:
            wqo = wqo1
        qkv, o = attention(a_all, wqo, bias[layer], tables, mask)
        if layer == 0:
            o, g_half, qo_half = tie(o, g_half, qo_half)
            g_parts = send_parts(g_half[1].reshape(cols, band, fc), "col")
            wqo1 = gather_qo(1)
        else:
            o, grad = tie(o, both[1])
            dy_parts = send_all(grad, "row")
        o_all = gather(o, "col")
        got = trade(heads_out(o_all, wqo).reshape(cols, tq, dc), "col")
        h = x + to_features(got).astype(F32)
        b, scaled2, inv2 = norm(h.astype(BF).astype(F32), g2, c2)
        if layer == 0:
            scaled2, *g_parts = tie(scaled2, *g_parts)
            g_parts = send_parts(to_blocks(place_all(g_parts, me_c)), "row")
        b_all = gather(to_gate(b), "row").reshape(rows * tq, width)
        wgd = wgd0 if layer == 0 else wgd1
        weights.append((wqo, wgd))
        gate, up, m, partial = mlp(b_all, wgd)
        if layer == 0:
            gate, *g_parts = tie(gate, *g_parts)
            wgd1 = gather_mlp(place_all(g_parts, me_r), d_half[1])
        else:
            gate, *parts = tie(gate, *dy_parts)
            dy_all = place_all(parts, me_r).reshape(rows * tq, width)
        y = h + total(partial.reshape(rows, tq, width), "row")
        outputs.append(y)
        kept.append((a_all, scaled1, inv1, qkv, o_all, scaled2, inv2, b_all, gate, up, m))
        x = y.astype(BF).astype(F32)

    input_grads, qo_grads, g_grads, d_grads, norm_sums, bias_sums = ([None] * 2 for _ in range(6))
    grad = grad.astype(F32)
    for layer in (1, 0):
        g1, g2, c1, c2 = wide[layer]
        wqo, wgd = weights[layer]
        a_all, scaled1, inv1, qkv, o_all, scaled2, inv2, b_all, gate, up, m = kept[layer]
        if layer == 0:
            dy_all = gather(grad.astype(BF), "row").reshape(rows * tq, width)
        d, partial = mlp_back(dy_all, gate, up, wgd)
        partial, d, dy_all, m, b_all = tie(partial, d, dy_all, m, b_all)
        got = total(partial.reshape(rows, tq, width), "row")
        wide_grad = mlp_grads(b_all, d, dy_all, m).reshape(-1, fr)
        gd_piece = lax.psum_scatter(wide_grad, ("section", "col"), scatter_dimension=0, tiled=True)
        back, gain2, shift2 = norm_back(from_gate(got), scaled2, inv2, g2)
        dh = grad + back
        dh_all = trade(by_feature(dh.astype(BF)), "col").reshape(seq, dc)
        dh_side = dh_all
        if layer == 0:
            dh_side, gd_late = tie(dh_all, gd_late)
            g_late = send_parts(gd_late[:dc].reshape(rows, band, fr), "row")
        d_o = total(heads_back(dh_all, wqo), "col").astype(BF)
        dp, bias_sum, partial = attention_back(d_o, qkv, wqo, tables, mask)
        partial, dp = tie(partial, dp)
        got = total(partial.reshape(cols, tq, width), "col")
        wide_grad = attention_grads(a_all, o_all, dp, dh_side)
        qo_piece = lax.psum_scatter(wide_grad, ("row", "section"), scatter_dimension=0, tiled=True)
        if layer == 0:
            bias_sum, *g_late = tie(bias_sum, *g_late)
            g_late = send_parts(from_blocks(place_all(g_late, me_r)), "col")
        back, gain1, shift1 = norm_back(got, scaled1, inv1, g1)
        dx = dh + back
        norm_sums[layer] = jnp.stack([gain1, gain2, shift1, shift2])
        bias_sums[layer] = bias_sum.reshape(3, dc)
        grad = dx.astype(BF).astype(F32)
        qo_grads[layer] = qo_piece
        d_grads[layer] = gd_piece[dc:]
        if layer == 1:
            gd_late = gd_piece
        else:
            dx, *g_late = tie(dx, *g_late)
            g_grads[1] = place_all(g_late, me_c).reshape(dr, fc)
            blocks = trade(gd_piece[:dc].reshape(rows, band, fr), "row")
            g_grads[0] = trade(from_blocks(blocks), "col").reshape(dr, fc)
        input_grads[layer] = dx

    def to_output(pair):
        both = trade(jnp.stack(pair), "section")
        blocks = trade(both.reshape(2, tq, cols, dc).transpose(2, 0, 1, 3), "col")
        return blocks.transpose(1, 0, 2, 3).reshape(1, 2, seq, dc)

    def unshare(pair):
        return trade(jnp.stack(pair), "section")

    sums = total(jnp.stack(norm_sums).reshape(2, 4, cols, dc).transpose(2, 0, 1, 3), "col")
    sums = jnp.concatenate([sums, jnp.stack(bias_sums)], axis=1)
    sums = total(jnp.sum(gather(sums, "row"), axis=0), "section")
    qo_grads = unshare(qo_grads).astype(F32).reshape(1, dr, 4, dc)
    return (
        to_output(outputs),
        to_output(input_grads),
        qo_grads[:, :, :3],
        sums[None, 4:],
        qo_grads[:, :, 3],
        unshare(g_grads).astype(F32).transpose(1, 0, 2)[None],
        unshare(d_grads).astype(F32).reshape(dc, fr).T[None],
        sums[None, 0:2],
        sums[None, 2:4],
    )


def solution(mesh):
    return jax.shard_map(
        shards,
        mesh=mesh,
        in_specs=(
            P(None, "row", "col"),
            P(None, "row", "col"),
            P(None, "row"),
            P(None, "row"),
            P("section", "row", None, "col"),
            P("section", None, "col"),
            P("section", "row", "col"),
            P("section", "row", None, "col"),
            P("section", "row", "col"),
            P("section", None, "col"),
            P("section", None, "col"),
        ),
        out_specs=(
            P("section", None, "row", "col"),
            P("section", None, "row", "col"),
            P("section", "row", None, "col"),
            P("section", None, "col"),
            P("section", "row", "col"),
            P("section", "row", None, "col"),
            P("section", "row", "col"),
            P("section", None, "col"),
            P("section", None, "col"),
        ),
        check_vma=False,
    )
```

```python
import jax
import jax.numpy as jnp
from jax import lax
from jax.experimental import pallas as pl
from jax.experimental.pallas import tpu as pltpu
from jax.sharding import PartitionSpec as P

HEAD_DIM = 64
ROT = 16
NORM_EPSILON = 1e-05
ROPE_BASE = 10000.0
SCORE_SCALE = 0.125
MASKED_SCORE = -1e30
BF = jnp.bfloat16
F32 = jnp.float32


def trade(stack, axis):
    return lax.all_to_all(stack, axis, split_axis=0, concat_axis=0)


def gather(value, axis):
    return trade(jnp.broadcast_to(value, (lax.axis_size(axis), *value.shape)), axis)


def total(stack, axis):
    return jnp.sum(trade(stack, axis).astype(F32), axis=0)


def tie(point, *values):
    return lax.optimization_barrier((point, *values))


def dot(a, b):
    return lax.dot_general(a, b, (((1,), (0,)), ((), ())), preferred_element_type=F32)


def dot_nt(a, b):
    return lax.dot_general(a, b, (((1,), (1,)), ((), ())), preferred_element_type=F32)


def dot_tn(a, b):
    return lax.dot_general(a, b, (((0,), (0,)), ((), ())), preferred_element_type=F32)


def norm(values, gain, shift):
    mean_value = jnp.mean(values, axis=-1, keepdims=True)
    centred = values - mean_value
    variance = jnp.mean(centred * centred, axis=-1, keepdims=True)
    inv = lax.rsqrt(variance + NORM_EPSILON)
    scaled = centred * inv
    return (scaled * gain + shift).astype(BF), scaled, inv


def norm_back(grad, scaled, inv, gain):
    e = grad * gain
    mean_e = jnp.mean(e, axis=-1, keepdims=True)
    mean_p = jnp.mean(e * scaled, axis=-1, keepdims=True)
    return inv * (e - mean_e - scaled * mean_p), jnp.sum(grad * scaled, axis=0), jnp.sum(grad, axis=0)


def call(body, grid, in_specs, out_specs, out_shape, scratch, flops, moved, table, *args):
    return pl.pallas_call(
        body,
        grid_spec=pltpu.PrefetchScalarGridSpec(
            num_scalar_prefetch=1,
            grid=(grid,),
            in_specs=in_specs,
            out_specs=out_specs,
            scratch_shapes=scratch,
        ),
        out_shape=out_shape,
        compiler_params=pltpu.CompilerParams(vmem_limit_bytes=56 * 2**20),
        cost_estimate=pl.CostEstimate(flops=int(flops), bytes_accessed=int(moved), transcendentals=0),
    )(table, *args)


def no_table():
    return jnp.zeros((1, 1), jnp.int32)


def turn(x, cosines, sines, sign):
    ahead = pltpu.roll(x, 128 - ROT // 2, 1)
    behind = pltpu.roll(x, ROT // 2, 1)
    return x * cosines + sign * (ahead * sines[0] + behind * sines[1])


def head_lanes(n):
    lanes = lax.broadcasted_iota(jnp.int32, (n, 128), 1)
    return lanes < HEAD_DIM


def softmax_of(q, k, allowed):
    scores = jnp.where(allowed, dot_nt(q, k) * SCORE_SCALE, MASKED_SCORE)
    shifted = jnp.exp(scores - jnp.max(scores, axis=1, keepdims=True))
    return shifted / jnp.sum(shifted, axis=1, keepdims=True)


def whole(*shape):
    return pl.BlockSpec(shape, lambda i, t: (0,) * len(shape))


HBM = pl.BlockSpec(memory_space=pl.ANY)


def fetch(pairs, sems):
    copies = [pltpu.make_async_copy(src, dst, sems.at[i]) for i, (src, dst) in enumerate(pairs)]
    for copy in copies:
        copy.start()
    return copies


def attention(a, w, bias, tables, mask):
    n, width = a.shape
    m = w.shape[1] // 4
    half = width // 2

    def body(_, a_ref, w_ref, bias_ref, tab_ref, mask_ref, qkv_ref, o_ref, held, acc, sems):
        parts = [pl.ds(i * half, half) for i in range(2)]
        copies = fetch([(w_ref.at[part, pl.ds(0, 3 * m)], held.at[part]) for part in parts], sems)
        copies[0].wait()
        acc[...] = dot(a_ref[:, :half], held[:half]) + bias_ref[...]
        copies[1].wait()
        acc[...] += dot(a_ref[:, half:], held[half:])
        low = head_lanes(n)
        zero = jnp.zeros((n, 128), BF)
        allowed = mask_ref[...] > 0
        cosines, sines = tab_ref[0], (tab_ref[1], tab_ref[2])
        for pair in range(m // 128):
            at = pair * 128
            q = turn(acc[:, at : at + 128], cosines, sines, 1.0).astype(BF)
            k = turn(acc[:, m + at : m + at + 128], cosines, sines, 1.0).astype(BF)
            v = acc[:, 2 * m + at : 2 * m + at + 128].astype(BF)
            qkv_ref[:, at : at + 128] = q
            qkv_ref[:, m + at : m + at + 128] = k
            qkv_ref[:, 2 * m + at : 2 * m + at + 128] = v
            p0 = softmax_of(jnp.where(low, q, zero), k, allowed).astype(BF)
            p1 = softmax_of(jnp.where(low, zero, q), k, allowed).astype(BF)
            o_ref[:, at : at + 128] = jnp.where(low, dot(p0, v), dot(p1, v)).astype(BF)

    return call(
        body,
        1,
        [whole(n, width), HBM, whole(1, 3 * m), whole(3, n, 128), whole(n, n)],
        [whole(n, 3 * m), whole(n, m)],
        [jax.ShapeDtypeStruct((n, 3 * m), BF), jax.ShapeDtypeStruct((n, m), BF)],
        [pltpu.VMEM((width, 3 * m), BF), pltpu.VMEM((n, 3 * m), F32), pltpu.SemaphoreType.DMA((2,))],
        2 * n * width * 3 * m,
        2 * width * 3 * m,
        no_table(),
        a,
        w,
        bias,
        tables,
        mask,
    )


def attention_back(d_o, qkv, w, tables, mask):
    n, m = d_o.shape
    width = w.shape[0]
    half = width // 2

    def body(_, d_ref, qkv_ref, w_ref, tab_ref, mask_ref, dp_ref, sum_ref, da_ref, held, sems):
        parts = [pl.ds(i * half, half) for i in range(2)]
        copies = fetch([(w_ref.at[part, pl.ds(0, 3 * m)], held.at[part]) for part in parts], sems)
        low = head_lanes(n)
        zero = jnp.zeros((n, 128), BF)
        allowed = mask_ref[...] > 0
        cosines, sines = tab_ref[0], (tab_ref[1], tab_ref[2])
        for pair in range(m // 128):
            at = pair * 128
            q = qkv_ref[:, at : at + 128]
            k = qkv_ref[:, m + at : m + at + 128]
            v = qkv_ref[:, 2 * m + at : 2 * m + at + 128]
            g = d_ref[:, at : at + 128]
            out = []
            for mine in (True, False):
                pick_q = jnp.where(low, q, zero) if mine else jnp.where(low, zero, q)
                pick_g = jnp.where(low, g, zero) if mine else jnp.where(low, zero, g)
                probs = softmax_of(pick_q, k, allowed)
                d_probs = dot_nt(pick_g, v)
                row = jnp.sum(d_probs * probs, axis=1, keepdims=True)
                ds = (probs * (d_probs - row)).astype(BF)
                out.append((dot(ds, k), dot_tn(ds, q), dot_tn(probs.astype(BF), g)))
            dq, dk, dv = (jnp.where(low, x, y) for x, y in zip(*out))
            dq = turn(dq * SCORE_SCALE, cosines, sines, -1.0)
            dk = turn(dk * SCORE_SCALE, cosines, sines, -1.0)
            for place, part in enumerate((dq, dk, dv)):
                part = part.astype(BF)
                dp_ref[:, place * m + at : place * m + at + 128] = part
                sum_ref[:, place * m + at : place * m + at + 128] = jnp.sum(part.astype(F32), axis=0, keepdims=True)
        for i, copy in enumerate(copies):
            copy.wait()
            da_ref[:, i * half : (i + 1) * half] = dot_nt(dp_ref[...], held[i * half : (i + 1) * half]).astype(BF)

    return call(
        body,
        1,
        [whole(n, m), whole(n, 3 * m), HBM, whole(3, n, 128), whole(n, n)],
        [whole(n, 3 * m), whole(1, 3 * m), whole(n, width)],
        [
            jax.ShapeDtypeStruct((n, 3 * m), BF),
            jax.ShapeDtypeStruct((1, 3 * m), F32),
            jax.ShapeDtypeStruct((n, width), BF),
        ],
        [pltpu.VMEM((width, 3 * m), BF), pltpu.SemaphoreType.DMA((2,))],
        2 * n * width * 3 * m,
        2 * width * 3 * m,
        no_table(),
        d_o,
        qkv,
        w,
        tables,
        mask,
    )


def heads_out(o, w):
    c, n, m = o.shape

    def body(_, o_ref, w_ref, out_ref, held, sems):
        (copy,) = fetch([(w_ref.at[:, pl.ds(3 * m, m)], held)], sems)
        o_wide = jnp.concatenate([o_ref[i] for i in range(c)], axis=1)
        copy.wait()
        out_ref[...] = dot(o_wide, held[...]).astype(BF)

    return call(
        body,
        1,
        [whole(c, n, m), HBM],
        whole(n, m),
        jax.ShapeDtypeStruct((n, m), BF),
        [pltpu.VMEM((c * m, m), BF), pltpu.SemaphoreType.DMA((1,))],
        2 * c * n * m * m,
        2 * c * m * m,
        no_table(),
        o,
        w,
    )


def heads_back(d_h, w):
    n, m = d_h.shape
    c = w.shape[0] // m

    def body(_, d_ref, w_ref, out_ref, held, sems):
        (copy,) = fetch([(w_ref.at[:, pl.ds(3 * m, m)], held)], sems)
        copy.wait()
        back = dot_nt(d_ref[...], held[...]).astype(BF)
        for i in range(c):
            out_ref[i] = back[:, i * m : (i + 1) * m]

    return call(
        body,
        1,
        [whole(n, m), HBM],
        whole(c, n, m),
        jax.ShapeDtypeStruct((c, n, m), BF),
        [pltpu.VMEM((c * m, m), BF), pltpu.SemaphoreType.DMA((1,))],
        2 * c * n * m * m,
        2 * c * m * m,
        no_table(),
        d_h,
        w,
    )


def attention_grads(a, o, dp, d_h, mates, table):
    n, width = a.shape
    m = d_h.shape[1]
    steps = table.shape[1]
    depth = width // (2 * steps)
    per = m // depth

    def body(_, a_ref, o_ref, dp_ref, dh_ref, a2_ref, o2_ref, dp2_ref, dh2_ref, out_ref, dp_all, dh_all):
        @pl.when(pl.program_id(0) == 0)
        def _():
            dp_all[:n], dp_all[n:] = dp_ref[...], dp2_ref[...]
            dh_all[:n], dh_all[n:] = dh_ref[...], dh2_ref[...]

        out_ref[:, : 3 * m] = dot_tn(jnp.concatenate([a_ref[...], a2_ref[...]]), dp_all[...]).astype(BF)
        out_ref[:, 3 * m :] = dot_tn(jnp.concatenate([o_ref[0], o2_ref[0]]), dh_all[...]).astype(BF)

    inputs = [
        pl.BlockSpec((n, depth), lambda i, t: (0, t[0, i])),
        pl.BlockSpec((1, n, depth), lambda i, t: (t[0, i] // per, 0, t[0, i] % per)),
        pl.BlockSpec((n, 3 * m), lambda i, t: (0, 0)),
        pl.BlockSpec((n, m), lambda i, t: (0, 0)),
    ]
    return call(
        body,
        steps,
        inputs * 2,
        pl.BlockSpec((depth, 4 * m), lambda i, t: (i, 0)),
        jax.ShapeDtypeStruct((steps * depth, 4 * m), BF),
        [pltpu.VMEM((2 * n, 3 * m), BF), pltpu.VMEM((2 * n, m), BF)],
        2 * n * width * 4 * m,
        width * 4 * m,
        table,
        a,
        o,
        dp,
        d_h,
        *mates,
    )


def band_list(width, c, band):
    if band % 128:
        return [slice(0, width)]
    rows = width // (c * band)
    return [slice((r * c + q) * band, (r * c + q + 1) * band) for q in range(c) for r in range(rows)]


def mlp(b, w, band):
    n, width = b.shape
    _, c, _, w2, f = w.shape
    bands = band_list(width, c, band)

    def body(_, b_ref, w_ref, gate_ref, up_ref, m_ref, y_ref, held, held_down, turned, sems):
        pairs = [(w_ref.at[i, :, pl.ds(0, 2)], held.at[i]) for i in range(2)]
        copies = fetch(pairs + [(w_ref.at[i, :, 2], held_down.at[i]) for i in range(2)], sems)
        at = 0
        for part in bands:
            size = part.stop - part.start
            turned[:, at : at + size] = b_ref[:, part]
            at += size
        copies[0].wait()
        gate_ref[...] = dot(turned[...], held[0].reshape(width, f))
        copies[1].wait()
        up_ref[...] = dot(turned[...], held[1].reshape(width, f))
        gate = gate_ref[...]
        m_ref[...] = (gate * jax.nn.sigmoid(gate) * up_ref[...]).astype(BF)
        for i in range(2):
            copies[2 + i].wait()
            y = dot_nt(m_ref[...], held_down[i].reshape(c * w2, f)).astype(BF)
            for k in range(c):
                y_ref[:, (2 * k + i) * w2 : (2 * k + i + 1) * w2] = y[:, k * w2 : (k + 1) * w2]

    return call(
        body,
        1,
        [whole(n, width), HBM],
        [whole(n, f)] * 3 + [whole(n, width)],
        [jax.ShapeDtypeStruct((n, f), F32)] * 2 + [jax.ShapeDtypeStruct((n, f), BF), jax.ShapeDtypeStruct((n, width), BF)],
        [
            pltpu.VMEM((2, c, 2, w2, f), BF),
            pltpu.VMEM((2, c, w2, f), BF),
            pltpu.VMEM((n, width), BF),
            pltpu.SemaphoreType.DMA((4,)),
        ],
        2 * n * width * 3 * f,
        2 * width * 3 * f,
        no_table(),
        b,
        w,
    )


def mlp_back(dy, gate, up, w, band):
    n, width = dy.shape
    _, c, _, w2, f = w.shape
    half = width // 2
    bands = band_list(width, c, band)

    def body(_, dy_ref, gate_ref, up_ref, w_ref, d_ref, db_ref, held, held_down, acc, sems):
        pairs = [(w_ref.at[i, :, 2], held_down.at[i]) for i in range(2)]
        copies = fetch(pairs + [(w_ref.at[i, :, pl.ds(0, 2)], held.at[i]) for i in range(2)], sems)
        for i in range(2):
            ours = jnp.concatenate([dy_ref[:, (2 * k + i) * w2 : (2 * k + i + 1) * w2] for k in range(c)], axis=1)
            copies[i].wait()
            part = dot(ours, held_down[i].reshape(c * w2, f))
            acc[...] = part if i == 0 else acc[...] + part
        dm, gate = acc[...], gate_ref[...]
        sig = jax.nn.sigmoid(gate)
        d_ref[0] = (dm * up_ref[...] * sig * (1.0 + gate * (1.0 - sig))).astype(BF)
        d_ref[1] = (dm * gate * sig).astype(BF)
        copies[2].wait()
        copies[3].wait()
        for i in range(2):
            part = slice(i * c // 2, (i + 1) * c // 2)
            back = dot_nt(d_ref[0], held[0, part].reshape(half, f)) + dot_nt(d_ref[1], held[1, part].reshape(half, f))
            back = back.astype(BF)
            if len(bands) == 1:
                db_ref[:, i * half : (i + 1) * half] = back
            for j in range(len(bands) // 2):
                db_ref[:, bands[i * len(bands) // 2 + j]] = back[:, j * band : (j + 1) * band]

    return call(
        body,
        1,
        [whole(n, width), whole(n, f), whole(n, f), HBM],
        [whole(2, n, f), whole(n, width)],
        [jax.ShapeDtypeStruct((2, n, f), BF), jax.ShapeDtypeStruct((n, width), BF)],
        [
            pltpu.VMEM((2, c, 2, w2, f), BF),
            pltpu.VMEM((2, c, w2, f), BF),
            pltpu.VMEM((n, f), F32),
            pltpu.SemaphoreType.DMA((4,)),
        ],
        2 * n * width * 3 * f,
        2 * width * 3 * f,
        no_table(),
        dy,
        gate,
        up,
        w,
    )


def mlp_grads(b, d, dy, m, mates, me_s, band):
    n, width = b.shape
    f = m.shape[1]
    c = lax.axis_size("col")
    depth, w2 = width // c, width // c // 2

    def body(_, b_ref, d_ref, dy_ref, m_ref, b2_ref, d2_ref, dy2_ref, m2_ref, out_ref, d_all, m_all):
        @pl.when(pl.program_id(0) == 0)
        def _():
            d_all[:n], d_all[n:] = d_ref[0], d2_ref[0]
            m_all[:n], m_all[n:] = m_ref[...], m2_ref[...]

        def rows_of(ref):
            if band % 128:
                return ref[:, pl.ds(pl.multiple_of(pl.program_id(0) * depth, depth), depth)]
            at = [pl.multiple_of((r * c + pl.program_id(0)) * band, band) for r in range(depth // band)]
            return jnp.concatenate([ref[:, pl.ds(i, band)] for i in at], axis=1)

        out_ref[0, :depth] = dot_tn(jnp.concatenate([rows_of(b_ref), rows_of(b2_ref)]), d_all[...]).astype(BF)
        out_ref[0, depth:] = dot_tn(jnp.concatenate([dy_ref[...], dy2_ref[...]]), m_all[...]).astype(BF)

    inputs = [
        pl.BlockSpec((n, width), lambda i, t: (0, 0)),
        pl.BlockSpec((1, n, f), lambda i, t: (t[0, 0], 0, 0)),
        pl.BlockSpec((n, w2), lambda i, t: (0, i * 2 + t[0, 0])),
        pl.BlockSpec((n, f), lambda i, t: (0, 0)),
    ]
    return call(
        body,
        c,
        inputs * 2,
        pl.BlockSpec((1, depth + w2, f), lambda i, t: (i, 0, 0)),
        jax.ShapeDtypeStruct((c, depth + w2, f), BF),
        [pltpu.VMEM((2 * n, f), BF)] * 2,
        2 * n * width * 3 * f,
        width * 3 * f,
        me_s.reshape(1, 1),
        b,
        d,
        dy,
        m,
        *mates,
    )


def swap(value):
    return lax.ppermute(value, "section", [(0, 1), (1, 0)])


def hop(value, axis, step):
    return lax.ppermute(value, axis, [(i, i ^ step) for i in range(lax.axis_size(axis))])


def pick(stack, index):
    return lax.dynamic_index_in_dim(stack, index, 0, keepdims=False)


def place_all(pieces, me):
    out = jnp.zeros((len(pieces), *pieces[0].shape), pieces[0].dtype)
    for k, piece in enumerate(pieces):
        out = lax.dynamic_update_index_in_dim(out, piece, me ^ k, 0)
    return out


def send_all(value, axis):
    return [value] + [hop(value, axis, k) for k in range(1, lax.axis_size(axis))]


def send_parts(stack, axis):
    me = lax.axis_index(axis)
    return [pick(stack, me)] + [hop(pick(stack, me ^ k), axis, k) for k in range(1, stack.shape[0])]


def by_place(pieces, me):
    bit = 1
    while bit < len(pieces):
        flip = (me & bit) != 0
        pieces = [jnp.where(flip, pieces[i ^ bit], pieces[i]) for i in range(len(pieces))]
        bit *= 2
    return pieces


def add_all(parts):
    out = parts[0].astype(F32)
    for part in parts[1:]:
        out = out + part.astype(F32)
    return out


def shards(
    tokens_in, out_grad, segments, positions, w_qkv, b_qkv, w_out, w_gate_up, w_down, norm_gains, norm_biases
):
    rows, cols = lax.axis_size("row"), lax.axis_size("col")
    me_s = lax.axis_index("section")
    first = me_s == 0
    seq, dc = tokens_in.shape[1:]
    width = dc * cols
    tq = seq // cols
    dr = width // rows
    fc, fr = w_gate_up.shape[3], w_down.shape[1]
    w2, v2 = dc // 2, dr // 2
    sub = rows // cols
    band = dr // cols

    def own_first(a, b):
        return jnp.where(first, a, b), jnp.where(first, b, a)

    def to_gate(x):
        if band % 128 == 0:
            return x
        return x.reshape(-1, rows, cols, band).transpose(0, 2, 1, 3).reshape(-1, width)

    def from_gate(x):
        if band % 128 == 0:
            return x
        return x.reshape(-1, cols, rows, band).transpose(0, 2, 1, 3).reshape(-1, width)

    def to_features(stack):
        return stack.transpose(1, 0, 2).reshape(stack.shape[1], width)

    def by_feature(x):
        return x.reshape(x.shape[0], cols, dc).transpose(1, 0, 2)

    me_r, me_c = lax.axis_index("row"), lax.axis_index("col")
    qo = jnp.concatenate([w_qkv[0, :, 0], w_qkv[0, :, 1], w_qkv[0, :, 2], w_out[0]], axis=1)
    qo_half = trade(qo.reshape(2, v2, 4 * dc), "section")
    qo_half, w_gate_up = tie(qo_half, w_gate_up)

    aligned = v2 % 128 == 0
    mine = 2 * jnp.arange(rows, dtype=jnp.int32) + me_s

    def gather_qo(layer):
        return lax.all_gather(qo_half[layer], ("row", "section"), axis=0, tiled=True)

    wqo0 = gather_qo(0)
    g_half = trade(w_gate_up[0].transpose(1, 0, 2), "section")

    def to_blocks(bands):
        return bands.reshape(cols, band, sub, fr).transpose(0, 2, 1, 3).reshape(rows, band, fr)

    def from_blocks(blocks):
        return blocks.reshape(cols, sub, band, fr).transpose(0, 2, 1, 3).reshape(cols, band, fc)

    def gather_mlp(piece, down):
        both = jnp.concatenate([piece.reshape(dc, fr), down])
        return lax.all_gather(both, ("section", "col"), axis=0, tiled=True).reshape(2, cols, 3, w2, fr)

    own_tokens = pick(tokens_in, me_s)
    own_grad = pick(out_grad, me_s)
    both = jnp.stack([own_tokens, own_grad]).reshape(2, cols, tq, dc).transpose(1, 0, 2, 3)
    small = jnp.concatenate([norm_gains[0], norm_biases[0], b_qkv[0]], axis=0)
    g_half, both, small, w_down = tie(g_half, both, small, w_down)
    g_parts = send_parts(g_half[0].reshape(cols, band, fc), "col")
    d_half = trade(w_down[0].T.reshape(2, w2, fr), "section")
    small = gather(small, "section")
    wide = gather(small[:, :4], "col").transpose(1, 2, 0, 3).reshape(2, 4, width).astype(F32)
    bias = small[:, 4:].astype(F32).reshape(2, 1, 3 * dc)

    segment = pick(segments, me_s)
    position = pick(positions, me_s)
    place = jnp.arange(seq, dtype=jnp.int32)
    allowed = (segment[:, None] == segment[None, :]) & (place[None, :] <= place[:, None])
    mask = allowed.astype(F32)
    freq = jnp.power(ROPE_BASE, -2.0 * jnp.arange(ROT // 2, dtype=F32) / ROT)
    angles = position.astype(F32)[:, None] * freq[None, :]
    cosines, sines = jnp.cos(angles), jnp.sin(angles)
    rest = jnp.zeros((seq, HEAD_DIM - ROT), F32)
    none = jnp.zeros_like(sines)
    tables = jnp.stack(
        [
            jnp.concatenate([cosines, cosines, rest + 1.0] * 2, axis=1),
            jnp.concatenate([-sines, none, rest] * 2, axis=1),
            jnp.concatenate([none, sines, rest] * 2, axis=1),
        ]
    )

    tables, mask, wide, *g_parts = tie(tables, mask, wide, *g_parts)
    blocks = to_blocks(place_all(g_parts, me_c))
    blocks, both = tie(blocks, both)
    g_parts = send_parts(blocks, "row")
    late_parts = send_parts(g_half[1].reshape(cols, band, fc), "col")
    both = trade(both, "col").transpose(1, 2, 0, 3).reshape(2, tq, width)
    x = both[0].astype(F32)

    weights, kept, outputs = [], [], []
    for layer in range(2):
        g1, g2, c1, c2 = wide[layer]
        a, scaled1, inv1 = norm(x, g1, c1)
        if layer == 0:
            a, *parts = tie(a, *g_parts, *late_parts)
            wgd0 = gather_mlp(place_all(parts[:rows], me_r), d_half[0])
            g_parts = send_parts(to_blocks(place_all(parts[rows:], me_c)), "row")
        a_all = gather(a, "col").reshape(seq, width)
        a_kept = a_all
        if layer == 0:
            wqo = wqo0
        else:
            wqo = wqo1
        a_mate = swap(a_kept)
        qkv, o = attention(a_all, wqo, bias[layer], tables, mask)
        if layer == 1:
            o, grad = tie(o, both[1])
            dy_parts = send_all(grad, "row")
        o_all = gather(o, "col")
        o_kept = o_all
        o_mate = swap(o_kept)
        out = heads_out(o_all, wqo)
        if layer == 0:
            out, *g_parts = tie(out, *g_parts)
            g_piece = place_all(g_parts, me_r)
        got = trade(out.reshape(cols, tq, dc), "col")
        h = x + to_features(got).astype(F32)
        b, scaled2, inv2 = norm(h.astype(BF).astype(F32), g2, c2)
        b_all = gather(to_gate(b), "row").reshape(rows * tq, width)
        b_mate = swap(b_all)
        if layer == 0:
            b_all, qo_half = tie(b_all, qo_half)
            wqo1 = gather_qo(1)
        wgd = wgd0 if layer == 0 else wgd1
        weights.append((wqo, wgd))
        gate, up, m, partial = mlp(b_all, wgd, band)
        m_mate = swap(m)
        if layer == 0:
            gate, g_piece = tie(gate, g_piece)
            wgd1 = gather_mlp(g_piece, d_half[1])
        else:
            gate, *parts = tie(gate, *dy_parts)
            dy_all = place_all(parts, me_r).reshape(rows * tq, width)
        partial = partial.reshape(rows, tq, width)
        if layer == 0:
            y = h + total(partial, "row")
            x = y.astype(BF).astype(F32)
            outputs.append(y)
        else:
            y_parts = send_parts(partial, "row")
        kept.append((a_kept, a_mate, scaled1, inv1, qkv, o_kept, o_mate, scaled2, inv2, b_all, b_mate, gate, up, m, m_mate))

    def to_output(pair):
        mine, theirs = own_first(*(part.astype(BF) for part in pair))
        both = jnp.stack(own_first(mine, swap(theirs)))
        parts = send_parts(both.reshape(2, tq, cols, dc).transpose(2, 0, 1, 3), "col")
        return jnp.concatenate(by_place(parts, me_c), axis=1).astype(F32)[None]

    input_grads, qo_grads, g_grads, d_grads, norm_sums, bias_sums = ([None] * 2 for _ in range(6))
    grad = grad.astype(F32)
    for layer in (1, 0):
        g1, g2, c1, c2 = wide[layer]
        wqo, wgd = weights[layer]
        a_all, a_mate, scaled1, inv1, qkv, o_all, o_mate, scaled2, inv2, b_all, b_mate, gate, up, m, m_mate = kept[layer]
        if layer == 0:
            dy_all = gather(grad.astype(BF), "row").reshape(rows * tq, width)
            dy_all, gd_late = tie(dy_all, gd_late)
        dy_mate = swap(dy_all)
        d, partial = mlp_back(dy_all, gate, up, wgd, band)
        partial, d, dy_all, m, b_all = tie(partial, d, dy_all, m, b_all)
        got = total(partial.reshape(rows, tq, width), "row")
        wide_grad = mlp_grads(b_all, d, dy_all, m, (b_mate, swap(d), dy_mate, m_mate), me_s, band).reshape(-1, fr)
        got, wide_grad = tie(got, wide_grad)
        if layer == 0:
            got, qo_grads[1], placed = tie(got, qo_grads[1], to_output(outputs))
        gd_piece = lax.psum_scatter(wide_grad, "col", scatter_dimension=0, tiled=True)
        back, gain2, shift2 = norm_back(from_gate(got), scaled2, inv2, g2)
        dh = grad + back
        dh_all = trade(by_feature(dh.astype(BF)), "col").reshape(seq, dc)
        dh_side = dh_all
        dh_mate = swap(dh_side)
        if layer == 0:
            g_late = send_parts(gd_late[:dc].reshape(rows, band, fr), "row")
        d_o = total(heads_back(dh_all, wqo), "col").astype(BF)
        if layer == 1:
            d_o, *parts = tie(d_o, *y_parts)
            outputs.append(h + add_all(parts))
        else:
            d_o, *g_late = tie(d_o, *g_late)
        dp, bias_sum, partial = attention_back(d_o, qkv, wqo, tables, mask)
        partial, dp = tie(partial, dp)
        got = total(partial.reshape(cols, tq, width), "col")
        if aligned:
            mates = (a_mate, o_mate, swap(dp), dh_mate)
            wide_grad = attention_grads(a_all, o_all, dp, dh_side, mates, mine[None])
            got, wide_grad = tie(got, wide_grad)
            if layer == 0:
                got, wide_grad, gd_piece = tie(got, wide_grad, gd_piece)
                g_parts = send_parts(gd_piece[:dc].reshape(rows, band, fr), "row")
                wide_grad, *g_parts = tie(wide_grad, *g_parts)
            qo_grads[layer] = lax.psum_scatter(wide_grad, "row", scatter_dimension=0, tiled=True)
        else:
            q_wide, o_wide = dot_tn(a_all, dp).astype(BF), dot_tn(to_features(o_all), dh_side).astype(BF)
            q_wide = lax.psum_scatter(q_wide, ("row", "section"), scatter_dimension=0, tiled=True)
            o_wide = lax.psum_scatter(o_wide, ("row", "section"), scatter_dimension=0, tiled=True)
            qo_grads[layer] = jnp.concatenate([q_wide, o_wide], axis=1)
        back, gain1, shift1 = norm_back(got, scaled1, inv1, g1)
        dx = dh + back
        norm_sums[layer] = jnp.stack([gain1, gain2, shift1, shift2])
        bias_sums[layer] = bias_sum.reshape(3, dc)
        grad = dx.astype(BF).astype(F32)
        d_grads[layer] = gd_piece[dc:]
        if layer == 1:
            gd_late = gd_piece
        else:
            sums = total(jnp.stack(norm_sums).reshape(2, 4, cols, dc).transpose(2, 0, 1, 3), "col")
            sums = jnp.concatenate([sums, jnp.stack(bias_sums)], axis=1)
            sums = total(add_all(send_all(sums, "row")), "section")
            sums, *parts = tie(sums, *g_parts, *g_late)
            blocks = place_all(parts[:rows], me_r)
            g_late = send_parts(from_blocks(place_all(parts[rows:], me_r)), "col")
            blocks, *g_late = tie(blocks, *g_late)
            g_grads[1] = place_all(g_late, me_c).reshape(dr, fc)
            g_grads[0] = trade(from_blocks(blocks), "col").reshape(dr, fc)
        input_grads[layer] = dx

    def unshare(pair):
        return trade(jnp.stack(pair), "section")

    qo_grads = unshare(qo_grads).reshape(dr, 4 * dc).astype(F32)
    qo_grads = [qo_grads[:, i * dc : (i + 1) * dc] for i in range(4)]
    return (
        placed,
        to_output(input_grads),
        jnp.stack(qo_grads[:3], axis=1)[None],
        sums[None, 4:],
        qo_grads[3][None],
        unshare(g_grads).astype(F32).transpose(1, 0, 2)[None],
        unshare(d_grads).astype(F32).reshape(dc, fr).T[None],
        sums[None, 0:2],
        sums[None, 2:4],
    )


def solution(mesh):
    return jax.shard_map(
        shards,
        mesh=mesh,
        in_specs=(
            P(None, "row", "col"),
            P(None, "row", "col"),
            P(None, "row"),
            P(None, "row"),
            P("section", "row", None, "col"),
            P("section", None, "col"),
            P("section", "row", "col"),
            P("section", "row", None, "col"),
            P("section", "row", "col"),
            P("section", None, "col"),
            P("section", None, "col"),
        ),
        out_specs=(
            P("section", None, "row", "col"),
            P("section", None, "row", "col"),
            P("section", "row", None, "col"),
            P("section", None, "col"),
            P("section", "row", "col"),
            P("section", "row", None, "col"),
            P("section", "row", "col"),
            P("section", None, "col"),
            P("section", None, "col"),
        ),
        check_vma=False,
    )
```

```python
import jax
import jax.numpy as jnp
from jax import lax
from jax.experimental import pallas as pl
from jax.experimental.pallas import tpu as pltpu
from jax.sharding import PartitionSpec as P

HEAD_DIM = 64
ROT = 16
NORM_EPSILON = 1e-05
ROPE_BASE = 10000.0
SCORE_SCALE = 0.125
MASKED_SCORE = -1e30
BF = jnp.bfloat16
F32 = jnp.float32


def trade(stack, axis):
    return lax.all_to_all(stack, axis, split_axis=0, concat_axis=0)


def gather(value, axis):
    return trade(jnp.broadcast_to(value, (lax.axis_size(axis), *value.shape)), axis)


def total(stack, axis):
    return jnp.sum(trade(stack, axis).astype(F32), axis=0)


def tie(point, *values):
    return lax.optimization_barrier((point, *values))


def dot(a, b):
    return lax.dot_general(a, b, (((1,), (0,)), ((), ())), preferred_element_type=F32)


def dot_nt(a, b):
    return lax.dot_general(a, b, (((1,), (1,)), ((), ())), preferred_element_type=F32)


def dot_tn(a, b):
    return lax.dot_general(a, b, (((0,), (0,)), ((), ())), preferred_element_type=F32)


def norm(values, gain, shift):
    mean_value = jnp.mean(values, axis=-1, keepdims=True)
    centred = values - mean_value
    variance = jnp.mean(centred * centred, axis=-1, keepdims=True)
    inv = lax.rsqrt(variance + NORM_EPSILON)
    scaled = centred * inv
    return (scaled * gain + shift).astype(BF), scaled, inv


def norm_back(grad, scaled, inv, gain):
    e = grad * gain
    mean_e = jnp.mean(e, axis=-1, keepdims=True)
    mean_p = jnp.mean(e * scaled, axis=-1, keepdims=True)
    return inv * (e - mean_e - scaled * mean_p), jnp.sum(grad * scaled, axis=0), jnp.sum(grad, axis=0)


def call(body, grid, in_specs, out_specs, out_shape, scratch, flops, moved, table, *args):
    return pl.pallas_call(
        body,
        grid_spec=pltpu.PrefetchScalarGridSpec(
            num_scalar_prefetch=1,
            grid=(grid,),
            in_specs=in_specs,
            out_specs=out_specs,
            scratch_shapes=scratch,
        ),
        out_shape=out_shape,
        compiler_params=pltpu.CompilerParams(vmem_limit_bytes=56 * 2**20),
        cost_estimate=pl.CostEstimate(flops=int(flops), bytes_accessed=int(moved), transcendentals=0),
    )(table, *args)


def no_table():
    return jnp.zeros((1, 1), jnp.int32)


def turn(x, cosines, sines, sign):
    ahead = pltpu.roll(x, 128 - ROT // 2, 1)
    behind = pltpu.roll(x, ROT // 2, 1)
    return x * cosines + sign * (ahead * sines[0] + behind * sines[1])


def head_lanes(n):
    lanes = lax.broadcasted_iota(jnp.int32, (n, 128), 1)
    return lanes < HEAD_DIM


def softmax_of(q, k, allowed):
    scores = jnp.where(allowed, dot_nt(q, k) * SCORE_SCALE, MASKED_SCORE)
    shifted = jnp.exp(scores - jnp.max(scores, axis=1, keepdims=True))
    return shifted / jnp.sum(shifted, axis=1, keepdims=True)


def whole(*shape):
    return pl.BlockSpec(shape, lambda i, t: (0,) * len(shape))


HBM = pl.BlockSpec(memory_space=pl.ANY)


def fetch(pairs, sems):
    copies = [pltpu.make_async_copy(src, dst, sems.at[i]) for i, (src, dst) in enumerate(pairs)]
    for copy in copies:
        copy.start()
    return copies


def attention(a, w, bias, tables, mask):
    n, width = a.shape
    m = w.shape[1] // 4
    half = width // 2

    def body(_, a_ref, w_ref, bias_ref, tab_ref, mask_ref, qkv_ref, o_ref, held, acc, sems):
        parts = [pl.ds(i * half, half) for i in range(2)]
        copies = fetch([(w_ref.at[part, pl.ds(0, 3 * m)], held.at[part]) for part in parts], sems)
        copies[0].wait()
        acc[...] = dot(a_ref[:, :half], held[:half]) + bias_ref[...]
        copies[1].wait()
        acc[...] += dot(a_ref[:, half:], held[half:])
        low = head_lanes(n)
        zero = jnp.zeros((n, 128), BF)
        allowed = mask_ref[...] > 0
        cosines, sines = tab_ref[0], (tab_ref[1], tab_ref[2])
        for pair in range(m // 128):
            at = pair * 128
            q = turn(acc[:, at : at + 128], cosines, sines, 1.0).astype(BF)
            k = turn(acc[:, m + at : m + at + 128], cosines, sines, 1.0).astype(BF)
            v = acc[:, 2 * m + at : 2 * m + at + 128].astype(BF)
            qkv_ref[:, at : at + 128] = q
            qkv_ref[:, m + at : m + at + 128] = k
            qkv_ref[:, 2 * m + at : 2 * m + at + 128] = v
            p0 = softmax_of(jnp.where(low, q, zero), k, allowed).astype(BF)
            p1 = softmax_of(jnp.where(low, zero, q), k, allowed).astype(BF)
            o_ref[:, at : at + 128] = jnp.where(low, dot(p0, v), dot(p1, v)).astype(BF)

    return call(
        body,
        1,
        [whole(n, width), HBM, whole(1, 3 * m), whole(3, n, 128), whole(n, n)],
        [whole(n, 3 * m), whole(n, m)],
        [jax.ShapeDtypeStruct((n, 3 * m), BF), jax.ShapeDtypeStruct((n, m), BF)],
        [pltpu.VMEM((width, 3 * m), BF), pltpu.VMEM((n, 3 * m), F32), pltpu.SemaphoreType.DMA((2,))],
        2 * n * width * 3 * m,
        2 * width * 3 * m,
        no_table(),
        a,
        w,
        bias,
        tables,
        mask,
    )


def attention_back(d_o, qkv, w, tables, mask):
    n, m = d_o.shape
    width = w.shape[0]
    half = width // 2

    def body(_, d_ref, qkv_ref, w_ref, tab_ref, mask_ref, dp_ref, sum_ref, da_ref, held, sems):
        parts = [pl.ds(i * half, half) for i in range(2)]
        copies = fetch([(w_ref.at[part, pl.ds(0, 3 * m)], held.at[part]) for part in parts], sems)
        low = head_lanes(n)
        zero = jnp.zeros((n, 128), BF)
        allowed = mask_ref[...] > 0
        cosines, sines = tab_ref[0], (tab_ref[1], tab_ref[2])
        for pair in range(m // 128):
            at = pair * 128
            q = qkv_ref[:, at : at + 128]
            k = qkv_ref[:, m + at : m + at + 128]
            v = qkv_ref[:, 2 * m + at : 2 * m + at + 128]
            g = d_ref[:, at : at + 128]
            out = []
            for mine in (True, False):
                pick_q = jnp.where(low, q, zero) if mine else jnp.where(low, zero, q)
                pick_g = jnp.where(low, g, zero) if mine else jnp.where(low, zero, g)
                probs = softmax_of(pick_q, k, allowed)
                d_probs = dot_nt(pick_g, v)
                row = jnp.sum(d_probs * probs, axis=1, keepdims=True)
                ds = (probs * (d_probs - row)).astype(BF)
                out.append((dot(ds, k), dot_tn(ds, q), dot_tn(probs.astype(BF), g)))
            dq, dk, dv = (jnp.where(low, x, y) for x, y in zip(*out))
            dq = turn(dq * SCORE_SCALE, cosines, sines, -1.0)
            dk = turn(dk * SCORE_SCALE, cosines, sines, -1.0)
            for place, part in enumerate((dq, dk, dv)):
                part = part.astype(BF)
                dp_ref[:, place * m + at : place * m + at + 128] = part
                sum_ref[:, place * m + at : place * m + at + 128] = jnp.sum(part.astype(F32), axis=0, keepdims=True)
        for i, copy in enumerate(copies):
            copy.wait()
            da_ref[:, i * half : (i + 1) * half] = dot_nt(dp_ref[...], held[i * half : (i + 1) * half]).astype(BF)

    return call(
        body,
        1,
        [whole(n, m), whole(n, 3 * m), HBM, whole(3, n, 128), whole(n, n)],
        [whole(n, 3 * m), whole(1, 3 * m), whole(n, width)],
        [
            jax.ShapeDtypeStruct((n, 3 * m), BF),
            jax.ShapeDtypeStruct((1, 3 * m), F32),
            jax.ShapeDtypeStruct((n, width), BF),
        ],
        [pltpu.VMEM((width, 3 * m), BF), pltpu.SemaphoreType.DMA((2,))],
        2 * n * width * 3 * m,
        2 * width * 3 * m,
        no_table(),
        d_o,
        qkv,
        w,
        tables,
        mask,
    )


def heads_out(o, w):
    c, n, m = o.shape

    def body(_, o_ref, w_ref, out_ref, held, sems):
        (copy,) = fetch([(w_ref.at[:, pl.ds(3 * m, m)], held)], sems)
        o_wide = jnp.concatenate([o_ref[i] for i in range(c)], axis=1)
        copy.wait()
        out_ref[...] = dot(o_wide, held[...]).astype(BF)

    return call(
        body,
        1,
        [whole(c, n, m), HBM],
        whole(n, m),
        jax.ShapeDtypeStruct((n, m), BF),
        [pltpu.VMEM((c * m, m), BF), pltpu.SemaphoreType.DMA((1,))],
        2 * c * n * m * m,
        2 * c * m * m,
        no_table(),
        o,
        w,
    )


def heads_back(d_h, w):
    n, m = d_h.shape
    c = w.shape[0] // m

    def body(_, d_ref, w_ref, out_ref, held, sems):
        (copy,) = fetch([(w_ref.at[:, pl.ds(3 * m, m)], held)], sems)
        copy.wait()
        back = dot_nt(d_ref[...], held[...]).astype(BF)
        for i in range(c):
            out_ref[i] = back[:, i * m : (i + 1) * m]

    return call(
        body,
        1,
        [whole(n, m), HBM],
        whole(c, n, m),
        jax.ShapeDtypeStruct((c, n, m), BF),
        [pltpu.VMEM((c * m, m), BF), pltpu.SemaphoreType.DMA((1,))],
        2 * c * n * m * m,
        2 * c * m * m,
        no_table(),
        d_h,
        w,
    )


def attention_grads(a, o, dp, d_h, mates, table):
    n, width = a.shape
    m = d_h.shape[1]
    steps = table.shape[1]
    depth = width // (2 * steps)
    per = m // depth

    def body(_, a_ref, o_ref, dp_ref, dh_ref, a2_ref, o2_ref, dp2_ref, dh2_ref, out_ref, dp_all, dh_all):
        @pl.when(pl.program_id(0) == 0)
        def _():
            dp_all[:n], dp_all[n:] = dp_ref[...], dp2_ref[...]
            dh_all[:n], dh_all[n:] = dh_ref[...], dh2_ref[...]

        out_ref[:, : 3 * m] = dot_tn(jnp.concatenate([a_ref[...], a2_ref[...]]), dp_all[...]).astype(BF)
        out_ref[:, 3 * m :] = dot_tn(jnp.concatenate([o_ref[0], o2_ref[0]]), dh_all[...]).astype(BF)

    inputs = [
        pl.BlockSpec((n, depth), lambda i, t: (0, t[0, i])),
        pl.BlockSpec((1, n, depth), lambda i, t: (t[0, i] // per, 0, t[0, i] % per)),
        pl.BlockSpec((n, 3 * m), lambda i, t: (0, 0)),
        pl.BlockSpec((n, m), lambda i, t: (0, 0)),
    ]
    return call(
        body,
        steps,
        inputs * 2,
        pl.BlockSpec((depth, 4 * m), lambda i, t: (i, 0)),
        jax.ShapeDtypeStruct((steps * depth, 4 * m), BF),
        [pltpu.VMEM((2 * n, 3 * m), BF), pltpu.VMEM((2 * n, m), BF)],
        2 * n * width * 4 * m,
        width * 4 * m,
        table,
        a,
        o,
        dp,
        d_h,
        *mates,
    )


def band_list(width, c, band):
    if band % 128:
        return [slice(0, width)]
    rows = width // (c * band)
    return [slice((r * c + q) * band, (r * c + q + 1) * band) for q in range(c) for r in range(rows)]


def mlp_copies(w_ref, down_refs, held, held_down):
    gate_up = [(w_ref.at[i, :, pl.ds(0, 2)], held.at[i]) for i in range(2)]
    sources = down_refs or [w_ref.at[i, :, 2] for i in range(2)]
    return gate_up, [(source, held_down.at[i]) for i, source in enumerate(sources)]


def mlp(b, w, down, halves, band):
    n, width = b.shape
    _, c, _, w2, f = w.shape
    bands = band_list(width, c, band)

    def body(t, b_ref, w_ref, *rest):
        down_refs, (gate_ref, up_ref, m_ref, y_ref, held, held_down, turned, sems) = rest[: len(down)], rest[len(down) :]
        first, later = mlp_copies(w_ref, down_refs, held, held_down)
        copies = fetch(first + later, sems)
        at = 0
        for part in bands:
            size = part.stop - part.start
            turned[:, at : at + size] = b_ref[:, part]
            at += size
        copies[0].wait()
        gate_ref[...] = dot(turned[...], held[0].reshape(width, f))
        copies[1].wait()
        up_ref[...] = dot(turned[...], held[1].reshape(width, f))
        gate = gate_ref[...]
        m_ref[...] = (gate * jax.nn.sigmoid(gate) * up_ref[...]).astype(BF)
        for i in range(2):
            copies[2 + i].wait()
            y = dot_nt(m_ref[...], held_down[i].reshape(c * w2, f)).astype(BF)
            half = t[0, i]
            for k in range(c):
                y_ref[:, pl.ds(pl.multiple_of((2 * k + half) * w2, w2), w2)] = y[:, k * w2 : (k + 1) * w2]

    return call(
        body,
        1,
        [whole(n, width), HBM] + [HBM] * len(down),
        [whole(n, f)] * 3 + [whole(n, width)],
        [jax.ShapeDtypeStruct((n, f), F32)] * 2 + [jax.ShapeDtypeStruct((n, f), BF), jax.ShapeDtypeStruct((n, width), BF)],
        [
            pltpu.VMEM((2, c, 2, w2, f), BF),
            pltpu.VMEM((2, c, w2, f), BF),
            pltpu.VMEM((n, width), BF),
            pltpu.SemaphoreType.DMA((4,)),
        ],
        2 * n * width * 3 * f,
        2 * width * 3 * f,
        halves,
        b,
        w,
        *down,
    )


def mlp_back(dy, gate, up, w, down, halves, band):
    n, width = dy.shape
    _, c, _, w2, f = w.shape
    half = width // 2
    bands = band_list(width, c, band)

    def body(t, dy_ref, gate_ref, up_ref, w_ref, *rest):
        down_refs, (d_ref, db_ref, held, held_down, acc, sems) = rest[: len(down)], rest[len(down) :]
        later, first = mlp_copies(w_ref, down_refs, held, held_down)
        copies = fetch(first + later, sems)
        for i in range(2):
            at = t[0, i]
            ours = [dy_ref[:, pl.ds(pl.multiple_of((2 * k + at) * w2, w2), w2)] for k in range(c)]
            ours = jnp.concatenate(ours, axis=1)
            copies[i].wait()
            part = dot(ours, held_down[i].reshape(c * w2, f))
            acc[...] = part if i == 0 else acc[...] + part
        dm, gate = acc[...], gate_ref[...]
        sig = jax.nn.sigmoid(gate)
        d_ref[0] = (dm * up_ref[...] * sig * (1.0 + gate * (1.0 - sig))).astype(BF)
        d_ref[1] = (dm * gate * sig).astype(BF)
        copies[2].wait()
        copies[3].wait()
        for i in range(2):
            part = slice(i * c // 2, (i + 1) * c // 2)
            back = dot_nt(d_ref[0], held[0, part].reshape(half, f)) + dot_nt(d_ref[1], held[1, part].reshape(half, f))
            back = back.astype(BF)
            if len(bands) == 1:
                db_ref[:, i * half : (i + 1) * half] = back
            for j in range(len(bands) // 2):
                db_ref[:, bands[i * len(bands) // 2 + j]] = back[:, j * band : (j + 1) * band]

    return call(
        body,
        1,
        [whole(n, width), whole(n, f), whole(n, f), HBM] + [HBM] * len(down),
        [whole(2, n, f), whole(n, width)],
        [jax.ShapeDtypeStruct((2, n, f), BF), jax.ShapeDtypeStruct((n, width), BF)],
        [
            pltpu.VMEM((2, c, 2, w2, f), BF),
            pltpu.VMEM((2, c, w2, f), BF),
            pltpu.VMEM((n, f), F32),
            pltpu.SemaphoreType.DMA((4,)),
        ],
        2 * n * width * 3 * f,
        2 * width * 3 * f,
        halves,
        dy,
        gate,
        up,
        w,
        *down,
    )


def mlp_grads(b, d, dy, m, mates, me_s, band, merged):
    n, width = b.shape
    f = m.shape[1]
    c = lax.axis_size("col")
    depth, w2 = width // c, width // c // 2
    sizes = (depth + w2,) if merged else (depth, w2)

    def body(_, b_ref, d_ref, dy_ref, m_ref, b2_ref, d2_ref, dy2_ref, m2_ref, *rest):
        *outs, d_all, m_all = rest

        @pl.when(pl.program_id(0) == 0)
        def _():
            d_all[:n], d_all[n:] = d_ref[0], d2_ref[0]
            m_all[:n], m_all[n:] = m_ref[...], m2_ref[...]

        def rows_of(ref):
            if band % 128:
                return ref[:, pl.ds(pl.multiple_of(pl.program_id(0) * depth, depth), depth)]
            at = [pl.multiple_of((r * c + pl.program_id(0)) * band, band) for r in range(depth // band)]
            return jnp.concatenate([ref[:, pl.ds(i, band)] for i in at], axis=1)

        outs[0][0, :depth] = dot_tn(jnp.concatenate([rows_of(b_ref), rows_of(b2_ref)]), d_all[...]).astype(BF)
        start = depth if merged else 0
        outs[-1][0, start : start + w2] = dot_tn(jnp.concatenate([dy_ref[...], dy2_ref[...]]), m_all[...]).astype(BF)

    inputs = [
        pl.BlockSpec((n, width), lambda i, t: (0, 0)),
        pl.BlockSpec((1, n, f), lambda i, t: (t[0, 0], 0, 0)),
        pl.BlockSpec((n, w2), lambda i, t: (0, i * 2 + t[0, 0])),
        pl.BlockSpec((n, f), lambda i, t: (0, 0)),
    ]
    return call(
        body,
        c,
        inputs * 2,
        [pl.BlockSpec((1, size, f), lambda i, t: (i, 0, 0)) for size in sizes],
        [jax.ShapeDtypeStruct((c, size, f), BF) for size in sizes],
        [pltpu.VMEM((2 * n, f), BF)] * 2,
        2 * n * width * 3 * f,
        width * 3 * f,
        me_s.reshape(1, 1),
        b,
        d,
        dy,
        m,
        *mates,
    )


def swap(value):
    return lax.ppermute(value, "section", [(0, 1), (1, 0)])


def hop(value, axis, step):
    return lax.ppermute(value, axis, [(i, i ^ step) for i in range(lax.axis_size(axis))])


def pick(stack, index):
    return lax.dynamic_index_in_dim(stack, index, 0, keepdims=False)


def place_all(pieces, me):
    out = jnp.zeros((len(pieces), *pieces[0].shape), pieces[0].dtype)
    for k, piece in enumerate(pieces):
        out = lax.dynamic_update_index_in_dim(out, piece, me ^ k, 0)
    return out


def send_all(value, axis):
    return [value] + [hop(value, axis, k) for k in range(1, lax.axis_size(axis))]


def send_parts(stack, axis):
    me = lax.axis_index(axis)
    return [pick(stack, me)] + [hop(pick(stack, me ^ k), axis, k) for k in range(1, stack.shape[0])]


def by_place(pieces, me):
    bit = 1
    while bit < len(pieces):
        flip = (me & bit) != 0
        pieces = [jnp.where(flip, pieces[i ^ bit], pieces[i]) for i in range(len(pieces))]
        bit *= 2
    return pieces


def add_all(parts):
    out = parts[0].astype(F32)
    for part in parts[1:]:
        out = out + part.astype(F32)
    return out


def shards(
    tokens_in, out_grad, segments, positions, w_qkv, b_qkv, w_out, w_gate_up, w_down, norm_gains, norm_biases
):
    rows, cols = lax.axis_size("row"), lax.axis_size("col")
    me_s = lax.axis_index("section")
    first = me_s == 0
    seq, dc = tokens_in.shape[1:]
    width = dc * cols
    tq = seq // cols
    dr = width // rows
    fc, fr = w_gate_up.shape[3], w_down.shape[1]
    w2, v2 = dc // 2, dr // 2
    sub = rows // cols
    band = dr // cols

    def own_first(a, b):
        return jnp.where(first, a, b), jnp.where(first, b, a)

    def to_gate(x):
        if band % 128 == 0:
            return x
        return x.reshape(-1, rows, cols, band).transpose(0, 2, 1, 3).reshape(-1, width)

    def from_gate(x):
        if band % 128 == 0:
            return x
        return x.reshape(-1, cols, rows, band).transpose(0, 2, 1, 3).reshape(-1, width)

    def to_features(stack):
        return stack.transpose(1, 0, 2).reshape(stack.shape[1], width)

    def by_feature(x):
        return x.reshape(x.shape[0], cols, dc).transpose(1, 0, 2)

    me_r, me_c = lax.axis_index("row"), lax.axis_index("col")
    qo = jnp.concatenate([w_qkv[0, :, 0], w_qkv[0, :, 1], w_qkv[0, :, 2], w_out[0]], axis=1)
    qo_half = trade(qo.reshape(2, v2, 4 * dc), "section")
    qo_half, w_gate_up = tie(qo_half, w_gate_up)

    aligned = v2 % 128 == 0
    mine = 2 * jnp.arange(rows, dtype=jnp.int32) + me_s

    def gather_qo(layer):
        return lax.all_gather(qo_half[layer], ("row", "section"), axis=0, tiled=True)

    wqo0 = gather_qo(0)
    g_half = trade(w_gate_up[0].transpose(1, 0, 2), "section")

    def to_blocks(bands):
        return bands.reshape(cols, band, sub, fr).transpose(0, 2, 1, 3).reshape(rows, band, fr)

    def from_blocks(blocks):
        return blocks.reshape(cols, sub, band, fr).transpose(0, 2, 1, 3).reshape(cols, band, fc)

    def gather_mlp(*pieces):
        whole_piece = jnp.concatenate([piece.reshape(-1, fr) for piece in pieces])
        return lax.all_gather(whole_piece, ("section", "col"), axis=0, tiled=True).reshape(2, cols, -1, w2, fr)

    plain = jnp.arange(2, dtype=jnp.int32).reshape(1, 2)
    halves_of = [plain, plain ^ me_s]

    def own_and_other(parts):
        own = place_all(parts, me_c)
        return own, swap(own)

    own_tokens = pick(tokens_in, me_s)
    own_grad = pick(out_grad, me_s)
    both = jnp.stack([own_tokens, own_grad]).reshape(2, cols, tq, dc).transpose(1, 0, 2, 3)
    small = jnp.concatenate([norm_gains[0], norm_biases[0], b_qkv[0]], axis=0)
    g_half, both, small, w_down = tie(g_half, both, small, w_down)
    g_parts = send_parts(g_half[0].reshape(cols, band, fc), "col")
    d_half = trade(w_down[0].T.reshape(2, w2, fr), "section")
    small = gather(small, "section")
    wide = gather(small[:, :4], "col").transpose(1, 2, 0, 3).reshape(2, 4, width).astype(F32)
    bias = small[:, 4:].astype(F32).reshape(2, 1, 3 * dc)

    segment = pick(segments, me_s)
    position = pick(positions, me_s)
    place = jnp.arange(seq, dtype=jnp.int32)
    allowed = (segment[:, None] == segment[None, :]) & (place[None, :] <= place[:, None])
    mask = allowed.astype(F32)
    freq = jnp.power(ROPE_BASE, -2.0 * jnp.arange(ROT // 2, dtype=F32) / ROT)
    angles = position.astype(F32)[:, None] * freq[None, :]
    cosines, sines = jnp.cos(angles), jnp.sin(angles)
    rest = jnp.zeros((seq, HEAD_DIM - ROT), F32)
    none = jnp.zeros_like(sines)
    tables = jnp.stack(
        [
            jnp.concatenate([cosines, cosines, rest + 1.0] * 2, axis=1),
            jnp.concatenate([-sines, none, rest] * 2, axis=1),
            jnp.concatenate([none, sines, rest] * 2, axis=1),
        ]
    )

    tables, mask, wide, *g_parts = tie(tables, mask, wide, *g_parts)
    blocks = to_blocks(place_all(g_parts, me_c))
    blocks, both = tie(blocks, both)
    g_parts = send_parts(blocks, "row")
    late_parts = send_parts(g_half[1].reshape(cols, band, fc), "col")
    both = trade(both, "col").transpose(1, 2, 0, 3).reshape(2, tq, width)
    x = both[0].astype(F32)

    weights, kept, outputs = [], [], []
    for layer in range(2):
        g1, g2, c1, c2 = wide[layer]
        a, scaled1, inv1 = norm(x, g1, c1)
        if layer == 0:
            a, *parts = tie(a, *g_parts, *late_parts)
            wg0 = gather_mlp(place_all(parts[:rows], me_r), d_half[0])
            g_parts = send_parts(to_blocks(place_all(parts[rows:], me_c)), "row")
            down = [(), None]
        a_all = gather(a, "col").reshape(seq, width)
        a_kept = a_all
        if layer == 0:
            wqo = wqo0
        else:
            wqo = wqo1
        a_mate = swap(a_kept)
        qkv, o = attention(a_all, wqo, bias[layer], tables, mask)
        if layer == 1:
            o, grad = tie(o, both[1])
            dy_parts = send_all(grad, "row")
        o_all = gather(o, "col")
        o_kept = o_all
        o_mate = swap(o_kept)
        out = heads_out(o_all, wqo)
        if layer == 0:
            out, *g_parts = tie(out, *g_parts)
            g_piece = place_all(g_parts, me_r)
        got = trade(out.reshape(cols, tq, dc), "col")
        h = x + to_features(got).astype(F32)
        b, scaled2, inv2 = norm(h.astype(BF).astype(F32), g2, c2)
        if layer == 0:
            b, qo_half = tie(b, qo_half)
            wqo1 = gather_qo(1)
        b_all = gather(to_gate(b), "row").reshape(rows * tq, width)
        b_mate = swap(b_all)
        wg = wg0 if layer == 0 else wg1
        weights.append((wqo, wg))
        gate, up, m, partial = mlp(b_all, wg, down[layer], halves_of[layer], band)
        m_mate = swap(m)
        if layer == 0:
            gate, g_piece = tie(gate, g_piece)
            wg1 = gather_mlp(g_piece)
        else:
            gate, *parts = tie(gate, *dy_parts)
            dy_all = place_all(parts, me_r).reshape(rows * tq, width)
        partial = partial.reshape(rows, tq, width)
        if layer == 0:
            y = h + total(partial, "row")
            y, *parts = tie(y, *send_all(d_half[1], "col"))
            down[1] = own_and_other(parts)
            x = y.astype(BF).astype(F32)
            outputs.append(y)
        else:
            y_parts = send_parts(partial, "row")
        kept.append((a_kept, a_mate, scaled1, inv1, qkv, o_kept, o_mate, scaled2, inv2, b_all, b_mate, gate, up, m, m_mate))

    def to_output(pair):
        mine, theirs = own_first(*(part.astype(BF) for part in pair))
        both = jnp.stack(own_first(mine, swap(theirs)))
        parts = send_parts(both.reshape(2, tq, cols, dc).transpose(2, 0, 1, 3), "col")
        return jnp.concatenate(by_place(parts, me_c), axis=1).astype(F32)[None]

    def unshare(pair):
        return trade(jnp.stack(pair), "section")

    input_grads, qo_grads, g_grads, d_grads, norm_sums, bias_sums = ([None] * 2 for _ in range(6))
    grad = grad.astype(F32)
    for layer in (1, 0):
        g1, g2, c1, c2 = wide[layer]
        wqo, wg = weights[layer]
        a_all, a_mate, scaled1, inv1, qkv, o_all, o_mate, scaled2, inv2, b_all, b_mate, gate, up, m, m_mate = kept[layer]
        if layer == 0:
            dy_all = gather(grad.astype(BF), "row").reshape(rows * tq, width)
        dy_mate = swap(dy_all)
        d, partial = mlp_back(dy_all, gate, up, wg, down[layer], halves_of[layer], band)
        partial, d, dy_all, m, b_all = tie(partial, d, dy_all, m, b_all)
        if layer == 0:
            partial, g_piece_late = tie(partial, g_piece_late)
        got = total(partial.reshape(rows, tq, width), "row")
        mates = (b_mate, swap(d), dy_mate, m_mate)
        wide_grad, *d_wide = mlp_grads(b_all, d, dy_all, m, mates, me_s, band, layer == 1)
        got, wide_grad = tie(got, wide_grad)
        if layer == 0:
            got, placed = tie(got, to_output(outputs))
        g_piece = lax.psum_scatter(wide_grad.reshape(-1, fr), "col", scatter_dimension=0, tiled=True)
        back, gain2, shift2 = norm_back(from_gate(got), scaled2, inv2, g2)
        dh = grad + back
        dh_all = trade(by_feature(dh.astype(BF)), "col").reshape(seq, dc)
        dh_side = dh_all
        dh_mate = swap(dh_side)
        if layer == 0:
            g_late = send_parts(g_piece_late.reshape(rows, band, fr), "row")
        d_o = total(heads_back(dh_all, wqo), "col").astype(BF)
        if layer == 1:
            d_o, *parts = tie(d_o, *y_parts)
            outputs.append(h + add_all(parts))
        else:
            d_o, qo_grads[1], *g_late = tie(d_o, qo_grads[1], *g_late)
        dp, bias_sum, partial = attention_back(d_o, qkv, wqo, tables, mask)
        partial, dp = tie(partial, dp)
        got = total(partial.reshape(cols, tq, width), "col")
        if aligned:
            mates = (a_mate, o_mate, swap(dp), dh_mate)
            wide_grads = [attention_grads(a_all, o_all, dp, dh_side, mates, mine[None])]
            over = "row"
        else:
            wide_grads = [dot_tn(a_all, dp).astype(BF), dot_tn(to_features(o_all), dh_side).astype(BF)]
            over = ("row", "section")
        got, *wide_grads = tie(got, *wide_grads)
        back, gain1, shift1 = norm_back(got, scaled1, inv1, g1)
        dx = dh + back
        norm_sums[layer] = jnp.stack([gain1, gain2, shift1, shift2])
        bias_sums[layer] = bias_sum.reshape(3, dc)
        grad = dx.astype(BF).astype(F32)
        input_grads[layer] = dx
        if layer == 1:
            g_piece_late, d_grads[1] = g_piece[:dc], g_piece[dc:]
        else:
            g_late = send_parts(from_blocks(place_all(g_late, me_r)), "col")
            dx, g_piece, norm_sums = tie(dx, g_piece, norm_sums)
            g_parts = send_parts(g_piece.reshape(rows, band, fr), "row")
            sums = total(jnp.stack(norm_sums).reshape(2, 4, cols, dc).transpose(2, 0, 1, 3), "col")
            sums, *parts = tie(sums, *g_parts)
            blocks = from_blocks(place_all(parts, me_r))
            blocks, d_wide[0], *wide_grads = tie(blocks, d_wide[0], *wide_grads)
            d_parts = send_parts(d_wide[0], "col")
            g_home = trade(blocks, "col").reshape(dr, fc)
            g_home, sums, input_grads[0], *g_late = tie(g_home, sums, dx, *g_late)
            g_grads = unshare([g_home, place_all(g_late, me_c).reshape(dr, fc)])
            placed_back = to_output(input_grads)
            sums = jnp.concatenate([sums, jnp.stack(bias_sums)], axis=1)
            sums = total(add_all(send_all(sums, "row")), "section")
            g_grads, *d_parts = tie(g_grads, *d_parts)
            d_grads[0] = add_all(d_parts).astype(BF)
        pieces = [lax.psum_scatter(part, over, scatter_dimension=0, tiled=True) for part in wide_grads]
        qo_grads[layer] = jnp.concatenate(pieces, axis=1)

    qo_grads = unshare(qo_grads).reshape(dr, 4 * dc).astype(F32)
    qo_grads = [qo_grads[:, i * dc : (i + 1) * dc] for i in range(4)]
    return (
        placed,
        placed_back,
        jnp.stack(qo_grads[:3], axis=1)[None],
        sums[None, 4:],
        qo_grads[3][None],
        g_grads.astype(F32).transpose(1, 0, 2)[None],
        unshare(d_grads).astype(F32).reshape(dc, fr).T[None],
        sums[None, 0:2],
        sums[None, 2:4],
    )


def solution(mesh):
    return jax.shard_map(
        shards,
        mesh=mesh,
        in_specs=(
            P(None, "row", "col"),
            P(None, "row", "col"),
            P(None, "row"),
            P(None, "row"),
            P("section", "row", None, "col"),
            P("section", None, "col"),
            P("section", "row", "col"),
            P("section", "row", None, "col"),
            P("section", "row", "col"),
            P("section", None, "col"),
            P("section", None, "col"),
        ),
        out_specs=(
            P("section", None, "row", "col"),
            P("section", None, "row", "col"),
            P("section", "row", None, "col"),
            P("section", None, "col"),
            P("section", "row", "col"),
            P("section", "row", None, "col"),
            P("section", "row", "col"),
            P("section", None, "col"),
            P("section", None, "col"),
        ),
        check_vma=False,
    )
```

```python
import jax
import jax.numpy as jnp
from jax import lax
from jax.experimental import pallas as pl
from jax.experimental.pallas import tpu as pltpu
from jax.sharding import PartitionSpec as P

HEAD_DIM = 64
ROT = 16
NORM_EPSILON = 1e-05
ROPE_BASE = 10000.0
SCORE_SCALE = 0.125
MASKED_SCORE = -1e30
BF = jnp.bfloat16
F32 = jnp.float32


def trade(stack, axis):
    return lax.all_to_all(stack, axis, split_axis=0, concat_axis=0)


def gather(value, axis):
    return trade(jnp.broadcast_to(value, (lax.axis_size(axis), *value.shape)), axis)


def total(stack, axis):
    return jnp.sum(trade(stack, axis).astype(F32), axis=0)


def tie(point, *values):
    return lax.optimization_barrier((point, *values))


def dot(a, b):
    return lax.dot_general(a, b, (((1,), (0,)), ((), ())), preferred_element_type=F32)


def dot_nt(a, b):
    return lax.dot_general(a, b, (((1,), (1,)), ((), ())), preferred_element_type=F32)


def dot_tn(a, b):
    return lax.dot_general(a, b, (((0,), (0,)), ((), ())), preferred_element_type=F32)


def norm(values, gain, shift):
    mean_value = jnp.mean(values, axis=-1, keepdims=True)
    centred = values - mean_value
    variance = jnp.mean(centred * centred, axis=-1, keepdims=True)
    inv = lax.rsqrt(variance + NORM_EPSILON)
    scaled = centred * inv
    return (scaled * gain + shift).astype(BF), scaled, inv


def norm_back(grad, scaled, inv, gain):
    e = grad * gain
    mean_e = jnp.mean(e, axis=-1, keepdims=True)
    mean_p = jnp.mean(e * scaled, axis=-1, keepdims=True)
    return inv * (e - mean_e - scaled * mean_p), jnp.sum(grad * scaled, axis=0), jnp.sum(grad, axis=0)


def call(body, grid, in_specs, out_specs, out_shape, scratch, flops, moved, table, *args):
    return pl.pallas_call(
        body,
        grid_spec=pltpu.PrefetchScalarGridSpec(
            num_scalar_prefetch=1,
            grid=(grid,),
            in_specs=in_specs,
            out_specs=out_specs,
            scratch_shapes=scratch,
        ),
        out_shape=out_shape,
        compiler_params=pltpu.CompilerParams(vmem_limit_bytes=56 * 2**20),
        cost_estimate=pl.CostEstimate(flops=int(flops), bytes_accessed=int(moved), transcendentals=0),
    )(table, *args)


def no_table():
    return jnp.zeros((1, 1), jnp.int32)


def turn(x, cosines, sines, sign):
    ahead = pltpu.roll(x, 128 - ROT // 2, 1)
    behind = pltpu.roll(x, ROT // 2, 1)
    return x * cosines + sign * (ahead * sines[0] + behind * sines[1])


def head_lanes(n):
    lanes = lax.broadcasted_iota(jnp.int32, (n, 128), 1)
    return lanes < HEAD_DIM


def softmax_of(q, k, allowed):
    scores = jnp.where(allowed, dot_nt(q, k) * SCORE_SCALE, MASKED_SCORE)
    shifted = jnp.exp(scores - jnp.max(scores, axis=1, keepdims=True))
    return shifted / jnp.sum(shifted, axis=1, keepdims=True)


def whole(*shape):
    return pl.BlockSpec(shape, lambda i, t: (0,) * len(shape))


HBM = pl.BlockSpec(memory_space=pl.ANY)


def fetch(pairs, sems):
    copies = [pltpu.make_async_copy(src, dst, sems.at[i]) for i, (src, dst) in enumerate(pairs)]
    for copy in copies:
        copy.start()
    return copies


def attention(a, w, bias, tables, mask):
    n, width = a.shape
    m = w.shape[1] // 4
    half = width // 2

    def body(_, a_ref, w_ref, bias_ref, tab_ref, mask_ref, qkv_ref, o_ref, held, acc, sems):
        parts = [pl.ds(i * half, half) for i in range(2)]
        copies = fetch([(w_ref.at[part, pl.ds(0, 3 * m)], held.at[part]) for part in parts], sems)
        copies[0].wait()
        acc[...] = dot(a_ref[:, :half], held[:half]) + bias_ref[...]
        copies[1].wait()
        acc[...] += dot(a_ref[:, half:], held[half:])
        low = head_lanes(n)
        zero = jnp.zeros((n, 128), BF)
        allowed = mask_ref[...] > 0
        cosines, sines = tab_ref[0], (tab_ref[1], tab_ref[2])
        for pair in range(m // 128):
            at = pair * 128
            q = turn(acc[:, at : at + 128], cosines, sines, 1.0).astype(BF)
            k = turn(acc[:, m + at : m + at + 128], cosines, sines, 1.0).astype(BF)
            v = acc[:, 2 * m + at : 2 * m + at + 128].astype(BF)
            qkv_ref[:, at : at + 128] = q
            qkv_ref[:, m + at : m + at + 128] = k
            qkv_ref[:, 2 * m + at : 2 * m + at + 128] = v
            p0 = softmax_of(jnp.where(low, q, zero), k, allowed).astype(BF)
            p1 = softmax_of(jnp.where(low, zero, q), k, allowed).astype(BF)
            o_ref[:, at : at + 128] = jnp.where(low, dot(p0, v), dot(p1, v)).astype(BF)

    return call(
        body,
        1,
        [whole(n, width), HBM, whole(1, 3 * m), whole(3, n, 128), whole(n, n)],
        [whole(n, 3 * m), whole(n, m)],
        [jax.ShapeDtypeStruct((n, 3 * m), BF), jax.ShapeDtypeStruct((n, m), BF)],
        [pltpu.VMEM((width, 3 * m), BF), pltpu.VMEM((n, 3 * m), F32), pltpu.SemaphoreType.DMA((2,))],
        2 * n * width * 3 * m,
        2 * width * 3 * m,
        no_table(),
        a,
        w,
        bias,
        tables,
        mask,
    )


def attention_back(d_o, qkv, w, tables, mask):
    n, m = d_o.shape
    width = w.shape[0]
    half = width // 2

    def body(_, d_ref, qkv_ref, w_ref, tab_ref, mask_ref, dp_ref, sum_ref, da_ref, held, sems):
        parts = [pl.ds(i * half, half) for i in range(2)]
        copies = fetch([(w_ref.at[part, pl.ds(0, 3 * m)], held.at[part]) for part in parts], sems)
        low = head_lanes(n)
        zero = jnp.zeros((n, 128), BF)
        allowed = mask_ref[...] > 0
        cosines, sines = tab_ref[0], (tab_ref[1], tab_ref[2])
        for pair in range(m // 128):
            at = pair * 128
            q = qkv_ref[:, at : at + 128]
            k = qkv_ref[:, m + at : m + at + 128]
            v = qkv_ref[:, 2 * m + at : 2 * m + at + 128]
            g = d_ref[:, at : at + 128]
            out = []
            for mine in (True, False):
                pick_q = jnp.where(low, q, zero) if mine else jnp.where(low, zero, q)
                pick_g = jnp.where(low, g, zero) if mine else jnp.where(low, zero, g)
                probs = softmax_of(pick_q, k, allowed)
                d_probs = dot_nt(pick_g, v)
                row = jnp.sum(d_probs * probs, axis=1, keepdims=True)
                ds = (probs * (d_probs - row)).astype(BF)
                out.append((dot(ds, k), dot_tn(ds, q), dot_tn(probs.astype(BF), g)))
            dq, dk, dv = (jnp.where(low, x, y) for x, y in zip(*out))
            dq = turn(dq * SCORE_SCALE, cosines, sines, -1.0)
            dk = turn(dk * SCORE_SCALE, cosines, sines, -1.0)
            for place, part in enumerate((dq, dk, dv)):
                part = part.astype(BF)
                dp_ref[:, place * m + at : place * m + at + 128] = part
                sum_ref[:, place * m + at : place * m + at + 128] = jnp.sum(part.astype(F32), axis=0, keepdims=True)
        for i, copy in enumerate(copies):
            copy.wait()
            da_ref[:, i * half : (i + 1) * half] = dot_nt(dp_ref[...], held[i * half : (i + 1) * half]).astype(BF)

    return call(
        body,
        1,
        [whole(n, m), whole(n, 3 * m), HBM, whole(3, n, 128), whole(n, n)],
        [whole(n, 3 * m), whole(1, 3 * m), whole(n, width)],
        [
            jax.ShapeDtypeStruct((n, 3 * m), BF),
            jax.ShapeDtypeStruct((1, 3 * m), F32),
            jax.ShapeDtypeStruct((n, width), BF),
        ],
        [pltpu.VMEM((width, 3 * m), BF), pltpu.SemaphoreType.DMA((2,))],
        2 * n * width * 3 * m,
        2 * width * 3 * m,
        no_table(),
        d_o,
        qkv,
        w,
        tables,
        mask,
    )


def heads_out(o, w):
    c, n, m = o.shape

    def body(_, o_ref, w_ref, out_ref, held, sems):
        (copy,) = fetch([(w_ref.at[:, pl.ds(3 * m, m)], held)], sems)
        o_wide = jnp.concatenate([o_ref[i] for i in range(c)], axis=1)
        copy.wait()
        out_ref[...] = dot(o_wide, held[...]).astype(BF)

    return call(
        body,
        1,
        [whole(c, n, m), HBM],
        whole(n, m),
        jax.ShapeDtypeStruct((n, m), BF),
        [pltpu.VMEM((c * m, m), BF), pltpu.SemaphoreType.DMA((1,))],
        2 * c * n * m * m,
        2 * c * m * m,
        no_table(),
        o,
        w,
    )


def heads_back(d_h, w):
    n, m = d_h.shape
    c = w.shape[0] // m

    def body(_, d_ref, w_ref, out_ref, held, sems):
        (copy,) = fetch([(w_ref.at[:, pl.ds(3 * m, m)], held)], sems)
        copy.wait()
        back = dot_nt(d_ref[...], held[...]).astype(BF)
        for i in range(c):
            out_ref[i] = back[:, i * m : (i + 1) * m]

    return call(
        body,
        1,
        [whole(n, m), HBM],
        whole(c, n, m),
        jax.ShapeDtypeStruct((c, n, m), BF),
        [pltpu.VMEM((c * m, m), BF), pltpu.SemaphoreType.DMA((1,))],
        2 * c * n * m * m,
        2 * c * m * m,
        no_table(),
        d_h,
        w,
    )


def attention_grads(a, o, dp, d_h, mates, table):
    n, width = a.shape
    m = d_h.shape[1]
    steps = table.shape[1]
    depth = width // (2 * steps)
    per = m // depth

    def body(_, a_ref, o_ref, dp_ref, dh_ref, a2_ref, o2_ref, dp2_ref, dh2_ref, out_ref, dp_all, dh_all):
        @pl.when(pl.program_id(0) == 0)
        def _():
            dp_all[:n], dp_all[n:] = dp_ref[...], dp2_ref[...]
            dh_all[:n], dh_all[n:] = dh_ref[...], dh2_ref[...]

        out_ref[:, : 3 * m] = dot_tn(jnp.concatenate([a_ref[...], a2_ref[...]]), dp_all[...]).astype(BF)
        out_ref[:, 3 * m :] = dot_tn(jnp.concatenate([o_ref[0], o2_ref[0]]), dh_all[...]).astype(BF)

    inputs = [
        pl.BlockSpec((n, depth), lambda i, t: (0, t[0, i])),
        pl.BlockSpec((1, n, depth), lambda i, t: (t[0, i] // per, 0, t[0, i] % per)),
        pl.BlockSpec((n, 3 * m), lambda i, t: (0, 0)),
        pl.BlockSpec((n, m), lambda i, t: (0, 0)),
    ]
    return call(
        body,
        steps,
        inputs * 2,
        pl.BlockSpec((depth, 4 * m), lambda i, t: (i, 0)),
        jax.ShapeDtypeStruct((steps * depth, 4 * m), BF),
        [pltpu.VMEM((2 * n, 3 * m), BF), pltpu.VMEM((2 * n, m), BF)],
        2 * n * width * 4 * m,
        width * 4 * m,
        table,
        a,
        o,
        dp,
        d_h,
        *mates,
    )


def band_list(width, c, band):
    if band % 128:
        return [slice(0, width)]
    rows = width // (c * band)
    return [slice((r * c + q) * band, (r * c + q + 1) * band) for q in range(c) for r in range(rows)]


def mlp_copies(w_ref, down_refs, held, held_down):
    gate_up = [(w_ref.at[i, :, pl.ds(0, 2)], held.at[i]) for i in range(2)]
    sources = down_refs or [w_ref.at[i, :, 2] for i in range(2)]
    return gate_up, [(source, held_down.at[i]) for i, source in enumerate(sources)]


def mlp(b, w, down, halves, band):
    n, width = b.shape
    _, c, _, w2, f = w.shape
    bands = band_list(width, c, band)

    def body(t, b_ref, w_ref, *rest):
        down_refs, (gate_ref, up_ref, m_ref, y_ref, held, held_down, turned, sems) = rest[: len(down)], rest[len(down) :]
        first, later = mlp_copies(w_ref, down_refs, held, held_down)
        copies = fetch(first + later, sems)
        at = 0
        for part in bands:
            size = part.stop - part.start
            turned[:, at : at + size] = b_ref[:, part]
            at += size
        copies[0].wait()
        gate_ref[...] = dot(turned[...], held[0].reshape(width, f))
        copies[1].wait()
        up_ref[...] = dot(turned[...], held[1].reshape(width, f))
        gate = gate_ref[...]
        m_ref[...] = (gate * jax.nn.sigmoid(gate) * up_ref[...]).astype(BF)
        for i in range(2):
            copies[2 + i].wait()
            y = dot_nt(m_ref[...], held_down[i].reshape(c * w2, f)).astype(BF)
            half = t[0, i]
            for k in range(c):
                y_ref[:, pl.ds(pl.multiple_of((2 * k + half) * w2, w2), w2)] = y[:, k * w2 : (k + 1) * w2]

    return call(
        body,
        1,
        [whole(n, width), HBM] + [HBM] * len(down),
        [whole(n, f)] * 3 + [whole(n, width)],
        [jax.ShapeDtypeStruct((n, f), F32)] * 2 + [jax.ShapeDtypeStruct((n, f), BF), jax.ShapeDtypeStruct((n, width), BF)],
        [
            pltpu.VMEM((2, c, 2, w2, f), BF),
            pltpu.VMEM((2, c, w2, f), BF),
            pltpu.VMEM((n, width), BF),
            pltpu.SemaphoreType.DMA((4,)),
        ],
        2 * n * width * 3 * f,
        2 * width * 3 * f,
        halves,
        b,
        w,
        *down,
    )


def mlp_back(dy, gate, up, w, down, halves, band):
    n, width = dy.shape
    _, c, _, w2, f = w.shape
    half = width // 2
    bands = band_list(width, c, band)

    def body(t, dy_ref, gate_ref, up_ref, w_ref, *rest):
        down_refs, (d_ref, db_ref, held, held_down, acc, sems) = rest[: len(down)], rest[len(down) :]
        later, first = mlp_copies(w_ref, down_refs, held, held_down)
        copies = fetch(first + later, sems)
        for i in range(2):
            at = t[0, i]
            ours = [dy_ref[:, pl.ds(pl.multiple_of((2 * k + at) * w2, w2), w2)] for k in range(c)]
            ours = jnp.concatenate(ours, axis=1)
            copies[i].wait()
            part = dot(ours, held_down[i].reshape(c * w2, f))
            acc[...] = part if i == 0 else acc[...] + part
        dm, gate = acc[...], gate_ref[...]
        sig = jax.nn.sigmoid(gate)
        d_ref[0] = (dm * up_ref[...] * sig * (1.0 + gate * (1.0 - sig))).astype(BF)
        d_ref[1] = (dm * gate * sig).astype(BF)
        copies[2].wait()
        copies[3].wait()
        for i in range(2):
            part = slice(i * c // 2, (i + 1) * c // 2)
            back = dot_nt(d_ref[0], held[0, part].reshape(half, f)) + dot_nt(d_ref[1], held[1, part].reshape(half, f))
            back = back.astype(BF)
            if len(bands) == 1:
                db_ref[:, i * half : (i + 1) * half] = back
            for j in range(len(bands) // 2):
                db_ref[:, bands[i * len(bands) // 2 + j]] = back[:, j * band : (j + 1) * band]

    return call(
        body,
        1,
        [whole(n, width), whole(n, f), whole(n, f), HBM] + [HBM] * len(down),
        [whole(2, n, f), whole(n, width)],
        [jax.ShapeDtypeStruct((2, n, f), BF), jax.ShapeDtypeStruct((n, width), BF)],
        [
            pltpu.VMEM((2, c, 2, w2, f), BF),
            pltpu.VMEM((2, c, w2, f), BF),
            pltpu.VMEM((n, f), F32),
            pltpu.SemaphoreType.DMA((4,)),
        ],
        2 * n * width * 3 * f,
        2 * width * 3 * f,
        halves,
        dy,
        gate,
        up,
        w,
        *down,
    )


def mlp_grads(b, d, dy, m, mates, me_s, band, merged):
    n, width = b.shape
    f = m.shape[1]
    c = lax.axis_size("col")
    depth, w2 = width // c, width // c // 2
    sizes = (depth + w2,) if merged else (depth, w2)

    def body(_, b_ref, d_ref, dy_ref, m_ref, b2_ref, d2_ref, dy2_ref, m2_ref, *rest):
        *outs, d_all, m_all = rest

        @pl.when(pl.program_id(0) == 0)
        def _():
            d_all[:n], d_all[n:] = d_ref[0], d2_ref[0]
            m_all[:n], m_all[n:] = m_ref[...], m2_ref[...]

        def rows_of(ref):
            if band % 128:
                return ref[:, pl.ds(pl.multiple_of(pl.program_id(0) * depth, depth), depth)]
            at = [pl.multiple_of((r * c + pl.program_id(0)) * band, band) for r in range(depth // band)]
            return jnp.concatenate([ref[:, pl.ds(i, band)] for i in at], axis=1)

        outs[0][0, :depth] = dot_tn(jnp.concatenate([rows_of(b_ref), rows_of(b2_ref)]), d_all[...]).astype(BF)
        start = depth if merged else 0
        outs[-1][0, start : start + w2] = dot_tn(jnp.concatenate([dy_ref[...], dy2_ref[...]]), m_all[...]).astype(BF)

    inputs = [
        pl.BlockSpec((n, width), lambda i, t: (0, 0)),
        pl.BlockSpec((1, n, f), lambda i, t: (t[0, 0], 0, 0)),
        pl.BlockSpec((n, w2), lambda i, t: (0, i * 2 + t[0, 0])),
        pl.BlockSpec((n, f), lambda i, t: (0, 0)),
    ]
    return call(
        body,
        c,
        inputs * 2,
        [pl.BlockSpec((1, size, f), lambda i, t: (i, 0, 0)) for size in sizes],
        [jax.ShapeDtypeStruct((c, size, f), BF) for size in sizes],
        [pltpu.VMEM((2 * n, f), BF)] * 2,
        2 * n * width * 3 * f,
        width * 3 * f,
        me_s.reshape(1, 1),
        b,
        d,
        dy,
        m,
        *mates,
    )


def swap(value):
    return lax.ppermute(value, "section", [(0, 1), (1, 0)])


def hop(value, axis, step):
    return lax.ppermute(value, axis, [(i, i ^ step) for i in range(lax.axis_size(axis))])


def pick(stack, index):
    return lax.dynamic_index_in_dim(stack, index, 0, keepdims=False)


def place_all(pieces, me):
    out = jnp.zeros((len(pieces), *pieces[0].shape), pieces[0].dtype)
    for k, piece in enumerate(pieces):
        out = lax.dynamic_update_index_in_dim(out, piece, me ^ k, 0)
    return out


def send_all(value, axis):
    return [value] + [hop(value, axis, k) for k in range(1, lax.axis_size(axis))]


def send_parts(stack, axis):
    me = lax.axis_index(axis)
    return [pick(stack, me)] + [hop(pick(stack, me ^ k), axis, k) for k in range(1, stack.shape[0])]


def by_place(pieces, me):
    bit = 1
    while bit < len(pieces):
        flip = (me & bit) != 0
        pieces = [jnp.where(flip, pieces[i ^ bit], pieces[i]) for i in range(len(pieces))]
        bit *= 2
    return pieces


def add_all(parts):
    out = parts[0].astype(F32)
    for part in parts[1:]:
        out = out + part.astype(F32)
    return out


def shards(
    tokens_in, out_grad, segments, positions, w_qkv, b_qkv, w_out, w_gate_up, w_down, norm_gains, norm_biases
):
    rows, cols = lax.axis_size("row"), lax.axis_size("col")
    me_s = lax.axis_index("section")
    first = me_s == 0
    seq, dc = tokens_in.shape[1:]
    width = dc * cols
    tq = seq // cols
    dr = width // rows
    fc, fr = w_gate_up.shape[3], w_down.shape[1]
    w2, v2 = dc // 2, dr // 2
    sub = rows // cols
    band = dr // cols

    def own_first(a, b):
        return jnp.where(first, a, b), jnp.where(first, b, a)

    def to_gate(x):
        if band % 128 == 0:
            return x
        return x.reshape(-1, rows, cols, band).transpose(0, 2, 1, 3).reshape(-1, width)

    def from_gate(x):
        if band % 128 == 0:
            return x
        return x.reshape(-1, cols, rows, band).transpose(0, 2, 1, 3).reshape(-1, width)

    def to_features(stack):
        return stack.transpose(1, 0, 2).reshape(stack.shape[1], width)

    def by_feature(x):
        return x.reshape(x.shape[0], cols, dc).transpose(1, 0, 2)

    me_r, me_c = lax.axis_index("row"), lax.axis_index("col")
    qo = jnp.concatenate([w_qkv[0, :, 0], w_qkv[0, :, 1], w_qkv[0, :, 2], w_out[0]], axis=1)
    qo_half = trade(qo.reshape(2, v2, 4 * dc), "section")
    qo_half, w_gate_up = tie(qo_half, w_gate_up)

    aligned = v2 % 128 == 0
    mine = 2 * jnp.arange(rows, dtype=jnp.int32) + me_s

    def gather_qo(layer):
        return lax.all_gather(qo_half[layer], ("row", "section"), axis=0, tiled=True)

    wqo0 = gather_qo(0)
    g_half = trade(w_gate_up[0].transpose(1, 0, 2), "section")

    def to_blocks(bands):
        return bands.reshape(cols, band, sub, fr).transpose(0, 2, 1, 3).reshape(rows, band, fr)

    def from_blocks(blocks):
        return blocks.reshape(cols, sub, band, fr).transpose(0, 2, 1, 3).reshape(cols, band, fc)

    def gather_mlp(*pieces):
        whole_piece = jnp.concatenate([piece.reshape(-1, fr) for piece in pieces])
        return lax.all_gather(whole_piece, ("section", "col"), axis=0, tiled=True).reshape(2, cols, -1, w2, fr)

    plain = jnp.arange(2, dtype=jnp.int32).reshape(1, 2)
    halves_of = [plain, plain ^ me_s]

    def own_and_other(parts):
        own = place_all(parts, me_c)
        return own, swap(own)

    own_tokens = pick(tokens_in, me_s)
    own_grad = pick(out_grad, me_s)
    both = jnp.stack([own_tokens, own_grad]).reshape(2, cols, tq, dc).transpose(1, 0, 2, 3)
    small = jnp.concatenate([norm_gains[0], norm_biases[0], b_qkv[0]], axis=0)
    g_half, both, small, w_down = tie(g_half, both, small, w_down)
    g_parts = send_parts(g_half[0].reshape(cols, band, fc), "col")
    d_half = trade(w_down[0].T.reshape(2, w2, fr), "section")
    small = gather(small, "section")
    wide = gather(small[:, :4], "col").transpose(1, 2, 0, 3).reshape(2, 4, width).astype(F32)
    bias = small[:, 4:].astype(F32).reshape(2, 1, 3 * dc)

    segment = pick(segments, me_s)
    position = pick(positions, me_s)
    place = jnp.arange(seq, dtype=jnp.int32)
    allowed = (segment[:, None] == segment[None, :]) & (place[None, :] <= place[:, None])
    mask = allowed.astype(F32)
    freq = jnp.power(ROPE_BASE, -2.0 * jnp.arange(ROT // 2, dtype=F32) / ROT)
    angles = position.astype(F32)[:, None] * freq[None, :]
    cosines, sines = jnp.cos(angles), jnp.sin(angles)
    rest = jnp.zeros((seq, HEAD_DIM - ROT), F32)
    none = jnp.zeros_like(sines)
    tables = jnp.stack(
        [
            jnp.concatenate([cosines, cosines, rest + 1.0] * 2, axis=1),
            jnp.concatenate([-sines, none, rest] * 2, axis=1),
            jnp.concatenate([none, sines, rest] * 2, axis=1),
        ]
    )

    tables, mask, wide, *g_parts = tie(tables, mask, wide, *g_parts)
    blocks = to_blocks(place_all(g_parts, me_c))
    blocks, both = tie(blocks, both)
    g_parts = send_parts(blocks, "row")
    late_parts = send_parts(g_half[1].reshape(cols, band, fc), "col")
    both = trade(both, "col").transpose(1, 2, 0, 3).reshape(2, tq, width)
    x = both[0].astype(F32)

    weights, kept, outputs = [], [], []
    for layer in range(2):
        g1, g2, c1, c2 = wide[layer]
        a, scaled1, inv1 = norm(x, g1, c1)
        if layer == 0:
            a, *parts = tie(a, *g_parts, *late_parts)
            wg0 = gather_mlp(place_all(parts[:rows], me_r), d_half[0])
            g_parts = send_parts(to_blocks(place_all(parts[rows:], me_c)), "row")
            down = [(), None]
        a_all = gather(a, "col").reshape(seq, width)
        a_kept = a_all
        if layer == 0:
            wqo = wqo0
        else:
            wqo = wqo1
        a_mate = swap(a_kept)
        qkv, o = attention(a_all, wqo, bias[layer], tables, mask)
        if layer == 1:
            o, grad = tie(o, both[1])
            dy_parts = send_all(grad, "row")
        o_all = gather(o, "col")
        o_kept = o_all
        o_mate = swap(o_kept)
        out = heads_out(o_all, wqo)
        if layer == 0:
            out, *g_parts = tie(out, *g_parts)
            g_piece = place_all(g_parts, me_r)
        if layer == 1:
            out, *parts = tie(out, *dy_parts)
            dy_all = place_all(parts, me_r).reshape(rows * tq, width)
        got = trade(out.reshape(cols, tq, dc), "col")
        h = x + to_features(got).astype(F32)
        b, scaled2, inv2 = norm(h.astype(BF).astype(F32), g2, c2)
        if layer == 0:
            b, qo_half = tie(b, qo_half)
            wqo1 = gather_qo(1)
        b_all = gather(to_gate(b), "row").reshape(rows * tq, width)
        b_mate = swap(b_all)
        wg = wg0 if layer == 0 else wg1
        weights.append((wqo, wg))
        gate, up, m, partial = mlp(b_all, wg, down[layer], halves_of[layer], band)
        m_mate = swap(m)
        if layer == 0:
            gate, g_piece = tie(gate, g_piece)
            wg1 = gather_mlp(g_piece)
        partial = partial.reshape(rows, tq, width)
        if layer == 0:
            y = h + total(partial, "row")
            y, *parts = tie(y, *send_all(d_half[1], "col"))
            down[1] = own_and_other(parts)
            x = y.astype(BF).astype(F32)
            outputs.append(y)
        else:
            y_parts = send_parts(partial, "row")
        kept.append((a_kept, a_mate, scaled1, inv1, qkv, o_kept, o_mate, scaled2, inv2, b_all, b_mate, gate, up, m, m_mate))

    def to_output(pair):
        mine, theirs = own_first(*(part.astype(BF) for part in pair))
        both = jnp.stack(own_first(mine, swap(theirs)))
        parts = send_parts(both.reshape(2, tq, cols, dc).transpose(2, 0, 1, 3), "col")
        return jnp.concatenate(by_place(parts, me_c), axis=1).astype(F32)[None]

    def unshare(pair):
        return trade(jnp.stack(pair), "section")

    input_grads, qo_grads, g_grads, d_grads, norm_sums, bias_sums = ([None] * 2 for _ in range(6))
    grad = grad.astype(F32)
    for layer in (1, 0):
        g1, g2, c1, c2 = wide[layer]
        wqo, wg = weights[layer]
        a_all, a_mate, scaled1, inv1, qkv, o_all, o_mate, scaled2, inv2, b_all, b_mate, gate, up, m, m_mate = kept[layer]
        if layer == 0:
            dy_all = gather(grad.astype(BF), "row").reshape(rows * tq, width)
        dy_mate = swap(dy_all)
        d, partial = mlp_back(dy_all, gate, up, wg, down[layer], halves_of[layer], band)
        partial, d, dy_all, m, b_all = tie(partial, d, dy_all, m, b_all)
        if layer == 0:
            partial, g_piece_late = tie(partial, g_piece_late)
        got = total(partial.reshape(rows, tq, width), "row")
        mates = (b_mate, swap(d), dy_mate, m_mate)
        wide_grad, *d_wide = mlp_grads(b_all, d, dy_all, m, mates, me_s, band, layer == 1)
        got, wide_grad = tie(got, wide_grad)
        g_piece = lax.psum_scatter(wide_grad.reshape(-1, fr), "col", scatter_dimension=0, tiled=True)
        back, gain2, shift2 = norm_back(from_gate(got), scaled2, inv2, g2)
        dh = grad + back
        dh_all = trade(by_feature(dh.astype(BF)), "col").reshape(seq, dc)
        dh_side = dh_all
        dh_mate = swap(dh_side)
        if layer == 0:
            g_late = send_parts(g_piece_late.reshape(rows, band, fr), "row")
        d_o = total(heads_back(dh_all, wqo), "col").astype(BF)
        if layer == 1:
            d_o, *parts = tie(d_o, *y_parts)
            outputs.append(h + add_all(parts))
        else:
            d_o, qo_grads[1], placed, *g_late = tie(d_o, qo_grads[1], to_output(outputs), *g_late)
        dp, bias_sum, partial = attention_back(d_o, qkv, wqo, tables, mask)
        partial, dp = tie(partial, dp)
        got = total(partial.reshape(cols, tq, width), "col")
        if aligned:
            mates = (a_mate, o_mate, swap(dp), dh_mate)
            wide_grads = [attention_grads(a_all, o_all, dp, dh_side, mates, mine[None])]
            over = "row"
        else:
            wide_grads = [dot_tn(a_all, dp).astype(BF), dot_tn(to_features(o_all), dh_side).astype(BF)]
            over = ("row", "section")
        got, *wide_grads = tie(got, *wide_grads)
        back, gain1, shift1 = norm_back(got, scaled1, inv1, g1)
        dx = dh + back
        norm_sums[layer] = jnp.stack([gain1, gain2, shift1, shift2])
        bias_sums[layer] = bias_sum.reshape(3, dc)
        grad = dx.astype(BF).astype(F32)
        input_grads[layer] = dx
        if layer == 1:
            g_piece_late, d_grads[1] = g_piece[:dc], g_piece[dc:]
        else:
            g_late = send_parts(from_blocks(place_all(g_late, me_r)), "col")
            dx, g_piece, norm_sums = tie(dx, g_piece, norm_sums)
            g_parts = send_parts(g_piece.reshape(rows, band, fr), "row")
            sums = total(jnp.stack(norm_sums).reshape(2, 4, cols, dc).transpose(2, 0, 1, 3), "col")
            sums, *parts = tie(sums, *g_parts, *g_late)
            g_late = parts[rows:]
            blocks = from_blocks(place_all(parts[:rows], me_r))
            blocks, d_wide[0], *wide_grads = tie(blocks, d_wide[0], *wide_grads)
            d_parts = send_parts(d_wide[0], "col")
            g_home = trade(blocks, "col").reshape(dr, fc)
            g_home, sums, input_grads[0] = tie(g_home, sums, dx)
            g_grads = unshare([g_home, place_all(g_late, me_c).reshape(dr, fc)])
            placed_back = to_output(input_grads)
            sums = jnp.concatenate([sums, jnp.stack(bias_sums)], axis=1)
            sums = total(add_all(send_all(sums, "row")), "section")
            g_grads, *d_parts = tie(g_grads, *d_parts)
            d_grads[0] = add_all(d_parts).astype(BF)
        pieces = [lax.psum_scatter(part, over, scatter_dimension=0, tiled=True) for part in wide_grads]
        qo_grads[layer] = jnp.concatenate(pieces, axis=1)

    qo_grads = unshare(qo_grads).reshape(dr, 4 * dc).astype(F32)
    qo_grads = [qo_grads[:, i * dc : (i + 1) * dc] for i in range(4)]
    return (
        placed,
        placed_back,
        jnp.stack(qo_grads[:3], axis=1)[None],
        sums[None, 4:],
        qo_grads[3][None],
        g_grads.astype(F32).transpose(1, 0, 2)[None],
        unshare(d_grads).astype(F32).reshape(dc, fr).T[None],
        sums[None, 0:2],
        sums[None, 2:4],
    )


def solution(mesh):
    return jax.shard_map(
        shards,
        mesh=mesh,
        in_specs=(
            P(None, "row", "col"),
            P(None, "row", "col"),
            P(None, "row"),
            P(None, "row"),
            P("section", "row", None, "col"),
            P("section", None, "col"),
            P("section", "row", "col"),
            P("section", "row", None, "col"),
            P("section", "row", "col"),
            P("section", None, "col"),
            P("section", None, "col"),
        ),
        out_specs=(
            P("section", None, "row", "col"),
            P("section", None, "row", "col"),
            P("section", "row", None, "col"),
            P("section", None, "col"),
            P("section", "row", "col"),
            P("section", "row", None, "col"),
            P("section", "row", "col"),
            P("section", None, "col"),
            P("section", None, "col"),
        ),
        check_vma=False,
    )
```

```python
import jax
import jax.numpy as jnp
from jax import lax
from jax.experimental import pallas as pl
from jax.experimental.pallas import tpu as pltpu
from jax.sharding import PartitionSpec as P

HEAD_DIM = 64
ROT = 16
NORM_EPSILON = 1e-05
ROPE_BASE = 10000.0
SCORE_SCALE = 0.125
MASKED_SCORE = -1e30
BF = jnp.bfloat16
F32 = jnp.float32


def trade(stack, axis):
    return lax.all_to_all(stack, axis, split_axis=0, concat_axis=0)


def gather(value, axis):
    return trade(jnp.broadcast_to(value, (lax.axis_size(axis), *value.shape)), axis)


def total(stack, axis):
    return jnp.sum(trade(stack, axis).astype(F32), axis=0)


def tie(point, *values):
    return lax.optimization_barrier((point, *values))


def dot(a, b):
    return lax.dot_general(a, b, (((1,), (0,)), ((), ())), preferred_element_type=F32)


def dot_nt(a, b):
    return lax.dot_general(a, b, (((1,), (1,)), ((), ())), preferred_element_type=F32)


def dot_tn(a, b):
    return lax.dot_general(a, b, (((0,), (0,)), ((), ())), preferred_element_type=F32)


def norm(values, gain, shift):
    mean_value = jnp.mean(values, axis=-1, keepdims=True)
    centred = values - mean_value
    variance = jnp.mean(centred * centred, axis=-1, keepdims=True)
    inv = lax.rsqrt(variance + NORM_EPSILON)
    scaled = centred * inv
    return (scaled * gain + shift).astype(BF), scaled, inv


def norm_back(grad, scaled, inv, gain):
    e = grad * gain
    mean_e = jnp.mean(e, axis=-1, keepdims=True)
    mean_p = jnp.mean(e * scaled, axis=-1, keepdims=True)
    return inv * (e - mean_e - scaled * mean_p), jnp.sum(grad * scaled, axis=0), jnp.sum(grad, axis=0)


def call(body, grid, in_specs, out_specs, out_shape, scratch, flops, moved, table, *args):
    return pl.pallas_call(
        body,
        grid_spec=pltpu.PrefetchScalarGridSpec(
            num_scalar_prefetch=1,
            grid=(grid,),
            in_specs=in_specs,
            out_specs=out_specs,
            scratch_shapes=scratch,
        ),
        out_shape=out_shape,
        compiler_params=pltpu.CompilerParams(vmem_limit_bytes=56 * 2**20),
        cost_estimate=pl.CostEstimate(flops=int(flops), bytes_accessed=int(moved), transcendentals=0),
    )(table, *args)


def no_table():
    return jnp.zeros((1, 1), jnp.int32)


def turn(x, cosines, sines, sign):
    ahead = pltpu.roll(x, 128 - ROT // 2, 1)
    behind = pltpu.roll(x, ROT // 2, 1)
    return x * cosines + sign * (ahead * sines[0] + behind * sines[1])


def head_lanes(n):
    lanes = lax.broadcasted_iota(jnp.int32, (n, 128), 1)
    return lanes < HEAD_DIM


def softmax_of(q, k, allowed):
    scores = jnp.where(allowed, dot_nt(q, k) * SCORE_SCALE, MASKED_SCORE)
    shifted = jnp.exp(scores - jnp.max(scores, axis=1, keepdims=True))
    return shifted / jnp.sum(shifted, axis=1, keepdims=True)


def whole(*shape):
    return pl.BlockSpec(shape, lambda i, t: (0,) * len(shape))


HBM = pl.BlockSpec(memory_space=pl.ANY)


def fetch(pairs, sems):
    copies = [pltpu.make_async_copy(src, dst, sems.at[i]) for i, (src, dst) in enumerate(pairs)]
    for copy in copies:
        copy.start()
    return copies


def attention(a, w, bias, tables, mask):
    n, width = a.shape
    m = w.shape[1] // 4
    half = width // 2

    def body(_, a_ref, w_ref, bias_ref, tab_ref, mask_ref, qkv_ref, o_ref, held, acc, sems):
        parts = [pl.ds(i * half, half) for i in range(2)]
        copies = fetch([(w_ref.at[part, pl.ds(0, 3 * m)], held.at[part]) for part in parts], sems)
        copies[0].wait()
        acc[...] = dot(a_ref[:, :half], held[:half]) + bias_ref[...]
        copies[1].wait()
        acc[...] += dot(a_ref[:, half:], held[half:])
        low = head_lanes(n)
        zero = jnp.zeros((n, 128), BF)
        allowed = mask_ref[...] > 0
        cosines, sines = tab_ref[0], (tab_ref[1], tab_ref[2])
        for pair in range(m // 128):
            at = pair * 128
            q = turn(acc[:, at : at + 128], cosines, sines, 1.0).astype(BF)
            k = turn(acc[:, m + at : m + at + 128], cosines, sines, 1.0).astype(BF)
            v = acc[:, 2 * m + at : 2 * m + at + 128].astype(BF)
            qkv_ref[:, at : at + 128] = q
            qkv_ref[:, m + at : m + at + 128] = k
            qkv_ref[:, 2 * m + at : 2 * m + at + 128] = v
            p0 = softmax_of(jnp.where(low, q, zero), k, allowed).astype(BF)
            p1 = softmax_of(jnp.where(low, zero, q), k, allowed).astype(BF)
            o_ref[:, at : at + 128] = jnp.where(low, dot(p0, v), dot(p1, v)).astype(BF)

    return call(
        body,
        1,
        [whole(n, width), HBM, whole(1, 3 * m), whole(3, n, 128), whole(n, n)],
        [whole(n, 3 * m), whole(n, m)],
        [jax.ShapeDtypeStruct((n, 3 * m), BF), jax.ShapeDtypeStruct((n, m), BF)],
        [pltpu.VMEM((width, 3 * m), BF), pltpu.VMEM((n, 3 * m), F32), pltpu.SemaphoreType.DMA((2,))],
        2 * n * width * 3 * m,
        2 * width * 3 * m,
        no_table(),
        a,
        w,
        bias,
        tables,
        mask,
    )


def attention_back(d_o, qkv, w, tables, mask):
    n, m = d_o.shape
    width = w.shape[0]
    half = width // 2

    def body(_, d_ref, qkv_ref, w_ref, tab_ref, mask_ref, dp_ref, sum_ref, da_ref, held, sems):
        parts = [pl.ds(i * half, half) for i in range(2)]
        copies = fetch([(w_ref.at[part, pl.ds(0, 3 * m)], held.at[part]) for part in parts], sems)
        low = head_lanes(n)
        zero = jnp.zeros((n, 128), BF)
        allowed = mask_ref[...] > 0
        cosines, sines = tab_ref[0], (tab_ref[1], tab_ref[2])
        for pair in range(m // 128):
            at = pair * 128
            q = qkv_ref[:, at : at + 128]
            k = qkv_ref[:, m + at : m + at + 128]
            v = qkv_ref[:, 2 * m + at : 2 * m + at + 128]
            g = d_ref[:, at : at + 128]
            out = []
            for mine in (True, False):
                pick_q = jnp.where(low, q, zero) if mine else jnp.where(low, zero, q)
                pick_g = jnp.where(low, g, zero) if mine else jnp.where(low, zero, g)
                probs = softmax_of(pick_q, k, allowed)
                d_probs = dot_nt(pick_g, v)
                row = jnp.sum(d_probs * probs, axis=1, keepdims=True)
                ds = (probs * (d_probs - row)).astype(BF)
                out.append((dot(ds, k), dot_tn(ds, q), dot_tn(probs.astype(BF), g)))
            dq, dk, dv = (jnp.where(low, x, y) for x, y in zip(*out))
            dq = turn(dq * SCORE_SCALE, cosines, sines, -1.0)
            dk = turn(dk * SCORE_SCALE, cosines, sines, -1.0)
            for place, part in enumerate((dq, dk, dv)):
                part = part.astype(BF)
                dp_ref[:, place * m + at : place * m + at + 128] = part
                sum_ref[:, place * m + at : place * m + at + 128] = jnp.sum(part.astype(F32), axis=0, keepdims=True)
        for i, copy in enumerate(copies):
            copy.wait()
            da_ref[:, i * half : (i + 1) * half] = dot_nt(dp_ref[...], held[i * half : (i + 1) * half]).astype(BF)

    return call(
        body,
        1,
        [whole(n, m), whole(n, 3 * m), HBM, whole(3, n, 128), whole(n, n)],
        [whole(n, 3 * m), whole(1, 3 * m), whole(n, width)],
        [
            jax.ShapeDtypeStruct((n, 3 * m), BF),
            jax.ShapeDtypeStruct((1, 3 * m), F32),
            jax.ShapeDtypeStruct((n, width), BF),
        ],
        [pltpu.VMEM((width, 3 * m), BF), pltpu.SemaphoreType.DMA((2,))],
        2 * n * width * 3 * m,
        2 * width * 3 * m,
        no_table(),
        d_o,
        qkv,
        w,
        tables,
        mask,
    )


def heads_out(o, w):
    c, n, m = o.shape

    def body(_, o_ref, w_ref, out_ref, held, sems):
        (copy,) = fetch([(w_ref.at[:, pl.ds(3 * m, m)], held)], sems)
        o_wide = jnp.concatenate([o_ref[i] for i in range(c)], axis=1)
        copy.wait()
        out_ref[...] = dot(o_wide, held[...]).astype(BF)

    return call(
        body,
        1,
        [whole(c, n, m), HBM],
        whole(n, m),
        jax.ShapeDtypeStruct((n, m), BF),
        [pltpu.VMEM((c * m, m), BF), pltpu.SemaphoreType.DMA((1,))],
        2 * c * n * m * m,
        2 * c * m * m,
        no_table(),
        o,
        w,
    )


def heads_back(d_h, w):
    n, m = d_h.shape
    c = w.shape[0] // m

    def body(_, d_ref, w_ref, out_ref, held, sems):
        (copy,) = fetch([(w_ref.at[:, pl.ds(3 * m, m)], held)], sems)
        copy.wait()
        back = dot_nt(d_ref[...], held[...]).astype(BF)
        for i in range(c):
            out_ref[i] = back[:, i * m : (i + 1) * m]

    return call(
        body,
        1,
        [whole(n, m), HBM],
        whole(c, n, m),
        jax.ShapeDtypeStruct((c, n, m), BF),
        [pltpu.VMEM((c * m, m), BF), pltpu.SemaphoreType.DMA((1,))],
        2 * c * n * m * m,
        2 * c * m * m,
        no_table(),
        d_h,
        w,
    )


def attention_grads(a, o, dp, d_h, mates, table):
    n, width = a.shape
    m = d_h.shape[1]
    steps = table.shape[1]
    depth = width // (2 * steps)
    per = m // depth

    def body(_, a_ref, o_ref, dp_ref, dh_ref, a2_ref, o2_ref, dp2_ref, dh2_ref, out_ref, dp_all, dh_all):
        @pl.when(pl.program_id(0) == 0)
        def _():
            dp_all[:n], dp_all[n:] = dp_ref[...], dp2_ref[...]
            dh_all[:n], dh_all[n:] = dh_ref[...], dh2_ref[...]

        out_ref[:, : 3 * m] = dot_tn(jnp.concatenate([a_ref[...], a2_ref[...]]), dp_all[...]).astype(BF)
        out_ref[:, 3 * m :] = dot_tn(jnp.concatenate([o_ref[0], o2_ref[0]]), dh_all[...]).astype(BF)

    inputs = [
        pl.BlockSpec((n, depth), lambda i, t: (0, t[0, i])),
        pl.BlockSpec((1, n, depth), lambda i, t: (t[0, i] // per, 0, t[0, i] % per)),
        pl.BlockSpec((n, 3 * m), lambda i, t: (0, 0)),
        pl.BlockSpec((n, m), lambda i, t: (0, 0)),
    ]
    return call(
        body,
        steps,
        inputs * 2,
        pl.BlockSpec((depth, 4 * m), lambda i, t: (i, 0)),
        jax.ShapeDtypeStruct((steps * depth, 4 * m), BF),
        [pltpu.VMEM((2 * n, 3 * m), BF), pltpu.VMEM((2 * n, m), BF)],
        2 * n * width * 4 * m,
        width * 4 * m,
        table,
        a,
        o,
        dp,
        d_h,
        *mates,
    )


def band_list(width, c, band):
    if band % 128:
        return [slice(0, width)]
    rows = width // (c * band)
    return [slice((r * c + q) * band, (r * c + q + 1) * band) for q in range(c) for r in range(rows)]


def mlp_copies(w_ref, down_refs, held, held_down):
    gate_up = [(w_ref.at[i, :, pl.ds(0, 2)], held.at[i]) for i in range(2)]
    sources = down_refs or [w_ref.at[i, :, 2] for i in range(2)]
    return gate_up, [(source, held_down.at[i]) for i, source in enumerate(sources)]


def mlp(b, w, down, halves, band):
    n, width = b.shape
    _, c, _, w2, f = w.shape
    bands = band_list(width, c, band)

    def body(t, b_ref, w_ref, *rest):
        down_refs, (gate_ref, up_ref, m_ref, y_ref, held, held_down, turned, sems) = rest[: len(down)], rest[len(down) :]
        first, later = mlp_copies(w_ref, down_refs, held, held_down)
        copies = fetch(first + later, sems)
        at = 0
        for part in bands:
            size = part.stop - part.start
            turned[:, at : at + size] = b_ref[:, part]
            at += size
        copies[0].wait()
        gate_ref[...] = dot(turned[...], held[0].reshape(width, f))
        copies[1].wait()
        up_ref[...] = dot(turned[...], held[1].reshape(width, f))
        gate = gate_ref[...]
        m_ref[...] = (gate * jax.nn.sigmoid(gate) * up_ref[...]).astype(BF)
        for i in range(2):
            copies[2 + i].wait()
            y = dot_nt(m_ref[...], held_down[i].reshape(c * w2, f)).astype(BF)
            half = t[0, i]
            for k in range(c):
                y_ref[:, pl.ds(pl.multiple_of((2 * k + half) * w2, w2), w2)] = y[:, k * w2 : (k + 1) * w2]

    return call(
        body,
        1,
        [whole(n, width), HBM] + [HBM] * len(down),
        [whole(n, f)] * 3 + [whole(n, width)],
        [jax.ShapeDtypeStruct((n, f), F32)] * 2 + [jax.ShapeDtypeStruct((n, f), BF), jax.ShapeDtypeStruct((n, width), BF)],
        [
            pltpu.VMEM((2, c, 2, w2, f), BF),
            pltpu.VMEM((2, c, w2, f), BF),
            pltpu.VMEM((n, width), BF),
            pltpu.SemaphoreType.DMA((4,)),
        ],
        2 * n * width * 3 * f,
        2 * width * 3 * f,
        halves,
        b,
        w,
        *down,
    )


def mlp_back(dy, gate, up, w, down, halves, band):
    n, width = dy.shape
    _, c, _, w2, f = w.shape
    half = width // 2
    bands = band_list(width, c, band)

    def body(t, dy_ref, gate_ref, up_ref, w_ref, *rest):
        down_refs, (d_ref, db_ref, held, held_down, acc, sems) = rest[: len(down)], rest[len(down) :]
        later, first = mlp_copies(w_ref, down_refs, held, held_down)
        copies = fetch(first + later, sems)
        for i in range(2):
            at = t[0, i]
            ours = [dy_ref[:, pl.ds(pl.multiple_of((2 * k + at) * w2, w2), w2)] for k in range(c)]
            ours = jnp.concatenate(ours, axis=1)
            copies[i].wait()
            part = dot(ours, held_down[i].reshape(c * w2, f))
            acc[...] = part if i == 0 else acc[...] + part
        dm, gate = acc[...], gate_ref[...]
        sig = jax.nn.sigmoid(gate)
        d_ref[0] = (dm * up_ref[...] * sig * (1.0 + gate * (1.0 - sig))).astype(BF)
        d_ref[1] = (dm * gate * sig).astype(BF)
        copies[2].wait()
        copies[3].wait()
        for i in range(2):
            part = slice(i * c // 2, (i + 1) * c // 2)
            back = dot_nt(d_ref[0], held[0, part].reshape(half, f)) + dot_nt(d_ref[1], held[1, part].reshape(half, f))
            back = back.astype(BF)
            if len(bands) == 1:
                db_ref[:, i * half : (i + 1) * half] = back
            for j in range(len(bands) // 2):
                db_ref[:, bands[i * len(bands) // 2 + j]] = back[:, j * band : (j + 1) * band]

    return call(
        body,
        1,
        [whole(n, width), whole(n, f), whole(n, f), HBM] + [HBM] * len(down),
        [whole(2, n, f), whole(n, width)],
        [jax.ShapeDtypeStruct((2, n, f), BF), jax.ShapeDtypeStruct((n, width), BF)],
        [
            pltpu.VMEM((2, c, 2, w2, f), BF),
            pltpu.VMEM((2, c, w2, f), BF),
            pltpu.VMEM((n, f), F32),
            pltpu.SemaphoreType.DMA((4,)),
        ],
        2 * n * width * 3 * f,
        2 * width * 3 * f,
        halves,
        dy,
        gate,
        up,
        w,
        *down,
    )


def mlp_grads(b, d, dy, m, mates, me_s, band, merged):
    n, width = b.shape
    f = m.shape[1]
    c = lax.axis_size("col")
    depth, w2 = width // c, width // c // 2
    sizes = (depth + w2,) if merged else (depth, w2)

    def body(_, b_ref, d_ref, dy_ref, m_ref, b2_ref, d2_ref, dy2_ref, m2_ref, *rest):
        *outs, d_all, m_all = rest

        @pl.when(pl.program_id(0) == 0)
        def _():
            d_all[:n], d_all[n:] = d_ref[0], d2_ref[0]
            m_all[:n], m_all[n:] = m_ref[...], m2_ref[...]

        def rows_of(ref):
            if band % 128:
                return ref[:, pl.ds(pl.multiple_of(pl.program_id(0) * depth, depth), depth)]
            at = [pl.multiple_of((r * c + pl.program_id(0)) * band, band) for r in range(depth // band)]
            return jnp.concatenate([ref[:, pl.ds(i, band)] for i in at], axis=1)

        outs[0][0, :depth] = dot_tn(jnp.concatenate([rows_of(b_ref), rows_of(b2_ref)]), d_all[...]).astype(BF)
        start = depth if merged else 0
        outs[-1][0, start : start + w2] = dot_tn(jnp.concatenate([dy_ref[...], dy2_ref[...]]), m_all[...]).astype(BF)

    inputs = [
        pl.BlockSpec((n, width), lambda i, t: (0, 0)),
        pl.BlockSpec((1, n, f), lambda i, t: (t[0, 0], 0, 0)),
        pl.BlockSpec((n, w2), lambda i, t: (0, i * 2 + t[0, 0])),
        pl.BlockSpec((n, f), lambda i, t: (0, 0)),
    ]
    return call(
        body,
        c,
        inputs * 2,
        [pl.BlockSpec((1, size, f), lambda i, t: (i, 0, 0)) for size in sizes],
        [jax.ShapeDtypeStruct((c, size, f), BF) for size in sizes],
        [pltpu.VMEM((2 * n, f), BF)] * 2,
        2 * n * width * 3 * f,
        width * 3 * f,
        me_s.reshape(1, 1),
        b,
        d,
        dy,
        m,
        *mates,
    )


def interleave(x):
    _, n, f = x.shape
    rows = 64 if n % 64 == 0 else n

    def body(_, x_ref, out_ref):
        for i in range(2):
            out_ref[:, i, :] = x_ref[i].astype(F32)

    return call(
        body,
        n // rows,
        [pl.BlockSpec((2, rows, f), lambda i, t: (0, i, 0))],
        pl.BlockSpec((rows, 2, f), lambda i, t: (i, 0, 0)),
        jax.ShapeDtypeStruct((n, 2, f), F32),
        [],
        2 * n * f,
        12 * n * f,
        no_table(),
        x,
    )


def swap(value):
    return lax.ppermute(value, "section", [(0, 1), (1, 0)])


def hop(value, axis, step):
    return lax.ppermute(value, axis, [(i, i ^ step) for i in range(lax.axis_size(axis))])


def pick(stack, index):
    return lax.dynamic_index_in_dim(stack, index, 0, keepdims=False)


def place_all(pieces, me):
    out = jnp.zeros((len(pieces), *pieces[0].shape), pieces[0].dtype)
    for k, piece in enumerate(pieces):
        out = lax.dynamic_update_index_in_dim(out, piece, me ^ k, 0)
    return out


def send_all(value, axis):
    return [value] + [hop(value, axis, k) for k in range(1, lax.axis_size(axis))]


def send_parts(stack, axis):
    me = lax.axis_index(axis)
    return [pick(stack, me)] + [hop(pick(stack, me ^ k), axis, k) for k in range(1, stack.shape[0])]


def by_place(pieces, me):
    bit = 1
    while bit < len(pieces):
        flip = (me & bit) != 0
        pieces = [jnp.where(flip, pieces[i ^ bit], pieces[i]) for i in range(len(pieces))]
        bit *= 2
    return pieces


def add_all(parts):
    out = parts[0].astype(F32)
    for part in parts[1:]:
        out = out + part.astype(F32)
    return out


def shards(
    tokens_in, out_grad, segments, positions, w_qkv, b_qkv, w_out, w_gate_up, w_down, norm_gains, norm_biases
):
    rows, cols = lax.axis_size("row"), lax.axis_size("col")
    me_s = lax.axis_index("section")
    first = me_s == 0
    seq, dc = tokens_in.shape[1:]
    width = dc * cols
    tq = seq // cols
    dr = width // rows
    fc, fr = w_gate_up.shape[3], w_down.shape[1]
    w2, v2 = dc // 2, dr // 2
    sub = rows // cols
    band = dr // cols

    def own_first(a, b):
        return jnp.where(first, a, b), jnp.where(first, b, a)

    def to_gate(x):
        if band % 128 == 0:
            return x
        return x.reshape(-1, rows, cols, band).transpose(0, 2, 1, 3).reshape(-1, width)

    def from_gate(x):
        if band % 128 == 0:
            return x
        return x.reshape(-1, cols, rows, band).transpose(0, 2, 1, 3).reshape(-1, width)

    def to_features(stack):
        return stack.transpose(1, 0, 2).reshape(stack.shape[1], width)

    def by_feature(x):
        return x.reshape(x.shape[0], cols, dc).transpose(1, 0, 2)

    me_r, me_c = lax.axis_index("row"), lax.axis_index("col")
    qo = jnp.concatenate([w_qkv[0, :, 0], w_qkv[0, :, 1], w_qkv[0, :, 2], w_out[0]], axis=1)
    qo_half = trade(qo.reshape(2, v2, 4 * dc), "section")
    qo_half, w_gate_up = tie(qo_half, w_gate_up)

    aligned = v2 % 128 == 0
    mine = 2 * jnp.arange(rows, dtype=jnp.int32) + me_s

    def gather_qo(layer):
        return lax.all_gather(qo_half[layer], ("row", "section"), axis=0, tiled=True)

    wqo0 = gather_qo(0)
    g_half = trade(w_gate_up[0].transpose(1, 0, 2), "section")

    def to_blocks(bands):
        return bands.reshape(cols, band, sub, fr).transpose(0, 2, 1, 3).reshape(rows, band, fr)

    def from_blocks(blocks):
        return blocks.reshape(cols, sub, band, fr).transpose(0, 2, 1, 3).reshape(cols, band, fc)

    def gather_mlp(*pieces):
        whole_piece = jnp.concatenate([piece.reshape(-1, fr) for piece in pieces])
        return lax.all_gather(whole_piece, ("section", "col"), axis=0, tiled=True).reshape(2, cols, -1, w2, fr)

    plain = jnp.arange(2, dtype=jnp.int32).reshape(1, 2)
    halves_of = [plain, plain ^ me_s]

    def own_and_other(parts):
        own = place_all(parts, me_c)
        return own, swap(own)

    own_tokens = pick(tokens_in, me_s)
    own_grad = pick(out_grad, me_s)
    both = jnp.stack([own_tokens, own_grad]).reshape(2, cols, tq, dc).transpose(1, 0, 2, 3)
    small = jnp.concatenate([norm_gains[0], norm_biases[0], b_qkv[0]], axis=0)
    g_half, both, small, w_down = tie(g_half, both, small, w_down)
    g_parts = send_parts(g_half[0].reshape(cols, band, fc), "col")
    d_half = trade(w_down[0].T.reshape(2, w2, fr), "section")
    small = gather(small, "section")
    wide = gather(small[:, :4], "col").transpose(1, 2, 0, 3).reshape(2, 4, width).astype(F32)
    bias = small[:, 4:].astype(F32).reshape(2, 1, 3 * dc)

    segment = pick(segments, me_s)
    position = pick(positions, me_s)
    place = jnp.arange(seq, dtype=jnp.int32)
    allowed = (segment[:, None] == segment[None, :]) & (place[None, :] <= place[:, None])
    mask = allowed.astype(F32)
    freq = jnp.power(ROPE_BASE, -2.0 * jnp.arange(ROT // 2, dtype=F32) / ROT)
    angles = position.astype(F32)[:, None] * freq[None, :]
    cosines, sines = jnp.cos(angles), jnp.sin(angles)
    rest = jnp.zeros((seq, HEAD_DIM - ROT), F32)
    none = jnp.zeros_like(sines)
    tables = jnp.stack(
        [
            jnp.concatenate([cosines, cosines, rest + 1.0] * 2, axis=1),
            jnp.concatenate([-sines, none, rest] * 2, axis=1),
            jnp.concatenate([none, sines, rest] * 2, axis=1),
        ]
    )

    tables, mask, wide, *g_parts = tie(tables, mask, wide, *g_parts)
    blocks = to_blocks(place_all(g_parts, me_c))
    blocks, both = tie(blocks, both)
    g_parts = send_parts(blocks, "row")
    late_parts = send_parts(g_half[1].reshape(cols, band, fc), "col")
    both = trade(both, "col").transpose(1, 2, 0, 3).reshape(2, tq, width)
    x = both[0].astype(F32)

    weights, kept, outputs = [], [], []
    for layer in range(2):
        g1, g2, c1, c2 = wide[layer]
        a, scaled1, inv1 = norm(x, g1, c1)
        if layer == 0:
            a, *parts = tie(a, *g_parts, *late_parts)
            wg0 = gather_mlp(place_all(parts[:rows], me_r), d_half[0])
            g_parts = send_parts(to_blocks(place_all(parts[rows:], me_c)), "row")
            down = [(), None]
        a_all = gather(a, "col").reshape(seq, width)
        a_kept = a_all
        if layer == 0:
            wqo = wqo0
        else:
            wqo = wqo1
        a_mate = swap(a_kept)
        qkv, o = attention(a_all, wqo, bias[layer], tables, mask)
        if layer == 1:
            o, grad = tie(o, both[1])
            dy_parts = send_all(grad, "row")
        o_all = gather(o, "col")
        o_kept = o_all
        o_mate = swap(o_kept)
        out = heads_out(o_all, wqo)
        if layer == 0:
            out, *g_parts = tie(out, *g_parts)
            g_piece = place_all(g_parts, me_r)
        if layer == 1:
            out, *parts = tie(out, *dy_parts)
            dy_all = place_all(parts, me_r).reshape(rows * tq, width)
        got = trade(out.reshape(cols, tq, dc), "col")
        h = x + to_features(got).astype(F32)
        b, scaled2, inv2 = norm(h.astype(BF).astype(F32), g2, c2)
        if layer == 0:
            b, qo_half = tie(b, qo_half)
            wqo1 = gather_qo(1)
        b_all = gather(to_gate(b), "row").reshape(rows * tq, width)
        b_mate = swap(b_all)
        wg = wg0 if layer == 0 else wg1
        weights.append((wqo, wg))
        gate, up, m, partial = mlp(b_all, wg, down[layer], halves_of[layer], band)
        m_mate = swap(m)
        if layer == 0:
            gate, g_piece = tie(gate, g_piece)
            wg1 = gather_mlp(g_piece)
        partial = partial.reshape(rows, tq, width)
        if layer == 0:
            y = h + total(partial, "row")
            y, *parts = tie(y, *send_all(d_half[1], "col"))
            down[1] = own_and_other(parts)
            x = y.astype(BF).astype(F32)
            outputs.append(y)
        else:
            y_parts = send_parts(partial, "row")
        kept.append((a_kept, a_mate, scaled1, inv1, qkv, o_kept, o_mate, scaled2, inv2, b_all, b_mate, gate, up, m, m_mate))

    def to_output(pair):
        mine, theirs = own_first(*(part.astype(BF) for part in pair))
        both = jnp.stack(own_first(mine, swap(theirs)))
        parts = send_parts(both.reshape(2, tq, cols, dc).transpose(2, 0, 1, 3), "col")
        return jnp.concatenate(by_place(parts, me_c), axis=1).astype(F32)[None]

    def unshare(pair):
        return trade(jnp.stack(pair), "section")

    input_grads, qo_grads, g_grads, d_grads, norm_sums, bias_sums = ([None] * 2 for _ in range(6))
    grad = grad.astype(F32)
    for layer in (1, 0):
        g1, g2, c1, c2 = wide[layer]
        wqo, wg = weights[layer]
        a_all, a_mate, scaled1, inv1, qkv, o_all, o_mate, scaled2, inv2, b_all, b_mate, gate, up, m, m_mate = kept[layer]
        if layer == 0:
            dy_all = gather(grad.astype(BF), "row").reshape(rows * tq, width)
        dy_mate = swap(dy_all)
        d, partial = mlp_back(dy_all, gate, up, wg, down[layer], halves_of[layer], band)
        partial, d, dy_all, m, b_all = tie(partial, d, dy_all, m, b_all)
        if layer == 0:
            partial, g_piece_late = tie(partial, g_piece_late)
        got = total(partial.reshape(rows, tq, width), "row")
        mates = (b_mate, swap(d), dy_mate, m_mate)
        wide_grad, *d_wide = mlp_grads(b_all, d, dy_all, m, mates, me_s, band, layer == 1)
        got, wide_grad = tie(got, wide_grad)
        g_piece = lax.psum_scatter(wide_grad.reshape(-1, fr), "col", scatter_dimension=0, tiled=True)
        back, gain2, shift2 = norm_back(from_gate(got), scaled2, inv2, g2)
        dh = grad + back
        dh_all = trade(by_feature(dh.astype(BF)), "col").reshape(seq, dc)
        dh_side = dh_all
        dh_mate = swap(dh_side)
        if layer == 0:
            g_late = send_parts(g_piece_late.reshape(rows, band, fr), "row")
        d_o = total(heads_back(dh_all, wqo), "col").astype(BF)
        if layer == 1:
            d_o, *parts = tie(d_o, *y_parts)
            outputs.append(h + add_all(parts))
        else:
            d_o, qo_grads[1], placed, *g_late = tie(d_o, qo_grads[1], to_output(outputs), *g_late)
        dp, bias_sum, partial = attention_back(d_o, qkv, wqo, tables, mask)
        partial, dp = tie(partial, dp)
        got = total(partial.reshape(cols, tq, width), "col")
        if aligned:
            mates = (a_mate, o_mate, swap(dp), dh_mate)
            wide_grads = [attention_grads(a_all, o_all, dp, dh_side, mates, mine[None])]
            over = "row"
        else:
            wide_grads = [dot_tn(a_all, dp).astype(BF), dot_tn(to_features(o_all), dh_side).astype(BF)]
            over = ("row", "section")
        got, *wide_grads = tie(got, *wide_grads)
        back, gain1, shift1 = norm_back(got, scaled1, inv1, g1)
        dx = dh + back
        norm_sums[layer] = jnp.stack([gain1, gain2, shift1, shift2])
        bias_sums[layer] = bias_sum.reshape(3, dc)
        grad = dx.astype(BF).astype(F32)
        input_grads[layer] = dx
        if layer == 1:
            g_piece_late, d_grads[1] = g_piece[:dc], g_piece[dc:]
        else:
            g_late = send_parts(from_blocks(place_all(g_late, me_r)), "col")
            dx, g_piece, norm_sums = tie(dx, g_piece, norm_sums)
            g_parts = send_parts(g_piece.reshape(rows, band, fr), "row")
            sums = total(jnp.stack(norm_sums).reshape(2, 4, cols, dc).transpose(2, 0, 1, 3), "col")
            sums, *parts = tie(sums, *g_parts, *g_late)
            g_late = parts[rows:]
            blocks = from_blocks(place_all(parts[:rows], me_r))
            blocks, d_wide[0], *wide_grads = tie(blocks, d_wide[0], *wide_grads)
            d_parts = send_parts(d_wide[0], "col")
            g_home = trade(blocks, "col").reshape(dr, fc)
            g_home, sums, input_grads[0] = tie(g_home, sums, dx)
            g_grads = unshare([g_home, place_all(g_late, me_c).reshape(dr, fc)])
            placed_back = to_output(input_grads)
            sums = jnp.concatenate([sums, jnp.stack(bias_sums)], axis=1)
            sums = total(add_all(send_all(sums, "row")), "section")
            g_grads, *d_parts = tie(g_grads, *d_parts)
            d_grads[0] = add_all(d_parts).astype(BF)
        pieces = [lax.psum_scatter(part, over, scatter_dimension=0, tiled=True) for part in wide_grads]
        qo_grads[layer] = jnp.concatenate(pieces, axis=1)

    qo_grads = unshare(qo_grads).reshape(dr, 4 * dc).astype(F32)
    qo_grads = [qo_grads[:, i * dc : (i + 1) * dc] for i in range(4)]
    return (
        placed,
        placed_back,
        jnp.stack(qo_grads[:3], axis=1)[None],
        sums[None, 4:],
        qo_grads[3][None],
        interleave(g_grads)[None],
        unshare(d_grads).astype(F32).reshape(dc, fr).T[None],
        sums[None, 0:2],
        sums[None, 2:4],
    )


def solution(mesh):
    return jax.shard_map(
        shards,
        mesh=mesh,
        in_specs=(
            P(None, "row", "col"),
            P(None, "row", "col"),
            P(None, "row"),
            P(None, "row"),
            P("section", "row", None, "col"),
            P("section", None, "col"),
            P("section", "row", "col"),
            P("section", "row", None, "col"),
            P("section", "row", "col"),
            P("section", None, "col"),
            P("section", None, "col"),
        ),
        out_specs=(
            P("section", None, "row", "col"),
            P("section", None, "row", "col"),
            P("section", "row", None, "col"),
            P("section", None, "col"),
            P("section", "row", "col"),
            P("section", "row", None, "col"),
            P("section", "row", "col"),
            P("section", None, "col"),
            P("section", None, "col"),
        ),
        check_vma=False,
    )
```

```python
import jax
import jax.numpy as jnp
from jax import lax
from jax.experimental import pallas as pl
from jax.experimental.pallas import tpu as pltpu
from jax.sharding import PartitionSpec as P

HEAD_DIM = 64
ROT = 16
NORM_EPSILON = 1e-05
ROPE_BASE = 10000.0
SCORE_SCALE = 0.125
MASKED_SCORE = -1e30
BF = jnp.bfloat16
F32 = jnp.float32


def trade(stack, axis):
    return lax.all_to_all(stack, axis, split_axis=0, concat_axis=0)


def gather(value, axis):
    return trade(jnp.broadcast_to(value, (lax.axis_size(axis), *value.shape)), axis)


def total(stack, axis):
    return jnp.sum(trade(stack, axis).astype(F32), axis=0)


def tie(point, *values):
    return lax.optimization_barrier((point, *values))


def dot(a, b):
    return lax.dot_general(a, b, (((1,), (0,)), ((), ())), preferred_element_type=F32)


def dot_nt(a, b):
    return lax.dot_general(a, b, (((1,), (1,)), ((), ())), preferred_element_type=F32)


def dot_tn(a, b):
    return lax.dot_general(a, b, (((0,), (0,)), ((), ())), preferred_element_type=F32)


def norm(values, gain, shift):
    mean_value = jnp.mean(values, axis=-1, keepdims=True)
    centred = values - mean_value
    variance = jnp.mean(centred * centred, axis=-1, keepdims=True)
    inv = lax.rsqrt(variance + NORM_EPSILON)
    scaled = centred * inv
    return (scaled * gain + shift).astype(BF), scaled, inv


def norm_back(grad, scaled, inv, gain):
    e = grad * gain
    mean_e = jnp.mean(e, axis=-1, keepdims=True)
    mean_p = jnp.mean(e * scaled, axis=-1, keepdims=True)
    return inv * (e - mean_e - scaled * mean_p), jnp.sum(grad * scaled, axis=0), jnp.sum(grad, axis=0)


def call(body, grid, in_specs, out_specs, out_shape, scratch, flops, moved, table, *args):
    return pl.pallas_call(
        body,
        grid_spec=pltpu.PrefetchScalarGridSpec(
            num_scalar_prefetch=1,
            grid=(grid,),
            in_specs=in_specs,
            out_specs=out_specs,
            scratch_shapes=scratch,
        ),
        out_shape=out_shape,
        compiler_params=pltpu.CompilerParams(vmem_limit_bytes=56 * 2**20),
        cost_estimate=pl.CostEstimate(flops=int(flops), bytes_accessed=int(moved), transcendentals=0),
    )(table, *args)


def no_table():
    return jnp.zeros((1, 1), jnp.int32)


def turn(x, cosines, sines, sign):
    ahead = pltpu.roll(x, 128 - ROT // 2, 1)
    behind = pltpu.roll(x, ROT // 2, 1)
    return x * cosines + sign * (ahead * sines[0] + behind * sines[1])


def head_lanes(n):
    lanes = lax.broadcasted_iota(jnp.int32, (n, 128), 1)
    return lanes < HEAD_DIM


def softmax_of(q, k, allowed):
    scores = jnp.where(allowed, dot_nt(q, k) * SCORE_SCALE, MASKED_SCORE)
    shifted = jnp.exp(scores - jnp.max(scores, axis=1, keepdims=True))
    return shifted / jnp.sum(shifted, axis=1, keepdims=True)


def whole(*shape):
    return pl.BlockSpec(shape, lambda i, t: (0,) * len(shape))


HBM = pl.BlockSpec(memory_space=pl.ANY)


def fetch(pairs, sems):
    copies = [pltpu.make_async_copy(src, dst, sems.at[i]) for i, (src, dst) in enumerate(pairs)]
    for copy in copies:
        copy.start()
    return copies


def attention(a, w, bias, tables, mask):
    n, width = a.shape
    m = w.shape[1] // 4
    half = width // 2

    def body(_, a_ref, w_ref, bias_ref, tab_ref, mask_ref, qkv_ref, o_ref, held, acc, sems):
        parts = [pl.ds(i * half, half) for i in range(2)]
        copies = fetch([(w_ref.at[part, pl.ds(0, 3 * m)], held.at[part]) for part in parts], sems)
        copies[0].wait()
        acc[...] = dot(a_ref[:, :half], held[:half]) + bias_ref[...]
        copies[1].wait()
        acc[...] += dot(a_ref[:, half:], held[half:])
        low = head_lanes(n)
        zero = jnp.zeros((n, 128), BF)
        allowed = mask_ref[...] > 0
        cosines, sines = tab_ref[0], (tab_ref[1], tab_ref[2])
        for pair in range(m // 128):
            at = pair * 128
            q = turn(acc[:, at : at + 128], cosines, sines, 1.0).astype(BF)
            k = turn(acc[:, m + at : m + at + 128], cosines, sines, 1.0).astype(BF)
            v = acc[:, 2 * m + at : 2 * m + at + 128].astype(BF)
            qkv_ref[:, at : at + 128] = q
            qkv_ref[:, m + at : m + at + 128] = k
            qkv_ref[:, 2 * m + at : 2 * m + at + 128] = v
            p0 = softmax_of(jnp.where(low, q, zero), k, allowed).astype(BF)
            p1 = softmax_of(jnp.where(low, zero, q), k, allowed).astype(BF)
            o_ref[:, at : at + 128] = jnp.where(low, dot(p0, v), dot(p1, v)).astype(BF)

    return call(
        body,
        1,
        [whole(n, width), HBM, whole(1, 3 * m), whole(3, n, 128), whole(n, n)],
        [whole(n, 3 * m), whole(n, m)],
        [jax.ShapeDtypeStruct((n, 3 * m), BF), jax.ShapeDtypeStruct((n, m), BF)],
        [pltpu.VMEM((width, 3 * m), BF), pltpu.VMEM((n, 3 * m), F32), pltpu.SemaphoreType.DMA((2,))],
        2 * n * width * 3 * m,
        2 * width * 3 * m,
        no_table(),
        a,
        w,
        bias,
        tables,
        mask,
    )


def attention_back(d_o, qkv, w, tables, mask):
    n, m = d_o.shape
    width = w.shape[0]
    half = width // 2

    def body(_, d_ref, qkv_ref, w_ref, tab_ref, mask_ref, dp_ref, sum_ref, da_ref, held, sems):
        parts = [pl.ds(i * half, half) for i in range(2)]
        copies = fetch([(w_ref.at[part, pl.ds(0, 3 * m)], held.at[part]) for part in parts], sems)
        low = head_lanes(n)
        zero = jnp.zeros((n, 128), BF)
        allowed = mask_ref[...] > 0
        cosines, sines = tab_ref[0], (tab_ref[1], tab_ref[2])
        for pair in range(m // 128):
            at = pair * 128
            q = qkv_ref[:, at : at + 128]
            k = qkv_ref[:, m + at : m + at + 128]
            v = qkv_ref[:, 2 * m + at : 2 * m + at + 128]
            g = d_ref[:, at : at + 128]
            out = []
            for mine in (True, False):
                pick_q = jnp.where(low, q, zero) if mine else jnp.where(low, zero, q)
                pick_g = jnp.where(low, g, zero) if mine else jnp.where(low, zero, g)
                probs = softmax_of(pick_q, k, allowed)
                d_probs = dot_nt(pick_g, v)
                row = jnp.sum(d_probs * probs, axis=1, keepdims=True)
                ds = (probs * (d_probs - row)).astype(BF)
                out.append((dot(ds, k), dot_tn(ds, q), dot_tn(probs.astype(BF), g)))
            dq, dk, dv = (jnp.where(low, x, y) for x, y in zip(*out))
            dq = turn(dq * SCORE_SCALE, cosines, sines, -1.0)
            dk = turn(dk * SCORE_SCALE, cosines, sines, -1.0)
            for place, part in enumerate((dq, dk, dv)):
                part = part.astype(BF)
                dp_ref[:, place * m + at : place * m + at + 128] = part
                sum_ref[:, place * m + at : place * m + at + 128] = jnp.sum(part.astype(F32), axis=0, keepdims=True)
        for i, copy in enumerate(copies):
            copy.wait()
            da_ref[:, i * half : (i + 1) * half] = dot_nt(dp_ref[...], held[i * half : (i + 1) * half]).astype(BF)

    return call(
        body,
        1,
        [whole(n, m), whole(n, 3 * m), HBM, whole(3, n, 128), whole(n, n)],
        [whole(n, 3 * m), whole(1, 3 * m), whole(n, width)],
        [
            jax.ShapeDtypeStruct((n, 3 * m), BF),
            jax.ShapeDtypeStruct((1, 3 * m), F32),
            jax.ShapeDtypeStruct((n, width), BF),
        ],
        [pltpu.VMEM((width, 3 * m), BF), pltpu.SemaphoreType.DMA((2,))],
        2 * n * width * 3 * m,
        2 * width * 3 * m,
        no_table(),
        d_o,
        qkv,
        w,
        tables,
        mask,
    )


def heads_out(o, w):
    c, n, m = o.shape

    def body(_, o_ref, w_ref, out_ref, held, sems):
        (copy,) = fetch([(w_ref.at[:, pl.ds(3 * m, m)], held)], sems)
        o_wide = jnp.concatenate([o_ref[i] for i in range(c)], axis=1)
        copy.wait()
        out_ref[...] = dot(o_wide, held[...]).astype(BF)

    return call(
        body,
        1,
        [whole(c, n, m), HBM],
        whole(n, m),
        jax.ShapeDtypeStruct((n, m), BF),
        [pltpu.VMEM((c * m, m), BF), pltpu.SemaphoreType.DMA((1,))],
        2 * c * n * m * m,
        2 * c * m * m,
        no_table(),
        o,
        w,
    )


def heads_back(d_h, w):
    n, m = d_h.shape
    c = w.shape[0] // m

    def body(_, d_ref, w_ref, out_ref, held, sems):
        (copy,) = fetch([(w_ref.at[:, pl.ds(3 * m, m)], held)], sems)
        copy.wait()
        back = dot_nt(d_ref[...], held[...]).astype(BF)
        for i in range(c):
            out_ref[i] = back[:, i * m : (i + 1) * m]

    return call(
        body,
        1,
        [whole(n, m), HBM],
        whole(c, n, m),
        jax.ShapeDtypeStruct((c, n, m), BF),
        [pltpu.VMEM((c * m, m), BF), pltpu.SemaphoreType.DMA((1,))],
        2 * c * n * m * m,
        2 * c * m * m,
        no_table(),
        d_h,
        w,
    )


def attention_grads(a, o, dp, d_h, mates, table):
    n, width = a.shape
    m = d_h.shape[1]
    steps = table.shape[1]
    depth = width // (2 * steps)
    per = m // depth

    def body(_, a_ref, o_ref, dp_ref, dh_ref, a2_ref, o2_ref, dp2_ref, dh2_ref, out_ref, dp_all, dh_all):
        @pl.when(pl.program_id(0) == 0)
        def _():
            dp_all[:n], dp_all[n:] = dp_ref[...], dp2_ref[...]
            dh_all[:n], dh_all[n:] = dh_ref[...], dh2_ref[...]

        out_ref[:, : 3 * m] = dot_tn(jnp.concatenate([a_ref[...], a2_ref[...]]), dp_all[...]).astype(BF)
        out_ref[:, 3 * m :] = dot_tn(jnp.concatenate([o_ref[0], o2_ref[0]]), dh_all[...]).astype(BF)

    inputs = [
        pl.BlockSpec((n, depth), lambda i, t: (0, t[0, i])),
        pl.BlockSpec((1, n, depth), lambda i, t: (t[0, i] // per, 0, t[0, i] % per)),
        pl.BlockSpec((n, 3 * m), lambda i, t: (0, 0)),
        pl.BlockSpec((n, m), lambda i, t: (0, 0)),
    ]
    return call(
        body,
        steps,
        inputs * 2,
        pl.BlockSpec((depth, 4 * m), lambda i, t: (i, 0)),
        jax.ShapeDtypeStruct((steps * depth, 4 * m), BF),
        [pltpu.VMEM((2 * n, 3 * m), BF), pltpu.VMEM((2 * n, m), BF)],
        2 * n * width * 4 * m,
        width * 4 * m,
        table,
        a,
        o,
        dp,
        d_h,
        *mates,
    )


def band_list(width, c, band):
    if band % 128:
        return [slice(0, width)]
    rows = width // (c * band)
    return [slice((r * c + q) * band, (r * c + q + 1) * band) for q in range(c) for r in range(rows)]


def mlp_copies(w_ref, down_refs, held, held_down):
    gate_up = [(w_ref.at[i, :, pl.ds(0, 2)], held.at[i]) for i in range(2)]
    sources = down_refs or [w_ref.at[i, :, 2] for i in range(2)]
    return gate_up, [(source, held_down.at[i]) for i, source in enumerate(sources)]


def mlp(b, w, down, halves, band):
    n, width = b.shape
    _, c, _, w2, f = w.shape
    bands = band_list(width, c, band)

    def body(t, b_ref, w_ref, *rest):
        down_refs, (gate_ref, up_ref, m_ref, y_ref, held, held_down, turned, sems) = rest[: len(down)], rest[len(down) :]
        first, later = mlp_copies(w_ref, down_refs, held, held_down)
        copies = fetch(first + later, sems)
        at = 0
        for part in bands:
            size = part.stop - part.start
            turned[:, at : at + size] = b_ref[:, part]
            at += size
        copies[0].wait()
        gate_ref[...] = dot(turned[...], held[0].reshape(width, f))
        copies[1].wait()
        up_ref[...] = dot(turned[...], held[1].reshape(width, f))
        gate = gate_ref[...]
        m_ref[...] = (gate * jax.nn.sigmoid(gate) * up_ref[...]).astype(BF)
        for i in range(2):
            copies[2 + i].wait()
            y = dot_nt(m_ref[...], held_down[i].reshape(c * w2, f)).astype(BF)
            half = t[0, i]
            for k in range(c):
                y_ref[:, pl.ds(pl.multiple_of((2 * k + half) * w2, w2), w2)] = y[:, k * w2 : (k + 1) * w2]

    return call(
        body,
        1,
        [whole(n, width), HBM] + [HBM] * len(down),
        [whole(n, f)] * 3 + [whole(n, width)],
        [jax.ShapeDtypeStruct((n, f), F32)] * 2 + [jax.ShapeDtypeStruct((n, f), BF), jax.ShapeDtypeStruct((n, width), BF)],
        [
            pltpu.VMEM((2, c, 2, w2, f), BF),
            pltpu.VMEM((2, c, w2, f), BF),
            pltpu.VMEM((n, width), BF),
            pltpu.SemaphoreType.DMA((4,)),
        ],
        2 * n * width * 3 * f,
        2 * width * 3 * f,
        halves,
        b,
        w,
        *down,
    )


def mlp_back(dy, gate, up, w, down, halves, band):
    n, width = dy.shape
    _, c, _, w2, f = w.shape
    half = width // 2
    bands = band_list(width, c, band)

    def body(t, dy_ref, gate_ref, up_ref, w_ref, *rest):
        down_refs, (d_ref, db_ref, held, held_down, acc, sems) = rest[: len(down)], rest[len(down) :]
        later, first = mlp_copies(w_ref, down_refs, held, held_down)
        copies = fetch(first + later, sems)
        for i in range(2):
            at = t[0, i]
            ours = [dy_ref[:, pl.ds(pl.multiple_of((2 * k + at) * w2, w2), w2)] for k in range(c)]
            ours = jnp.concatenate(ours, axis=1)
            copies[i].wait()
            part = dot(ours, held_down[i].reshape(c * w2, f))
            acc[...] = part if i == 0 else acc[...] + part
        dm, gate = acc[...], gate_ref[...]
        sig = jax.nn.sigmoid(gate)
        d_ref[0] = (dm * up_ref[...] * sig * (1.0 + gate * (1.0 - sig))).astype(BF)
        d_ref[1] = (dm * gate * sig).astype(BF)
        copies[2].wait()
        copies[3].wait()
        for i in range(2):
            part = slice(i * c // 2, (i + 1) * c // 2)
            back = dot_nt(d_ref[0], held[0, part].reshape(half, f)) + dot_nt(d_ref[1], held[1, part].reshape(half, f))
            back = back.astype(BF)
            if len(bands) == 1:
                db_ref[:, i * half : (i + 1) * half] = back
            for j in range(len(bands) // 2):
                db_ref[:, bands[i * len(bands) // 2 + j]] = back[:, j * band : (j + 1) * band]

    return call(
        body,
        1,
        [whole(n, width), whole(n, f), whole(n, f), HBM] + [HBM] * len(down),
        [whole(2, n, f), whole(n, width)],
        [jax.ShapeDtypeStruct((2, n, f), BF), jax.ShapeDtypeStruct((n, width), BF)],
        [
            pltpu.VMEM((2, c, 2, w2, f), BF),
            pltpu.VMEM((2, c, w2, f), BF),
            pltpu.VMEM((n, f), F32),
            pltpu.SemaphoreType.DMA((4,)),
        ],
        2 * n * width * 3 * f,
        2 * width * 3 * f,
        halves,
        dy,
        gate,
        up,
        w,
        *down,
    )


def mlp_grads(b, d, dy, m, mates, me_s, band, merged):
    n, width = b.shape
    f = m.shape[1]
    c = lax.axis_size("col")
    depth, w2 = width // c, width // c // 2
    sizes = (depth + w2,) if merged else (depth, w2)

    def body(_, b_ref, d_ref, dy_ref, m_ref, b2_ref, d2_ref, dy2_ref, m2_ref, *rest):
        *outs, d_all, m_all = rest

        @pl.when(pl.program_id(0) == 0)
        def _():
            d_all[:n], d_all[n:] = d_ref[0], d2_ref[0]
            m_all[:n], m_all[n:] = m_ref[...], m2_ref[...]

        def rows_of(ref):
            if band % 128:
                return ref[:, pl.ds(pl.multiple_of(pl.program_id(0) * depth, depth), depth)]
            at = [pl.multiple_of((r * c + pl.program_id(0)) * band, band) for r in range(depth // band)]
            return jnp.concatenate([ref[:, pl.ds(i, band)] for i in at], axis=1)

        outs[0][0, :depth] = dot_tn(jnp.concatenate([rows_of(b_ref), rows_of(b2_ref)]), d_all[...]).astype(BF)
        start = depth if merged else 0
        outs[-1][0, start : start + w2] = dot_tn(jnp.concatenate([dy_ref[...], dy2_ref[...]]), m_all[...]).astype(BF)

    inputs = [
        pl.BlockSpec((n, width), lambda i, t: (0, 0)),
        pl.BlockSpec((1, n, f), lambda i, t: (t[0, 0], 0, 0)),
        pl.BlockSpec((n, w2), lambda i, t: (0, i * 2 + t[0, 0])),
        pl.BlockSpec((n, f), lambda i, t: (0, 0)),
    ]
    return call(
        body,
        c,
        inputs * 2,
        [pl.BlockSpec((1, size, f), lambda i, t: (i, 0, 0)) for size in sizes],
        [jax.ShapeDtypeStruct((c, size, f), BF) for size in sizes],
        [pltpu.VMEM((2 * n, f), BF)] * 2,
        2 * n * width * 3 * f,
        width * 3 * f,
        me_s.reshape(1, 1),
        b,
        d,
        dy,
        m,
        *mates,
    )


def interleave(x, n):
    f = x.shape[2]
    rows = 64 if n % 64 == 0 else n

    def body(_, x_ref, out_ref):
        for i in range(2):
            out_ref[:, i, :] = x_ref[i].astype(F32)

    return call(
        body,
        n // rows,
        [pl.BlockSpec((2, rows, f), lambda i, t: (0, i, 0))],
        pl.BlockSpec((rows, 2, f), lambda i, t: (i, 0, 0)),
        jax.ShapeDtypeStruct((n, 2, f), F32),
        [],
        2 * n * f,
        12 * n * f,
        no_table(),
        x,
    )


def swap(value):
    return lax.ppermute(value, "section", [(0, 1), (1, 0)])


def hop(value, axis, step):
    return lax.ppermute(value, axis, [(i, i ^ step) for i in range(lax.axis_size(axis))])


def pick(stack, index):
    return lax.dynamic_index_in_dim(stack, index, 0, keepdims=False)


def place_all(pieces, me):
    out = jnp.zeros((len(pieces), *pieces[0].shape), pieces[0].dtype)
    for k, piece in enumerate(pieces):
        out = lax.dynamic_update_index_in_dim(out, piece, me ^ k, 0)
    return out


def send_all(value, axis):
    return [value] + [hop(value, axis, k) for k in range(1, lax.axis_size(axis))]


def send_parts(stack, axis):
    me = lax.axis_index(axis)
    return [pick(stack, me)] + [hop(pick(stack, me ^ k), axis, k) for k in range(1, stack.shape[0])]


def by_place(pieces, me):
    bit = 1
    while bit < len(pieces):
        flip = (me & bit) != 0
        pieces = [jnp.where(flip, pieces[i ^ bit], pieces[i]) for i in range(len(pieces))]
        bit *= 2
    return pieces


def add_all(parts):
    out = parts[0].astype(F32)
    for part in parts[1:]:
        out = out + part.astype(F32)
    return out


def shards(
    tokens_in, out_grad, segments, positions, w_qkv, b_qkv, w_out, w_gate_up, w_down, norm_gains, norm_biases
):
    rows, cols = lax.axis_size("row"), lax.axis_size("col")
    me_s = lax.axis_index("section")
    first = me_s == 0
    seq, dc = tokens_in.shape[1:]
    width = dc * cols
    tq = seq // cols
    dr = width // rows
    fc, fr = w_gate_up.shape[3], w_down.shape[1]
    w2, v2 = dc // 2, dr // 2
    sub = rows // cols
    band = dr // cols

    def own_first(a, b):
        return jnp.where(first, a, b), jnp.where(first, b, a)

    def to_gate(x):
        if band % 128 == 0:
            return x
        return x.reshape(-1, rows, cols, band).transpose(0, 2, 1, 3).reshape(-1, width)

    def from_gate(x):
        if band % 128 == 0:
            return x
        return x.reshape(-1, cols, rows, band).transpose(0, 2, 1, 3).reshape(-1, width)

    def to_features(stack):
        return stack.transpose(1, 0, 2).reshape(stack.shape[1], width)

    def by_feature(x):
        return x.reshape(x.shape[0], cols, dc).transpose(1, 0, 2)

    me_r, me_c = lax.axis_index("row"), lax.axis_index("col")
    qo = jnp.concatenate([w_qkv[0, :, 0], w_qkv[0, :, 1], w_qkv[0, :, 2], w_out[0]], axis=1)
    qo_half = trade(qo.reshape(2, v2, 4 * dc), "section")
    qo_half, w_gate_up = tie(qo_half, w_gate_up)

    aligned = v2 % 128 == 0
    mine = 2 * jnp.arange(rows, dtype=jnp.int32) + me_s

    def gather_qo(layer):
        return lax.all_gather(qo_half[layer], ("row", "section"), axis=0, tiled=True)

    wqo0 = gather_qo(0)
    g_half = trade(w_gate_up[0].transpose(1, 0, 2), "section")

    def to_blocks(bands):
        return bands.reshape(cols, band, sub, fr).transpose(0, 2, 1, 3).reshape(rows, band, fr)

    def from_blocks(blocks):
        return blocks.reshape(cols, sub, band, fr).transpose(0, 2, 1, 3).reshape(cols, band, fc)

    def gather_mlp(*pieces):
        whole_piece = jnp.concatenate([piece.reshape(-1, fr) for piece in pieces])
        return lax.all_gather(whole_piece, ("section", "col"), axis=0, tiled=True).reshape(2, cols, -1, w2, fr)

    plain = jnp.arange(2, dtype=jnp.int32).reshape(1, 2)
    halves_of = [plain, plain ^ me_s]

    def own_and_other(parts):
        own = place_all(parts, me_c)
        return own, swap(own)

    own_tokens = pick(tokens_in, me_s)
    own_grad = pick(out_grad, me_s)
    both = jnp.stack([own_tokens, own_grad]).reshape(2, cols, tq, dc).transpose(1, 0, 2, 3)
    small = jnp.concatenate([norm_gains[0], norm_biases[0], b_qkv[0]], axis=0)
    g_half, both, small, w_down = tie(g_half, both, small, w_down)
    g_parts = send_parts(g_half[0].reshape(cols, band, fc), "col")
    d_half = trade(w_down[0].T.reshape(2, w2, fr), "section")
    small = gather(small, "section")
    wide = gather(small[:, :4], "col").transpose(1, 2, 0, 3).reshape(2, 4, width).astype(F32)
    bias = small[:, 4:].astype(F32).reshape(2, 1, 3 * dc)

    segment = pick(segments, me_s)
    position = pick(positions, me_s)
    place = jnp.arange(seq, dtype=jnp.int32)
    allowed = (segment[:, None] == segment[None, :]) & (place[None, :] <= place[:, None])
    mask = allowed.astype(F32)
    freq = jnp.power(ROPE_BASE, -2.0 * jnp.arange(ROT // 2, dtype=F32) / ROT)
    angles = position.astype(F32)[:, None] * freq[None, :]
    cosines, sines = jnp.cos(angles), jnp.sin(angles)
    rest = jnp.zeros((seq, HEAD_DIM - ROT), F32)
    none = jnp.zeros_like(sines)
    tables = jnp.stack(
        [
            jnp.concatenate([cosines, cosines, rest + 1.0] * 2, axis=1),
            jnp.concatenate([-sines, none, rest] * 2, axis=1),
            jnp.concatenate([none, sines, rest] * 2, axis=1),
        ]
    )

    tables, mask, wide, *g_parts = tie(tables, mask, wide, *g_parts)
    blocks = to_blocks(place_all(g_parts, me_c))
    blocks, both = tie(blocks, both)
    g_parts = send_parts(blocks, "row")
    late_parts = send_parts(g_half[1].reshape(cols, band, fc), "col")
    both = trade(both, "col").transpose(1, 2, 0, 3).reshape(2, tq, width)
    x = both[0].astype(F32)

    weights, kept, outputs = [], [], []
    for layer in range(2):
        g1, g2, c1, c2 = wide[layer]
        a, scaled1, inv1 = norm(x, g1, c1)
        if layer == 0:
            a, *parts = tie(a, *g_parts, *late_parts)
            wg0 = gather_mlp(place_all(parts[:rows], me_r), d_half[0])
            g_parts = send_parts(to_blocks(place_all(parts[rows:], me_c)), "row")
            down = [(), None]
        a_all = gather(a, "col").reshape(seq, width)
        a_kept = a_all
        if layer == 0:
            wqo = wqo0
        else:
            wqo = wqo1
        a_mate = swap(a_kept)
        qkv, o = attention(a_all, wqo, bias[layer], tables, mask)
        if layer == 1:
            o, grad = tie(o, both[1])
            dy_parts = send_all(grad, "row")
        o_all = gather(o, "col")
        o_kept = o_all
        o_mate = swap(o_kept)
        out = heads_out(o_all, wqo)
        if layer == 0:
            out, *g_parts = tie(out, *g_parts)
            g_piece = place_all(g_parts, me_r)
        if layer == 1:
            out, *parts = tie(out, *dy_parts)
            dy_all = place_all(parts, me_r).reshape(rows * tq, width)
        got = trade(out.reshape(cols, tq, dc), "col")
        h = x + to_features(got).astype(F32)
        b, scaled2, inv2 = norm(h.astype(BF).astype(F32), g2, c2)
        if layer == 0:
            b, qo_half = tie(b, qo_half)
            wqo1 = gather_qo(1)
        b_all = gather(to_gate(b), "row").reshape(rows * tq, width)
        b_mate = swap(b_all)
        wg = wg0 if layer == 0 else wg1
        weights.append((wqo, wg))
        gate, up, m, partial = mlp(b_all, wg, down[layer], halves_of[layer], band)
        m_mate = swap(m)
        if layer == 0:
            gate, g_piece = tie(gate, g_piece)
            wg1 = gather_mlp(g_piece)
        partial = partial.reshape(rows, tq, width)
        if layer == 0:
            y = h + total(partial, "row")
            y, *parts = tie(y, *send_all(d_half[1], "col"))
            down[1] = own_and_other(parts)
            x = y.astype(BF).astype(F32)
            outputs.append(y)
        else:
            y_parts = send_parts(partial, "row")
        kept.append((a_kept, a_mate, scaled1, inv1, qkv, o_kept, o_mate, scaled2, inv2, b_all, b_mate, gate, up, m, m_mate))

    def to_output(pair):
        mine, theirs = own_first(*(part.astype(BF) for part in pair))
        both = jnp.stack(own_first(mine, swap(theirs)))
        parts = send_parts(both.reshape(2, tq, cols, dc).transpose(2, 0, 1, 3), "col")
        return jnp.concatenate(by_place(parts, me_c), axis=1).astype(F32)[None]

    def unshare(pair):
        return trade(jnp.stack(pair), "section")

    input_grads, qo_grads, g_grads, d_grads, norm_sums, bias_sums = ([None] * 2 for _ in range(6))
    grad = grad.astype(F32)
    for layer in (1, 0):
        g1, g2, c1, c2 = wide[layer]
        wqo, wg = weights[layer]
        a_all, a_mate, scaled1, inv1, qkv, o_all, o_mate, scaled2, inv2, b_all, b_mate, gate, up, m, m_mate = kept[layer]
        if layer == 0:
            dy_all = gather(grad.astype(BF), "row").reshape(rows * tq, width)
        dy_mate = swap(dy_all)
        d, partial = mlp_back(dy_all, gate, up, wg, down[layer], halves_of[layer], band)
        partial, d, dy_all, m, b_all = tie(partial, d, dy_all, m, b_all)
        if layer == 0:
            partial, g_piece_late = tie(partial, g_piece_late)
        got = total(partial.reshape(rows, tq, width), "row")
        mates = (b_mate, swap(d), dy_mate, m_mate)
        wide_grad, *d_wide = mlp_grads(b_all, d, dy_all, m, mates, me_s, band, layer == 1)
        got, wide_grad = tie(got, wide_grad)
        g_piece = lax.psum_scatter(wide_grad.reshape(-1, fr), "col", scatter_dimension=0, tiled=True)
        back, gain2, shift2 = norm_back(from_gate(got), scaled2, inv2, g2)
        dh = grad + back
        dh_all = trade(by_feature(dh.astype(BF)), "col").reshape(seq, dc)
        dh_side = dh_all
        dh_mate = swap(dh_side)
        if layer == 0:
            g_late = send_parts(g_piece_late.reshape(rows, band, fr), "row")
        d_o = total(heads_back(dh_all, wqo), "col").astype(BF)
        if layer == 1:
            d_o, *parts = tie(d_o, *y_parts)
            outputs.append(h + add_all(parts))
        else:
            d_o, qo_grads[1], placed, *g_late = tie(d_o, qo_grads[1], to_output(outputs), *g_late)
        dp, bias_sum, partial = attention_back(d_o, qkv, wqo, tables, mask)
        partial, dp = tie(partial, dp)
        got = total(partial.reshape(cols, tq, width), "col")
        if aligned:
            mates = (a_mate, o_mate, swap(dp), dh_mate)
            wide_grads = [attention_grads(a_all, o_all, dp, dh_side, mates, mine[None])]
            over = "row"
        else:
            wide_grads = [dot_tn(a_all, dp).astype(BF), dot_tn(to_features(o_all), dh_side).astype(BF)]
            over = ("row", "section")
        got, *wide_grads = tie(got, *wide_grads)
        back, gain1, shift1 = norm_back(got, scaled1, inv1, g1)
        dx = dh + back
        norm_sums[layer] = jnp.stack([gain1, gain2, shift1, shift2])
        bias_sums[layer] = bias_sum.reshape(3, dc)
        grad = dx.astype(BF).astype(F32)
        input_grads[layer] = dx
        if layer == 1:
            g_piece_late, d_grads[1] = g_piece[:dc], g_piece[dc:]
        else:
            g_late = send_parts(from_blocks(place_all(g_late, me_r)), "col")
            dx, g_piece, norm_sums = tie(dx, g_piece, norm_sums)
            g_parts = send_parts(g_piece.reshape(rows, band, fr), "row")
            sums = total(jnp.stack(norm_sums).reshape(2, 4, cols, dc).transpose(2, 0, 1, 3), "col")
            sums, *parts = tie(sums, *g_parts, *g_late)
            g_late = parts[rows:]
            blocks = from_blocks(place_all(parts[:rows], me_r))
            blocks, d_wide[0], *wide_grads = tie(blocks, d_wide[0], *wide_grads)
            d_parts = send_parts(d_wide[0], "col")
            g_home = trade(blocks, "col").reshape(dr, fc)
            g_home, sums, input_grads[0] = tie(g_home, sums, dx)
            g_grads = [g_home, place_all(g_late, me_c).reshape(dr, fc)]
            placed_back = to_output(input_grads)
            sums = jnp.concatenate([sums, jnp.stack(bias_sums)], axis=1)
            sums = total(add_all(send_all(sums, "row")), "section")
            g_grads[0], *d_parts = tie(g_grads[0], *d_parts)
            d_grads[0] = add_all(d_parts).astype(BF)
            if fc == fr:
                g_grads = unshare([jnp.concatenate(pair) for pair in zip(g_grads, d_grads)])
                d_grads = g_grads[:, dr:]
            else:
                g_grads, d_grads = unshare(g_grads), unshare(d_grads)
        pieces = [lax.psum_scatter(part, over, scatter_dimension=0, tiled=True) for part in wide_grads]
        qo_grads[layer] = jnp.concatenate(pieces, axis=1)

    qo_grads = unshare(qo_grads).reshape(dr, 4 * dc).astype(F32)
    qo_grads = [qo_grads[:, i * dc : (i + 1) * dc] for i in range(4)]
    return (
        placed,
        placed_back,
        jnp.stack(qo_grads[:3], axis=1)[None],
        sums[None, 4:],
        qo_grads[3][None],
        interleave(g_grads, dr)[None],
        d_grads.astype(F32).reshape(dc, fr).T[None],
        sums[None, 0:2],
        sums[None, 2:4],
    )


def solution(mesh):
    return jax.shard_map(
        shards,
        mesh=mesh,
        in_specs=(
            P(None, "row", "col"),
            P(None, "row", "col"),
            P(None, "row"),
            P(None, "row"),
            P("section", "row", None, "col"),
            P("section", None, "col"),
            P("section", "row", "col"),
            P("section", "row", None, "col"),
            P("section", "row", "col"),
            P("section", None, "col"),
            P("section", None, "col"),
        ),
        out_specs=(
            P("section", None, "row", "col"),
            P("section", None, "row", "col"),
            P("section", "row", None, "col"),
            P("section", None, "col"),
            P("section", "row", "col"),
            P("section", "row", None, "col"),
            P("section", "row", "col"),
            P("section", None, "col"),
            P("section", None, "col"),
        ),
        check_vma=False,
    )
```
